512 devices in a mesh: blk: 64 (over z_lo, y, core), aux: 8 (over z_hi, x).
Axes of the slice: x: 4, y: 4, z: 16 (z_hi: 2, z_lo: 8; z = z_hi * 8 + z_lo), core: 2. Of those that a mesh axis runs over, the one named last changes fastest.
Arguments:
- factors: bfloat16 [2048, 64, 512], P('aux', 'blk'), may hold values from -0.119628906 to 0.119628906
- occ_energy: float32 [64], P('blk'), may hold values from -1.5 to -0.3
- vir_energy: float32 [512], replicated, may hold values from 0.5 to 3
Outputs:
- pair_energy: float32 [64, 4], P('blk')
- gamma: float32 [2048, 64, 512], P('aux', 'blk')
The draws below stay inside these ranges and needn't reach their ends.
All inputs are finite; a program needn't handle non-finite values.
Results may differ from the reference program's by a relative error of at most 0.012.
Values may be sent and summed in bfloat16 or wider, within the bound.
A program may use at most 64 MiB of HBM per device.

```python
import jax
import jax.numpy as jnp
from jax import lax

NAUX = 2048
V = 512
REACH = 3
OCC = 64
N_AUX = 8


def block_scale(own_key, extent, cuts, least, largest):
    loudness = 1.0
    for dim, shards_of in cuts:
        steps = jax.random.uniform(jax.random.fold_in(jax.random.fold_in(own_key, 6), dim), (shards_of,), jnp.float32, least / len(cuts), largest / len(cuts))
        loudness = loudness * jnp.repeat(jnp.exp(steps), extent[dim] // shards_of).reshape((-1,) + (1,) * (len(extent) - 1 - dim))
    return loudness


def scatter_about(key, shape, spread, most, pieces=(), kind=jnp.bfloat16):
    gain = block_scale(key, shape, pieces, -0.22, 0.18) if pieces else 1.0
    drawn = jax.random.normal(key, shape, jnp.float32) * spread * gain
    return jnp.minimum(jnp.maximum(drawn, -most), most).astype(kind)


def setup_inputs(seed: int = 0) -> dict:
    key_of = jax.random.split(jax.random.key(seed), 4)
    factors = scatter_about(key_of[0], (NAUX, OCC, V), 0.02, 0.119628906, ((0, 8), (1, 64)))
    occ_energy = jnp.clip(-1.5 + 1.2 * jax.random.uniform(key_of[1], (OCC,), jnp.float32) ** block_scale(key_of[1], (OCC,), ((0, 64),), -0.2, 0.2), -1.5, -0.3)
    vir_energy = jnp.clip(jax.random.uniform(key_of[2], (V,), jnp.float32, 0.5, 3.0), 0.5, 3.0)
    return {"factors": factors, "occ_energy": occ_energy, "vir_energy": vir_energy}


def pair_terms(first_b, second_b, first_eps, second_eps, vir_energy):
    per_group = NAUX // N_AUX
    first_f = first_b.astype(jnp.float32).reshape(N_AUX, per_group, V)
    second_f = second_b.astype(jnp.float32).reshape(N_AUX, per_group, V)
    partials = jnp.einsum("gqa,gqb->gab", first_f, second_f, precision=lax.Precision.HIGHEST)
    rounded = lax.optimization_barrier(partials.astype(jnp.bfloat16)).astype(jnp.float32)
    integral = jnp.sum(rounded, axis=0)
    gap = vir_energy[:, None] + vir_energy[None, :] - first_eps - second_eps
    amplitude = (-integral / gap).astype(jnp.bfloat16)
    amp_f = amplitude.astype(jnp.float32)
    energy = -jnp.sum(gap * amp_f * (2.0 * amp_f - amp_f.T))
    weight = (2.0 * amp_f - amp_f.T).astype(jnp.bfloat16)
    return energy, weight


def reference(factors, occ_energy, vir_energy):
    def one_orbital(gamma, index):
        first_b = lax.dynamic_index_in_dim(factors, index, 1, keepdims=False)
        first_eps = occ_energy[index]
        energies = []
        for offset in range(REACH + 1):
            other = ((index + offset) % OCC).astype(jnp.int32)
            second_b = lax.dynamic_index_in_dim(factors, other, 1, keepdims=False)
            energy, weight = pair_terms(first_b, second_b, first_eps, occ_energy[other], vir_energy)
            gamma = gamma.at[:, index, :].add(jnp.dot(second_b, weight.T, preferred_element_type=jnp.float32))
            if offset > 0:
                gamma = gamma.at[:, other, :].add(jnp.dot(first_b, weight, preferred_element_type=jnp.float32))
            energies.append(energy)
        return gamma, jnp.stack(energies)

    start = jnp.zeros((NAUX, OCC, V), jnp.float32)
    gamma, pair_energy = lax.scan(one_orbital, start, jnp.arange(OCC, dtype=jnp.int32))
    return pair_energy, gamma
```

```python
import jax
import jax.numpy as jnp
from jax import lax
from jax.experimental import pallas as pl
from jax.experimental.pallas import tpu as pltpu
from jax.sharding import PartitionSpec as P

MESH = pl.DeviceIdType.MESH
BF = jnp.bfloat16
F32 = jnp.float32
NX = 4
NU = 64
HALF = NU // 2
COPIES = 72


def place(x, u, k):
    u = lax.rem(u, NU)
    return lax.rem(u, HALF) * 2 + k, lax.div(u, HALF) * NX + lax.rem(x, NX)


def nt(lhs, rhs):
    return lax.dot_general(lhs, rhs, (((1,), (1,)), ((), ())), preferred_element_type=F32)


def kernel(
    f_ref, occ_ref, vir_ref, gamma_ref, energy_ref,
    bo, bx, sf, sg, rf, rg, t, a0, vv, acc, acc2, w, wt,
    gown, goth, gf, out3, in3, eps, esum, en, send, recv,
):
    b = lax.axis_index("blk")
    a = lax.axis_index("aux")
    k = lax.rem(b, 2)
    h = lax.div(a, NX)
    x = lax.rem(a, NX)
    u = HALF * h + lax.div(b, 2)
    g = NX * h + x
    near = NX * h
    far = NX * (1 - h)
    gfar = far + x
    xs = [place(x + d, u, k) for d in (1, 2, 3)]
    partner = place(x, u + HALF, k)
    twin = place(x, u, 1 - k)
    down1, down2 = place(x, u + NU - 1, k), place(x, u + NU - 2, k)
    up1, up2 = place(x, u + 1, k), place(x, u + 2, k)
    h_down1 = lax.div(lax.rem(u + NU - 1, NU), HALF)
    h_down2 = lax.div(lax.rem(u + NU - 2, NU), HALF)
    g_up1 = NX * lax.div(lax.rem(u + 1, NU), HALF) + x
    g_up2 = (1 - k) * (NX * lax.div(lax.rem(u + 2, NU), HALF) + x) + k * g
    mine = pl.ds(pl.multiple_of(32 * x, 32), 32)

    barrier = pltpu.get_barrier_semaphore()
    others = xs + [partner, twin, down1, down2, up1, up2]
    for device in others:
        pl.semaphore_signal(barrier, inc=1, device_id=device, device_id_type=MESH)

    used = []

    def copy(src, dst, device):
        n = len(used)
        made = pltpu.make_async_remote_copy(
            src_ref=src, dst_ref=dst, send_sem=send.at[n], recv_sem=recv.at[n],
            device_id=device, device_id_type=MESH,
        )
        used.append(made)
        return made

    def even(body):
        pl.when(k == 0)(body)

    def odd(body):
        pl.when(k == 1)(body)

    bo[g] = f_ref[...].T.reshape(4, 128, 256)
    eps[0] = jnp.full((8, 512), occ_ref[0], F32)
    row = jnp.broadcast_to(vir_ref[...], (128, 512))
    for q in range(4):
        column = jnp.broadcast_to(row[:, 128 * q:128 * q + 128].T[:, 0:1], (128, 512))
        vv[q] = column + row
    esum[...] = jnp.zeros_like(esum)

    pl.semaphore_wait(barrier, len(others))

    cz = [copy(bo.at[g, q], bo.at[g, q], partner) for q in range(4)]
    cx = [copy(bo.at[g], bo.at[g], xs[d]) for d in range(3)]
    ce = [copy(eps.at[0], eps.at[n], device) for n, device in ((1, twin), (2, down1), (3, down2))]
    for c in cz + cx + ce:
        c.start()
    near4, far4 = pl.ds(near, NX), pl.ds(far, NX)
    ct_near = copy(bo.at[near4], bx.at[near4], twin)
    cf_near = copy(bo.at[near4, :, mine], sf.at[near4], down1)
    cg_near = copy(bo.at[near4, :, mine], sg.at[near4], down2)
    for c in cx:
        c.wait_recv()
    ct_near.start()
    cf_near.start()
    even(cg_near.start)

    def gram(dst, lhs, rhs, base, init):
        @pl.loop(0, 2)
        def _(c):
            total = None
            for n in range(NX):
                part = nt(lhs[base + n].reshape(512, 256), rhs[base + n, pl.ds(2 * c, 2)].reshape(256, 256))
                total = part if total is None else total + part
            cols = pl.ds(pl.multiple_of(256 * c, 256), 256)
            dst[:, cols] = total if init else dst[:, cols] + total

    gram(acc, bo, bo, near, True)
    ct_near.wait_recv()
    odd(lambda: gram(acc2, bo, bx, near, True))

    cxf = [[copy(bo.at[gfar, q], bo.at[gfar, q], xs[d]) for d in range(3)] for q in range(4)]
    ct_far = [copy(bo.at[far4, q], bx.at[far4, q], twin) for q in range(4)]
    cf_far = [copy(bo.at[far4, q, mine], sf.at[far4, q], down1) for q in range(4)]
    cg_far = [copy(bo.at[far4, q, mine], sg.at[far4, q], down2) for q in range(4)]
    for q in range(5):
        if q < 4:
            cz[q].wait_recv()
            for c in cxf[q]:
                c.start()
        if q > 0:
            for c in cxf[q - 1]:
                c.wait_recv()
            cf_far[q - 1].start()
            even(cg_far[q - 1].start)
            ct_far[q - 1].start()
    cr_f = copy(bo.at[NX * h_down1 + x], rf, down1)
    cr_g = copy(bo.at[NX * h_down2 + x], rg, down2)
    cr_f.start()
    even(cr_g.start)

    for c in ce[:2]:
        c.wait_recv()
    ce[2].wait_recv()
    for c in [cf_near] + cf_far + ct_far:
        c.wait_recv()

    def amplitude(integral, first, second, q, rows):
        gap = vv[q, rows] - eps[first, 0:1, :] - eps[second, 0:1, :]
        return (-integral / gap).astype(BF)

    def sliced(p, piece, whole, first, second):
        halves = []
        for half in range(2):
            total = None
            for n in range(NX):
                group = NX * half + n
                part = nt(piece[group].reshape(128, 256), whole[group].reshape(512, 256))
                total = part if total is None else total + part
            halves.append(total)
        total = halves[0] + halves[1]
        for q in range(4):
            t[p, q, mine] = amplitude(total[32 * q:32 * q + 32], first, second, q, mine)

    ca = [[copy(t.at[p, :, mine], t.at[p, :, mine], xs[d]) for d in range(3)] for p in range(3)]
    sliced(0, sf, bo, 0, 2)
    for c in ca[0]:
        c.start()
    sliced(1, sf, bx, 1, 2)
    for c in ca[1]:
        c.start()

    @even
    def _():
        for c in [cg_near] + cg_far:
            c.wait_recv()
        sliced(2, sg, bx, 1, 3)
        for c in ca[2]:
            c.start()

    def pair(read, first, second, slot, both):
        @pl.loop(0, 4)
        def _(q):
            rows = pl.ds(pl.multiple_of(128 * q, 128), 128)
            tq = read(q, slice(None)).astype(F32)
            turned = jnp.concatenate([read(n, rows).T for n in range(4)], axis=1).astype(F32)
            wide = 2.0 * tq - turned
            gap = vv[q] - eps[first, 0:1, :] - eps[second, 0:1, :]
            esum[slot, 0:1] += jnp.sum(gap * tq * wide, axis=0, keepdims=True)
            if both:
                wt[rows] = wide.astype(BF)
            w[rows] = (2.0 * turned - tq).astype(BF)

    def times(weight, factor):
        return jnp.dot(weight[...], factor, preferred_element_type=F32)

    gram(acc, bo, bo, far, False)

    @pl.loop(0, 4)
    def _(q):
        rows = pl.ds(pl.multiple_of(128 * q, 128), 128)
        a0[q] = amplitude(acc[rows], 0, 0, q, slice(None))

    pair(lambda q, cols: a0[q, :, cols], 0, 0, 0, False)
    gown[...] = times(w, bo[g].reshape(512, 256))

    @odd
    def _():
        gram(acc2, bo, bx, far, False)

        @pl.loop(0, 4)
        def _(q):
            rows = pl.ds(pl.multiple_of(128 * q, 128), 128)
            t[2, q] = amplitude(acc2[rows], 1, 0, q, slice(None))
        rg[...] = bo[g]

    c_f = copy(out3.at[0], in3.at[0], up1)
    c_g = copy(out3.at[1], in3.at[1], up2)
    c_x = copy(out3.at[2], in3.at[2], twin)
    c_e = copy(en.at[0], en.at[1], twin)

    cr_f.wait_recv()
    for c in ca[0]:
        c.wait_recv()
    pair(lambda q, cols: t[0, q, :, cols], 0, 2, 2, True)
    gown[...] += times(w, rf[...].reshape(512, 256))
    gf[...] = times(wt, bo[g_up1].reshape(512, 256))
    for c in ca[1]:
        c.wait_recv()
    pair(lambda q, cols: t[1, q, :, cols], 1, 2, 1, True)
    out3[0] = (gf[...] + times(wt, bx[g_up1].reshape(512, 256))).astype(BF)
    c_f.start()
    goth[...] = times(w, rf[...].reshape(512, 256))

    @even
    def _():
        for c in ca[2]:
            c.wait_recv()
        cr_g.wait_recv()
        pair(lambda q, cols: t[2, q, :, cols], 1, 3, 3, True)

    @odd
    def _():
        pair(lambda q, cols: t[2, q, :, cols], 1, 0, 3, True)

    gf[...] = times(wt, bx[g_up2].reshape(512, 256))

    @even
    def _():
        out3[1] = gf[...].astype(BF)
        c_g.start()

    out3[2] = (goth[...] + times(w, rg[...].reshape(512, 256))).astype(BF)
    c_x.start()

    lane = lax.broadcasted_iota(jnp.int32, (8, 128), 1)
    total = [-jnp.sum(esum[n, 0:1], axis=1, keepdims=True) for n in range(4)]
    first_at = 1 + 2 * k
    en[0] = jnp.where(lane == first_at, total[1], jnp.where(lane == 4 - first_at, total[3], 0.0))
    c_e.start()
    kept = jnp.where(lane == 0, total[0], jnp.where(lane == 2, total[2], 0.0))
    c_e.wait_recv()
    energy_ref[...] = (kept + en[1])[0:1, 0:4]

    @odd
    def _():
        gown[...] += gf[...]

    c_x.wait_recv()
    gown[...] += in3[2].astype(F32)
    c_f.wait_recv()
    gown[...] += in3[0].astype(F32)

    @even
    def _():
        c_g.wait_recv()
        gown[...] += in3[1].astype(F32)

    for n in range(4):
        gamma_ref[:, 128 * n:128 * n + 128] = gown[128 * n:128 * n + 128].T

    only_even = [cg_near, cr_g, c_g] + cg_far + ca[2]
    for c in used:
        if all(c is not e for e in only_even):
            c.wait_send()

    @even
    def _():
        for c in only_even:
            c.wait_send()


def per_device(factors, occ_energy, vir_energy):
    vmem = pl.BlockSpec(memory_space=pltpu.VMEM)
    gamma, energy = pl.pallas_call(
        kernel,
        out_shape=(
            jax.ShapeDtypeStruct((256, 512), F32),
            jax.ShapeDtypeStruct((1, 4), F32),
        ),
        in_specs=[vmem, pl.BlockSpec(memory_space=pltpu.SMEM), vmem],
        out_specs=(vmem, vmem),
        scratch_shapes=[
            pltpu.VMEM((8, 4, 128, 256), BF),
            pltpu.VMEM((8, 4, 128, 256), BF),
            pltpu.VMEM((8, 4, 32, 256), BF),
            pltpu.VMEM((8, 4, 32, 256), BF),
            pltpu.VMEM((4, 128, 256), BF),
            pltpu.VMEM((4, 128, 256), BF),
            pltpu.VMEM((3, 4, 128, 512), BF),
            pltpu.VMEM((4, 128, 512), BF),
            pltpu.VMEM((4, 128, 512), F32),
            pltpu.VMEM((512, 512), F32),
            pltpu.VMEM((512, 512), F32),
            pltpu.VMEM((512, 512), BF),
            pltpu.VMEM((512, 512), BF),
            pltpu.VMEM((512, 256), F32),
            pltpu.VMEM((512, 256), F32),
            pltpu.VMEM((512, 256), F32),
            pltpu.VMEM((3, 512, 256), BF),
            pltpu.VMEM((3, 512, 256), BF),
            pltpu.VMEM((4, 8, 512), F32),
            pltpu.VMEM((4, 8, 512), F32),
            pltpu.VMEM((2, 8, 128), F32),
            pltpu.SemaphoreType.DMA((COPIES,)),
            pltpu.SemaphoreType.DMA((COPIES,)),
        ],
        compiler_params=pltpu.CompilerParams(
            collective_id=0, has_side_effects=True, vmem_limit_bytes=44 << 20
        ),
        name="pairs",
    )(factors.reshape(256, 512), occ_energy, vir_energy.reshape(1, 512))
    return energy, gamma.reshape(256, 1, 512)


def solution(mesh):
    return jax.shard_map(
        per_device,
        mesh=mesh,
        in_specs=(P("aux", "blk", None), P("blk"), P()),
        out_specs=(P("blk", None), P("aux", "blk", None)),
        check_vma=False,
    )
```

```python
import jax
import jax.numpy as jnp
from jax import lax
from jax.experimental import pallas as pl
from jax.experimental.pallas import tpu as pltpu
from jax.sharding import PartitionSpec as P

MESH = pl.DeviceIdType.MESH
BF = jnp.bfloat16
F32 = jnp.float32
NX = 4
NU = 64
HALF = NU // 2
COPIES = 72


def place(x, u, k):
    u = lax.rem(u, NU)
    return lax.rem(u, HALF) * 2 + k, lax.div(u, HALF) * NX + lax.rem(x, NX)


def nt(lhs, rhs):
    return lax.dot_general(lhs, rhs, (((1,), (1,)), ((), ())), preferred_element_type=F32)


def kernel(
    f_ref, occ_ref, vir_ref, gamma_ref, energy_ref,
    bo, bx, sf, sg, rf, rg, t, a0, vv, acc, acc2, w, wt,
    gown, goth, gf, out3, in3, eps, esum, en, send, recv,
):
    b = lax.axis_index("blk")
    a = lax.axis_index("aux")
    k = lax.rem(b, 2)
    h = lax.div(a, NX)
    x = lax.rem(a, NX)
    u = HALF * h + lax.div(b, 2)
    y = lax.rem(u, 4)
    g = NX * h + x
    near = NX * h
    far = NX * (1 - h)
    gfar = far + x
    xs = [place(x + d, u, k) for d in (1, 2, 3)]
    partner = place(x, u + HALF, k)
    twin = place(x, u, 1 - k)
    down1, down2 = place(x, u + NU - 1, k), place(x, u + NU - 2, k)
    up1, up2 = place(x, u + 1, k), place(x, u + 2, k)
    h_down1 = lax.div(lax.rem(u + NU - 1, NU), HALF)
    h_down2 = lax.div(lax.rem(u + NU - 2, NU), HALF)
    g_up1 = NX * lax.div(lax.rem(u + 1, NU), HALF) + x
    g_up2 = (1 - k) * (NX * lax.div(lax.rem(u + 2, NU), HALF) + x) + k * g
    mine = pl.ds(pl.multiple_of(32 * x, 32), 32)

    barrier = pltpu.get_barrier_semaphore()
    others = xs + [partner, twin, down1, down2, up1, up2]
    for device in others:
        pl.semaphore_signal(barrier, inc=1, device_id=device, device_id_type=MESH)

    used, done = [], []

    def copy(src, dst, device, only_even=False):
        n = len(used)
        made = pltpu.make_async_remote_copy(
            src_ref=src, dst_ref=dst, send_sem=send.at[n], recv_sem=recv.at[n],
            device_id=device, device_id_type=MESH,
        )
        used.append((made, only_even))
        return made

    def sent(*copies):
        for c in copies:
            c.wait_send()
            done.append(c)

    def even(body):
        pl.when(k == 0)(body)

    def odd(body):
        pl.when(k == 1)(body)

    bo[g] = f_ref[...].T.reshape(4, 128, 256)
    eps[0] = jnp.full((8, 512), occ_ref[0], F32)
    row = jnp.broadcast_to(vir_ref[...], (128, 512))
    for q in range(4):
        column = jnp.broadcast_to(row[:, 128 * q:128 * q + 128].T[:, 0:1], (128, 512))
        vv[q] = column + row
    esum[...] = jnp.zeros_like(esum)

    pl.semaphore_wait(barrier, len(others))

    cz = [copy(bo.at[g, q], bo.at[g, q], partner) for q in range(4)]
    cx = [copy(bo.at[g], bo.at[g], xs[d]) for d in range(3)]
    ce = [copy(eps.at[0], eps.at[n], device) for n, device in ((1, twin), (2, down1), (3, down2))]
    cr_f = copy(bo.at[NX * h_down1 + x], rf, down1)
    cr_g = copy(bo.at[NX * h_down2 + x], rg, down2, True)
    for c in cz[:2] + cx + ce:
        c.start()
    pl.when(y > 0)(cr_f.start)
    pl.when((y > 1) & (k == 0))(cr_g.start)
    near4, far4 = pl.ds(near, NX), pl.ds(far, NX)
    ct_near = copy(bo.at[near4], bx.at[near4], twin)
    cf_near = copy(bo.at[near4, :, mine], sf.at[near4], down1)
    cg_near = copy(bo.at[near4, :, mine], sg.at[near4], down2, True)
    sent(cz[0])
    cz[2].start()
    for c in cx:
        c.wait_recv()
    ct_near.start()
    cf_near.start()
    even(cg_near.start)
    sent(cz[1])
    cz[3].start()

    def gram(dst, lhs, rhs, base, init):
        @pl.loop(0, 2)
        def _(c):
            total = None
            for n in range(NX):
                part = nt(lhs[base + n].reshape(512, 256), rhs[base + n, pl.ds(2 * c, 2)].reshape(256, 256))
                total = part if total is None else total + part
            cols = pl.ds(pl.multiple_of(256 * c, 256), 256)
            dst[:, cols] = total if init else dst[:, cols] + total

    gram(acc, bo, bo, near, True)
    ct_near.wait_recv()
    odd(lambda: gram(acc2, bo, bx, near, True))

    cxf = [[copy(bo.at[gfar, q], bo.at[gfar, q], xs[d]) for d in range(3)] for q in range(4)]
    ct_far = [copy(bo.at[far4, q], bx.at[far4, q], twin) for q in range(4)]
    cf_far = [copy(bo.at[far4, q, mine], sf.at[far4, q], down1) for q in range(4)]
    cg_far = [copy(bo.at[far4, q, mine], sg.at[far4, q], down2, True) for q in range(4)]
    for q in range(5):
        if q < 4:
            cz[q].wait_recv()
            for c in cxf[q]:
                c.start()
        if q > 0:
            for c in cxf[q - 1]:
                c.wait_recv()
            cf_far[q - 1].start()
            even(cg_far[q - 1].start)
            ct_far[q - 1].start()
    pl.when(y == 0)(cr_f.start)
    pl.when((y < 2) & (k == 0))(cr_g.start)

    for c in ce[:2]:
        c.wait_recv()
    ce[2].wait_recv()
    for c in [cf_near] + cf_far + ct_far:
        c.wait_recv()

    def amplitude(integral, first, second, q, rows):
        gap = vv[q, rows] - eps[first, 0:1, :] - eps[second, 0:1, :]
        return (-integral / gap).astype(BF)

    def sliced(p, piece, whole, first, second):
        halves = []
        for half in range(2):
            total = None
            for n in range(NX):
                group = NX * half + n
                part = nt(piece[group].reshape(128, 256), whole[group].reshape(512, 256))
                total = part if total is None else total + part
            halves.append(total)
        total = halves[0] + halves[1]
        for q in range(4):
            t[p, q, mine] = amplitude(total[32 * q:32 * q + 32], first, second, q, mine)

    ca = [[copy(t.at[p, :, mine], t.at[p, :, mine], xs[d], p == 2) for d in range(3)] for p in range(3)]

    @even
    def _():
        for c in [cg_near] + cg_far:
            c.wait_recv()
        sliced(2, sg, bx, 1, 3)
        for c in ca[2]:
            c.start()

    sliced(0, sf, bo, 0, 2)

    @odd
    def _():
        for c in ca[0]:
            c.start()

    sliced(1, sf, bx, 1, 2)

    def pair(read, first, second, slot, both):
        @pl.loop(0, 4)
        def _(q):
            rows = pl.ds(pl.multiple_of(128 * q, 128), 128)
            tq = read(q, slice(None)).astype(F32)
            turned = jnp.concatenate([read(n, rows).T for n in range(4)], axis=1).astype(F32)
            wide = 2.0 * tq - turned
            gap = vv[q] - eps[first, 0:1, :] - eps[second, 0:1, :]
            esum[slot, 0:1] += jnp.sum(gap * tq * wide, axis=0, keepdims=True)
            if both:
                wt[rows] = wide.astype(BF)
            w[rows] = (2.0 * turned - tq).astype(BF)

    def times(weight, factor):
        return jnp.dot(weight[...], factor, preferred_element_type=F32)

    gram(acc, bo, bo, far, False)

    @pl.loop(0, 4)
    def _(q):
        rows = pl.ds(pl.multiple_of(128 * q, 128), 128)
        a0[q] = amplitude(acc[rows], 0, 0, q, slice(None))

    @even
    def _():
        for c in ca[2]:
            c.wait_send()
        for c in ca[0]:
            c.start()
    done.extend(ca[2])

    pair(lambda q, cols: a0[q, :, cols], 0, 0, 0, False)
    gown[...] = times(w, bo[g].reshape(512, 256))

    c_g = copy(out3.at[1], in3.at[1], up1, True)

    @odd
    def _():
        gram(acc2, bo, bx, far, False)

        @pl.loop(0, 4)
        def _(q):
            rows = pl.ds(pl.multiple_of(128 * q, 128), 128)
            t[2, q] = amplitude(acc2[rows], 1, 0, q, slice(None))
        rg[...] = bo[g]
        pair(lambda q, cols: t[2, q, :, cols], 1, 0, 3, True)

    @even
    def _():
        for c in ca[2]:
            c.wait_recv()
        cr_g.wait_recv()
        pair(lambda q, cols: t[2, q, :, cols], 1, 3, 3, True)

    gf[...] = times(wt, bx[g_up2].reshape(512, 256))

    @even
    def _():
        out3[1] = gf[...].astype(BF)
        c_g.start()

    goth[...] = times(w, rg[...].reshape(512, 256))

    @odd
    def _():
        gown[...] += gf[...]

    sent(*ca[0])
    for c in ca[1]:
        c.start()
    c_f = copy(out3.at[0], in3.at[0], up1)
    c_x = copy(out3.at[2], in3.at[2], twin)
    cr_f.wait_recv()
    for c in ca[0]:
        c.wait_recv()
    pair(lambda q, cols: t[0, q, :, cols], 0, 2, 2, True)
    gown[...] += times(w, rf[...].reshape(512, 256))
    gf[...] = times(wt, bo[g_up1].reshape(512, 256))

    @even
    def _():
        c_g.wait_recv()
        gf[...] += in3[1].astype(F32)

    for c in ca[1]:
        c.wait_recv()
    pair(lambda q, cols: t[1, q, :, cols], 1, 2, 1, True)
    out3[0] = (gf[...] + times(wt, bx[g_up1].reshape(512, 256))).astype(BF)
    c_f.start()
    out3[2] = (goth[...] + times(w, rf[...].reshape(512, 256))).astype(BF)
    c_x.start()

    lane = lax.broadcasted_iota(jnp.int32, (8, 128), 1)
    total = [-jnp.sum(esum[n, 0:1], axis=1, keepdims=True) for n in range(4)]
    first_at = 1 + 2 * k
    en[0] = jnp.where(lane == first_at, total[1], jnp.where(lane == 4 - first_at, total[3], 0.0))
    c_e = copy(en.at[0], en.at[1], twin)
    c_e.start()
    kept = jnp.where(lane == 0, total[0], jnp.where(lane == 2, total[2], 0.0))
    c_e.wait_recv()
    energy_ref[...] = (kept + en[1])[0:1, 0:4]

    c_x.wait_recv()
    gown[...] += in3[2].astype(F32)
    c_f.wait_recv()
    gown[...] += in3[0].astype(F32)

    for n in range(4):
        gamma_ref[:, 128 * n:128 * n + 128] = gown[128 * n:128 * n + 128].T

    for c, only_even in used:
        if not only_even and all(c is not d for d in done):
            c.wait_send()

    @even
    def _():
        for c, only_even in used:
            if only_even and all(c is not d for d in done):
                c.wait_send()


def per_device(factors, occ_energy, vir_energy):
    vmem = pl.BlockSpec(memory_space=pltpu.VMEM)
    gamma, energy = pl.pallas_call(
        kernel,
        out_shape=(
            jax.ShapeDtypeStruct((256, 512), F32),
            jax.ShapeDtypeStruct((1, 4), F32),
        ),
        in_specs=[vmem, pl.BlockSpec(memory_space=pltpu.SMEM), vmem],
        out_specs=(vmem, vmem),
        scratch_shapes=[
            pltpu.VMEM((8, 4, 128, 256), BF),
            pltpu.VMEM((8, 4, 128, 256), BF),
            pltpu.VMEM((8, 4, 32, 256), BF),
            pltpu.VMEM((8, 4, 32, 256), BF),
            pltpu.VMEM((4, 128, 256), BF),
            pltpu.VMEM((4, 128, 256), BF),
            pltpu.VMEM((3, 4, 128, 512), BF),
            pltpu.VMEM((4, 128, 512), BF),
            pltpu.VMEM((4, 128, 512), F32),
            pltpu.VMEM((512, 512), F32),
            pltpu.VMEM((512, 512), F32),
            pltpu.VMEM((512, 512), BF),
            pltpu.VMEM((512, 512), BF),
            pltpu.VMEM((512, 256), F32),
            pltpu.VMEM((512, 256), F32),
            pltpu.VMEM((512, 256), F32),
            pltpu.VMEM((3, 512, 256), BF),
            pltpu.VMEM((3, 512, 256), BF),
            pltpu.VMEM((4, 8, 512), F32),
            pltpu.VMEM((4, 8, 512), F32),
            pltpu.VMEM((2, 8, 128), F32),
            pltpu.SemaphoreType.DMA((COPIES,)),
            pltpu.SemaphoreType.DMA((COPIES,)),
        ],
        compiler_params=pltpu.CompilerParams(
            collective_id=0, has_side_effects=True, vmem_limit_bytes=44 << 20
        ),
        name="pairs",
    )(factors.reshape(256, 512), occ_energy, vir_energy.reshape(1, 512))
    return energy, gamma.reshape(256, 1, 512)


def solution(mesh):
    return jax.shard_map(
        per_device,
        mesh=mesh,
        in_specs=(P("aux", "blk", None), P("blk"), P()),
        out_specs=(P("blk", None), P("aux", "blk", None)),
        check_vma=False,
    )
```

```python
import jax
import jax.numpy as jnp
from jax import lax
from jax.experimental import pallas as pl
from jax.experimental.pallas import tpu as pltpu
from jax.sharding import PartitionSpec as P

MESH = pl.DeviceIdType.MESH
BF = jnp.bfloat16
F32 = jnp.float32
NX = 4
NU = 64
HALF = NU // 2
COPIES = 96


def place(x, u, k):
    u = lax.rem(u, NU)
    return lax.rem(u, HALF) * 2 + k, lax.div(u, HALF) * NX + lax.rem(x, NX)


def nt(lhs, rhs):
    return lax.dot_general(lhs, rhs, (((1,), (1,)), ((), ())), preferred_element_type=F32)


def kernel(
    f_ref, occ_ref, vir_ref, gamma_ref, energy_ref,
    bo, bx, sf, sg, sv, rf, rg, t, a0, vv, acc, acc2, w, wt,
    gown, goth, gf, out3, in3, eps, esum, en, send, recv,
):
    b = lax.axis_index("blk")
    a = lax.axis_index("aux")
    k = lax.rem(b, 2)
    h = lax.div(a, NX)
    x = lax.rem(a, NX)
    u = HALF * h + lax.div(b, 2)
    y = lax.rem(u, 4)
    g = NX * h + x
    near = NX * h
    far = NX * (1 - h)
    gfar = far + x
    xs = [place(x + d, u, k) for d in (1, 2, 3)]
    partner = place(x, u + HALF, k)
    twin = place(x, u, 1 - k)
    down1, down2 = place(x, u + NU - 1, k), place(x, u + NU - 2, k)
    up1, up2 = place(x, u + 1, k), place(x, u + 2, k)
    h_down1 = lax.div(lax.rem(u + NU - 1, NU), HALF)
    h_down2 = lax.div(lax.rem(u + NU - 2, NU), HALF)
    g_up1 = NX * lax.div(lax.rem(u + 1, NU), HALF) + x
    h_up1 = lax.div(lax.rem(u + 1, NU), HALF)
    g_up2 = (1 - k) * (NX * lax.div(lax.rem(u + 2, NU), HALF) + x) + k * g
    mine = pl.ds(pl.multiple_of(32 * x, 32), 32)

    barrier = pltpu.get_barrier_semaphore()
    detour, undetour = place(x, u + 3, k), place(x, u + NU - 3, k)
    down4, up4 = place(x, u + NU - 4, k), place(x, u + 4, k)
    others = xs + [partner, twin, down1, down2, up1, up2, detour, undetour, down4, up4]
    for device in others:
        pl.semaphore_signal(barrier, inc=1, device_id=device, device_id_type=MESH)

    who = {
        "all": None,
        "even": k == 0,
        "skip": (k == 0) & (y == 1),
        "relay": (k == 0) & (y > 0),
        "direct": (k == 0) | (y > 0),
        "detour": (k == 1) & (y == 0),
        "detoured": (k == 1) & (y == 3),
    }
    used, done = [], []

    def copy(src, dst, device, sender="all", lands_as=None):
        n = len(used)
        made = pltpu.make_async_remote_copy(
            src_ref=src, dst_ref=dst, send_sem=send.at[n],
            recv_sem=recv.at[n if lands_as is None else slot_of[id(lands_as)]],
            device_id=device, device_id_type=MESH,
        )
        slot_of[id(made)] = n
        used.append((made, sender))
        return made

    slot_of = {}

    def only(sender, body):
        pl.when(who[sender])(body)

    def sent(*copies):
        for c in copies:
            c.wait_send()
            done.append(c)

    def even(body):
        pl.when(k == 0)(body)

    def odd(body):
        pl.when(k == 1)(body)

    bo[g] = f_ref[...].T.reshape(4, 128, 256)
    eps[0] = jnp.full((8, 512), occ_ref[0], F32)
    row = jnp.broadcast_to(vir_ref[...], (128, 512))
    for q in range(4):
        column = jnp.broadcast_to(row[:, 128 * q:128 * q + 128].T[:, 0:1], (128, 512))
        vv[q] = column + row
    esum[...] = jnp.zeros_like(esum)

    pl.semaphore_wait(barrier, len(others))

    cz = [copy(bo.at[g, q], bo.at[g, q], partner) for q in range(4)]
    cx = [copy(bo.at[g], bo.at[g], xs[d]) for d in range(3)]
    ce = [copy(eps.at[0], eps.at[n], device) for n, device in ((1, twin), (2, down1), (3, down2))]
    cr_f = copy(bo.at[NX * h_down1 + x], rf, down1)
    cr_g = copy(bo.at[NX * h_down2 + x], rg, down2, "even")
    for c in cz[:2] + cx + ce:
        c.start()
    pl.when(y > 0)(cr_f.start)
    pl.when((y > 1) & (k == 0))(cr_g.start)
    near4, far4 = pl.ds(near, NX), pl.ds(far, NX)
    up_near4 = pl.ds(NX * h_up1, NX)
    up_far4 = pl.ds(NX - NX * h_up1, NX)
    ct_near = copy(bo.at[near4], bx.at[near4], twin)

    def slices(groups, up_groups, q):
        own = bo.at[groups, q, mine]
        f = copy(own, sf.at[groups, q], down1, "direct")
        f_out = copy(own, sv.at[groups, q], detour, "detour")
        f_in = copy(sv.at[groups, q], sf.at[groups, q], down4, "detoured", f)
        g = copy(own, sg.at[groups, q], down2, "skip")
        g_in = copy(sf.at[up_groups, q], sg.at[up_groups, q], down1, "relay", g)

        def first():
            only("direct", f.start)
            only("detour", f_out.start)
            only("skip", g.start)

        def second():
            @pl.when(who["detoured"])
            def _():
                f_out.wait_recv()
                f_in.start()

            @even
            def _():
                f.wait_recv()

            only("relay", g_in.start)

        def last():
            odd(f.wait_recv)
            even(g.wait_recv)

        return first, second, last

    to_near = slices(near4, up_near4, slice(None))
    sent(cz[0])
    cz[2].start()
    for c in cx:
        c.wait_recv()
    ct_near.start()
    to_near[0]()
    sent(cz[1])
    cz[3].start()

    def gram(dst, lhs, rhs, base, init):
        @pl.loop(0, 2)
        def _(c):
            total = None
            for n in range(NX):
                part = nt(lhs[base + n].reshape(512, 256), rhs[base + n, pl.ds(2 * c, 2)].reshape(256, 256))
                total = part if total is None else total + part
            cols = pl.ds(pl.multiple_of(256 * c, 256), 256)
            dst[:, cols] = total if init else dst[:, cols] + total

    gram(acc, bo, bo, near, True)
    to_near[1]()
    ct_near.wait_recv()
    odd(lambda: gram(acc2, bo, bx, near, True))

    cxf = [[copy(bo.at[gfar, q], bo.at[gfar, q], xs[d]) for d in range(3)] for q in range(4)]
    ct_far = [copy(bo.at[far4, q], bx.at[far4, q], twin) for q in range(4)]
    to_far = [slices(far4, up_far4, q) for q in range(4)]
    for step in range(6):
        if step < 4:
            cz[step].wait_recv()
            for c in cxf[step]:
                c.start()
        if 1 <= step < 5:
            for c in cxf[step - 1]:
                c.wait_recv()
            to_far[step - 1][0]()
            ct_far[step - 1].start()
        if step >= 2:
            to_far[step - 2][1]()
    pl.when(y == 0)(cr_f.start)
    pl.when((y < 2) & (k == 0))(cr_g.start)

    for c in ce + ct_far:
        c.wait_recv()
    for part in [to_near] + to_far:
        part[2]()

    def amplitude(integral, first, second, q, rows):
        gap = vv[q, rows] - eps[first, 0:1, :] - eps[second, 0:1, :]
        return (-integral / gap).astype(BF)

    def sliced(p, piece, whole, first, second):
        halves = []
        for half in range(2):
            total = None
            for n in range(NX):
                group = NX * half + n
                part = nt(piece[group].reshape(128, 256), whole[group].reshape(512, 256))
                total = part if total is None else total + part
            halves.append(total)
        total = halves[0] + halves[1]
        for q in range(4):
            t[p, q, mine] = amplitude(total[32 * q:32 * q + 32], first, second, q, mine)

    ca = [[copy(t.at[p, :, mine], t.at[p, :, mine], xs[d], "even" if p == 2 else "all") for d in range(3)] for p in range(3)]

    def begin(copies):
        for c in copies:
            c.start()

    @even
    def _():
        sliced(2, sg, bx, 1, 3)
        begin(ca[2])

    sliced(0, sf, bo, 0, 2)
    begin(ca[0])
    sliced(1, sf, bx, 1, 2)
    odd(lambda: begin(ca[1]))

    def pair(read, first, second, slot, both):
        @pl.loop(0, 4)
        def _(q):
            rows = pl.ds(pl.multiple_of(128 * q, 128), 128)
            tq = read(q, slice(None)).astype(F32)
            turned = jnp.concatenate([read(n, rows).T for n in range(4)], axis=1).astype(F32)
            wide = 2.0 * tq - turned
            gap = vv[q] - eps[first, 0:1, :] - eps[second, 0:1, :]
            esum[slot, 0:1] += jnp.sum(gap * tq * wide, axis=0, keepdims=True)
            if both:
                wt[rows] = wide.astype(BF)
            w[rows] = (2.0 * turned - tq).astype(BF)

    def times(weight, factor):
        return jnp.dot(weight[...], factor, preferred_element_type=F32)

    gram(acc, bo, bo, far, False)

    @pl.loop(0, 4)
    def _(q):
        rows = pl.ds(pl.multiple_of(128 * q, 128), 128)
        a0[q] = amplitude(acc[rows], 0, 0, q, slice(None))

    @even
    def _():
        for c in ca[2]:
            c.wait_send()
        begin(ca[1])
    done.extend(ca[2])

    pair(lambda q, cols: a0[q, :, cols], 0, 0, 0, False)
    gown[...] = times(w, bo[g].reshape(512, 256))

    c_g = copy(out3.at[1], in3.at[1], up1, "even")

    @odd
    def _():
        gram(acc2, bo, bx, far, False)

        @pl.loop(0, 4)
        def _(q):
            rows = pl.ds(pl.multiple_of(128 * q, 128), 128)
            t[2, q] = amplitude(acc2[rows], 1, 0, q, slice(None))
        rg[...] = bo[g]
        pair(lambda q, cols: t[2, q, :, cols], 1, 0, 3, True)

    @even
    def _():
        for c in ca[2]:
            c.wait_recv()
        cr_g.wait_recv()
        pair(lambda q, cols: t[2, q, :, cols], 1, 3, 3, True)

    gf[...] = times(wt, bx[g_up2].reshape(512, 256))

    @even
    def _():
        out3[1] = gf[...].astype(BF)
        c_g.start()

    goth[...] = times(w, rg[...].reshape(512, 256))

    @odd
    def _():
        gown[...] += gf[...]

    c_f = copy(out3.at[0], in3.at[0], up1)
    c_x = copy(out3.at[2], in3.at[2], twin)
    cr_f.wait_recv()
    for c in ca[0]:
        c.wait_recv()
    pair(lambda q, cols: t[0, q, :, cols], 0, 2, 2, True)
    gown[...] += times(w, rf[...].reshape(512, 256))
    gf[...] = times(wt, bo[g_up1].reshape(512, 256))

    @even
    def _():
        c_g.wait_recv()
        gf[...] += in3[1].astype(F32)

    for c in ca[1]:
        c.wait_recv()
    pair(lambda q, cols: t[1, q, :, cols], 1, 2, 1, True)
    out3[0] = (gf[...] + times(wt, bx[g_up1].reshape(512, 256))).astype(BF)
    c_f.start()
    out3[2] = (goth[...] + times(w, rf[...].reshape(512, 256))).astype(BF)
    c_x.start()

    lane = lax.broadcasted_iota(jnp.int32, (8, 128), 1)
    total = [-jnp.sum(esum[n, 0:1], axis=1, keepdims=True) for n in range(4)]
    first_at = 1 + 2 * k
    en[0] = jnp.where(lane == first_at, total[1], jnp.where(lane == 4 - first_at, total[3], 0.0))
    c_e = copy(en.at[0], en.at[1], twin)
    c_e.start()
    kept = jnp.where(lane == 0, total[0], jnp.where(lane == 2, total[2], 0.0))
    c_e.wait_recv()
    energy_ref[...] = (kept + en[1])[0:1, 0:4]

    c_x.wait_recv()
    gown[...] += in3[2].astype(F32)
    c_f.wait_recv()
    gown[...] += in3[0].astype(F32)

    for n in range(4):
        gamma_ref[:, 128 * n:128 * n + 128] = gown[128 * n:128 * n + 128].T

    for name, sender in who.items():
        left = [c for c, n in used if n == name and all(c is not d for d in done)]

        def finish(left=left):
            for c in left:
                c.wait_send()
        finish() if sender is None else pl.when(sender)(finish)


def per_device(factors, occ_energy, vir_energy):
    vmem = pl.BlockSpec(memory_space=pltpu.VMEM)
    gamma, energy = pl.pallas_call(
        kernel,
        out_shape=(
            jax.ShapeDtypeStruct((256, 512), F32),
            jax.ShapeDtypeStruct((1, 4), F32),
        ),
        in_specs=[vmem, pl.BlockSpec(memory_space=pltpu.SMEM), vmem],
        out_specs=(vmem, vmem),
        scratch_shapes=[
            pltpu.VMEM((8, 4, 128, 256), BF),
            pltpu.VMEM((8, 4, 128, 256), BF),
            pltpu.VMEM((8, 4, 32, 256), BF),
            pltpu.VMEM((8, 4, 32, 256), BF),
            pltpu.VMEM((8, 4, 32, 256), BF),
            pltpu.VMEM((4, 128, 256), BF),
            pltpu.VMEM((4, 128, 256), BF),
            pltpu.VMEM((3, 4, 128, 512), BF),
            pltpu.VMEM((4, 128, 512), BF),
            pltpu.VMEM((4, 128, 512), F32),
            pltpu.VMEM((512, 512), F32),
            pltpu.VMEM((512, 512), F32),
            pltpu.VMEM((512, 512), BF),
            pltpu.VMEM((512, 512), BF),
            pltpu.VMEM((512, 256), F32),
            pltpu.VMEM((512, 256), F32),
            pltpu.VMEM((512, 256), F32),
            pltpu.VMEM((3, 512, 256), BF),
            pltpu.VMEM((3, 512, 256), BF),
            pltpu.VMEM((4, 8, 512), F32),
            pltpu.VMEM((4, 8, 512), F32),
            pltpu.VMEM((2, 8, 128), F32),
            pltpu.SemaphoreType.DMA((COPIES,)),
            pltpu.SemaphoreType.DMA((COPIES,)),
        ],
        compiler_params=pltpu.CompilerParams(
            collective_id=0, has_side_effects=True, vmem_limit_bytes=44 << 20
        ),
        name="pairs",
    )(factors.reshape(256, 512), occ_energy, vir_energy.reshape(1, 512))
    return energy, gamma.reshape(256, 1, 512)


def solution(mesh):
    return jax.shard_map(
        per_device,
        mesh=mesh,
        in_specs=(P("aux", "blk", None), P("blk"), P()),
        out_specs=(P("blk", None), P("aux", "blk", None)),
        check_vma=False,
    )
```

```python
import jax
import jax.numpy as jnp
from jax import lax
from jax.experimental import pallas as pl
from jax.experimental.pallas import tpu as pltpu
from jax.sharding import PartitionSpec as P

MESH = pl.DeviceIdType.MESH
BF = jnp.bfloat16
F32 = jnp.float32
NX = 4
NU = 64
HALF = NU // 2
COPIES = 112


def place(x, u, k):
    u = lax.rem(u, NU)
    return lax.rem(u, HALF) * 2 + k, lax.div(u, HALF) * NX + lax.rem(x, NX)


def nt(lhs, rhs):
    return lax.dot_general(lhs, rhs, (((1,), (1,)), ((), ())), preferred_element_type=F32)


def kernel(
    f_ref, occ_ref, vir_ref, gamma_ref, energy_ref,
    bo, bx, sf, sg, sv, rf, rg, t, a0, vv, acc, acc2, w, wt,
    gown, goth, gf, out3, in3, eps, esum, en, send, recv,
):
    b = lax.axis_index("blk")
    a = lax.axis_index("aux")
    k = lax.rem(b, 2)
    h = lax.div(a, NX)
    x = lax.rem(a, NX)
    u = HALF * h + lax.div(b, 2)
    y = lax.rem(u, 4)
    g = NX * h + x
    near = NX * h
    far = NX * (1 - h)
    gfar = far + x
    xs = [place(x + d, u, k) for d in (1, 2, 3)]
    partner = place(x, u + HALF, k)
    twin = place(x, u, 1 - k)
    down1, down2 = place(x, u + NU - 1, k), place(x, u + NU - 2, k)
    up1, up2 = place(x, u + 1, k), place(x, u + 2, k)
    h_down1 = lax.div(lax.rem(u + NU - 1, NU), HALF)
    h_down2 = lax.div(lax.rem(u + NU - 2, NU), HALF)
    g_up1 = NX * lax.div(lax.rem(u + 1, NU), HALF) + x
    h_up1 = lax.div(lax.rem(u + 1, NU), HALF)
    g_up2 = (1 - k) * (NX * lax.div(lax.rem(u + 2, NU), HALF) + x) + k * g
    mine = pl.ds(pl.multiple_of(32 * x, 32), 32)

    barrier = pltpu.get_barrier_semaphore()
    detour, undetour = place(x, u + 3, k), place(x, u + NU - 3, k)
    down4, up4 = place(x, u + NU - 4, k), place(x, u + 4, k)
    others = xs + [partner, twin, down1, down2, up1, up2, detour, undetour, down4, up4]
    for device in others:
        pl.semaphore_signal(barrier, inc=1, device_id=device, device_id_type=MESH)

    who = {
        "all": None,
        "even": k == 0,
        "skip": (k == 0) & (y > 0),
        "relay": (k == 0) & (y == 3),
        "direct": (k == 0) | (y > 0),
        "detour": (k == 1) & (y == 0),
        "detoured": (k == 1) & (y == 3),
    }
    used, done = [], []

    def copy(src, dst, device, sender="all", lands_as=None):
        n = len(used)
        made = pltpu.make_async_remote_copy(
            src_ref=src, dst_ref=dst, send_sem=send.at[n],
            recv_sem=recv.at[n if lands_as is None else slot_of[id(lands_as)]],
            device_id=device, device_id_type=MESH,
        )
        slot_of[id(made)] = n
        used.append((made, sender))
        return made

    slot_of = {}

    def only(sender, body):
        pl.when(who[sender])(body)

    def sent(*copies):
        for c in copies:
            c.wait_send()
            done.append(c)

    def even(body):
        pl.when(k == 0)(body)

    def odd(body):
        pl.when(k == 1)(body)

    bo[g] = f_ref[...].T.reshape(4, 128, 256)
    eps[0] = jnp.full((8, 512), occ_ref[0], F32)
    row = jnp.broadcast_to(vir_ref[...], (128, 512))
    for q in range(4):
        column = jnp.broadcast_to(row[:, 128 * q:128 * q + 128].T[:, 0:1], (128, 512))
        vv[q] = column + row
    esum[...] = jnp.zeros_like(esum)

    pl.semaphore_wait(barrier, len(others))

    def chunk(group, c):
        return bo.at[group, c // 2, pl.ds(64 * (c % 2), 64)]

    cz = [copy(chunk(g, c), chunk(g, c), partner) for c in range(8)]
    cx = [copy(bo.at[g], bo.at[g], xs[d]) for d in range(3)]
    ce = [copy(eps.at[0], eps.at[n], device) for n, device in ((1, twin), (2, down1), (3, down2))]
    cr_f = copy(bo.at[NX * h_down1 + x], rf, down1)
    cr_g = copy(bo.at[NX * h_down2 + x], rg, down2, "even")
    for c in cz[:2] + cx + ce:
        c.start()
    pl.when(y > 0)(cr_f.start)
    pl.when((y > 1) & (k == 0))(cr_g.start)
    near4, far4 = pl.ds(near, NX), pl.ds(far, NX)
    up_near4 = pl.ds(NX * h_up1, NX)
    up_far4 = pl.ds(NX - NX * h_up1, NX)
    ct_near = copy(bo.at[near4], bx.at[near4], twin)

    def slices(groups, up_groups, q):
        own = bo.at[groups, q, mine]
        f = copy(own, sf.at[groups, q], down1, "direct")
        f_out = copy(own, sv.at[groups, q], detour, "detour")
        f_in = copy(sv.at[groups, q], sf.at[groups, q], down4, "detoured", f)
        g = copy(own, sg.at[groups, q], down2, "skip")
        g_in = copy(sf.at[up_groups, q], sg.at[up_groups, q], down1, "relay", g)

        def first():
            only("direct", f.start)
            only("detour", f_out.start)
            only("skip", g.start)

        def second():
            @pl.when(who["detoured"])
            def _():
                f_out.wait_recv()
                f_in.start()

        def third():
            @pl.when(who["relay"])
            def _():
                f.wait_recv()
                g_in.start()

        def last():
            pl.when((k == 1) | (y < 3))(f.wait_recv)
            even(g.wait_recv)

        return first, second, third, last

    to_near = slices(near4, up_near4, slice(None))
    for n in range(3):
        sent(cz[n])
        cz[n + 2].start()
    for c in cx:
        c.wait_recv()
    ct_near.start()
    to_near[0]()
    for n in range(3, 6):
        sent(cz[n])
        cz[n + 2].start()

    def gram(dst, lhs, rhs, base, init):
        @pl.loop(0, 2)
        def _(c):
            total = None
            for n in range(NX):
                part = nt(lhs[base + n].reshape(512, 256), rhs[base + n, pl.ds(2 * c, 2)].reshape(256, 256))
                total = part if total is None else total + part
            cols = pl.ds(pl.multiple_of(256 * c, 256), 256)
            dst[:, cols] = total if init else dst[:, cols] + total

    gram(acc, bo, bo, near, True)
    to_near[1]()
    ct_near.wait_recv()
    odd(lambda: gram(acc2, bo, bx, near, True))

    cxf = [[copy(chunk(gfar, c), chunk(gfar, c), xs[d]) for d in range(3)] for c in range(8)]
    ct_far = [copy(bo.at[far4, q], bx.at[far4, q], twin) for q in range(4)]
    to_far = [slices(far4, up_far4, q) for q in range(4)]
    for step in range(9):
        if step < 8:
            cz[step].wait_recv()
            for c in cxf[step]:
                c.start()
        if step > 0:
            for c in cxf[step - 1]:
                c.wait_recv()
        if step > 0 and step % 2 == 0:
            to_far[step // 2 - 1][0]()
            ct_far[step // 2 - 1].start()
        if step > 1 and step % 2 == 1:
            to_far[step // 2 - 1][1]()
    to_far[3][1]()
    for part in [to_near] + to_far:
        part[2]()
    pl.when(y == 0)(cr_f.start)
    pl.when((y < 2) & (k == 0))(cr_g.start)

    for c in ce + ct_far:
        c.wait_recv()
    for part in [to_near] + to_far:
        part[3]()

    def amplitude(integral, first, second, q, rows):
        gap = vv[q, rows] - eps[first, 0:1, :] - eps[second, 0:1, :]
        return (-integral / gap).astype(BF)

    def sliced(p, piece, whole, first, second):
        halves = []
        for half in range(2):
            total = None
            for n in range(NX):
                group = NX * half + n
                part = nt(piece[group].reshape(128, 256), whole[group].reshape(512, 256))
                total = part if total is None else total + part
            halves.append(total)
        total = halves[0] + halves[1]
        for q in range(4):
            t[p, q, mine] = amplitude(total[32 * q:32 * q + 32], first, second, q, mine)

    ca = [[copy(t.at[p, :, mine], t.at[p, :, mine], xs[d], "even" if p == 2 else "all") for d in range(3)] for p in range(3)]

    def begin(copies):
        for c in copies:
            c.start()

    @even
    def _():
        sliced(2, sg, bx, 1, 3)
        begin(ca[2])

    sliced(0, sf, bo, 0, 2)
    begin(ca[0])
    sliced(1, sf, bx, 1, 2)
    odd(lambda: begin(ca[1]))

    def pair(read, first, second, slot, both):
        @pl.loop(0, 4)
        def _(q):
            rows = pl.ds(pl.multiple_of(128 * q, 128), 128)
            tq = read(q, slice(None)).astype(F32)
            turned = jnp.concatenate([read(n, rows).T for n in range(4)], axis=1).astype(F32)
            wide = 2.0 * tq - turned
            gap = vv[q] - eps[first, 0:1, :] - eps[second, 0:1, :]
            esum[slot, 0:1] += jnp.sum(gap * tq * wide, axis=0, keepdims=True)
            if both:
                wt[rows] = wide.astype(BF)
            w[rows] = (2.0 * turned - tq).astype(BF)

    def times(weight, factor):
        return jnp.dot(weight[...], factor, preferred_element_type=F32)

    gram(acc, bo, bo, far, False)

    @pl.loop(0, 4)
    def _(q):
        rows = pl.ds(pl.multiple_of(128 * q, 128), 128)
        a0[q] = amplitude(acc[rows], 0, 0, q, slice(None))

    @even
    def _():
        for c in ca[2]:
            c.wait_send()
        begin(ca[1])
    done.extend(ca[2])

    pair(lambda q, cols: a0[q, :, cols], 0, 0, 0, False)
    gown[...] = times(w, bo[g].reshape(512, 256))

    c_g = copy(out3.at[1], in3.at[1], up1, "even")

    @odd
    def _():
        gram(acc2, bo, bx, far, False)

        @pl.loop(0, 4)
        def _(q):
            rows = pl.ds(pl.multiple_of(128 * q, 128), 128)
            t[2, q] = amplitude(acc2[rows], 1, 0, q, slice(None))
        rg[...] = bo[g]
        pair(lambda q, cols: t[2, q, :, cols], 1, 0, 3, True)

    @even
    def _():
        for c in ca[2]:
            c.wait_recv()
        cr_g.wait_recv()
        pair(lambda q, cols: t[2, q, :, cols], 1, 3, 3, True)

    gf[...] = times(wt, bx[g_up2].reshape(512, 256))

    @even
    def _():
        out3[1] = gf[...].astype(BF)
        c_g.start()

    goth[...] = times(w, rg[...].reshape(512, 256))

    @odd
    def _():
        gown[...] += gf[...]

    c_f = copy(out3.at[0], in3.at[0], up1)
    c_x = copy(out3.at[2], in3.at[2], twin)
    cr_f.wait_recv()
    for c in ca[0]:
        c.wait_recv()
    pair(lambda q, cols: t[0, q, :, cols], 0, 2, 2, True)
    gown[...] += times(w, rf[...].reshape(512, 256))
    gf[...] = times(wt, bo[g_up1].reshape(512, 256))

    @even
    def _():
        c_g.wait_recv()
        gf[...] += in3[1].astype(F32)

    for c in ca[1]:
        c.wait_recv()
    pair(lambda q, cols: t[1, q, :, cols], 1, 2, 1, True)
    out3[0] = (gf[...] + times(wt, bx[g_up1].reshape(512, 256))).astype(BF)
    c_f.start()
    out3[2] = (goth[...] + times(w, rf[...].reshape(512, 256))).astype(BF)
    c_x.start()

    lane = lax.broadcasted_iota(jnp.int32, (8, 128), 1)
    total = [-jnp.sum(esum[n, 0:1], axis=1, keepdims=True) for n in range(4)]
    first_at = 1 + 2 * k
    en[0] = jnp.where(lane == first_at, total[1], jnp.where(lane == 4 - first_at, total[3], 0.0))
    c_e = copy(en.at[0], en.at[1], twin)
    c_e.start()
    kept = jnp.where(lane == 0, total[0], jnp.where(lane == 2, total[2], 0.0))
    c_e.wait_recv()
    energy_ref[...] = (kept + en[1])[0:1, 0:4]

    c_x.wait_recv()
    gown[...] += in3[2].astype(F32)
    c_f.wait_recv()
    gown[...] += in3[0].astype(F32)

    for n in range(4):
        gamma_ref[:, 128 * n:128 * n + 128] = gown[128 * n:128 * n + 128].T

    for name, sender in who.items():
        left = [c for c, n in used if n == name and all(c is not d for d in done)]

        def finish(left=left):
            for c in left:
                c.wait_send()
        finish() if sender is None else pl.when(sender)(finish)


def per_device(factors, occ_energy, vir_energy):
    vmem = pl.BlockSpec(memory_space=pltpu.VMEM)
    gamma, energy = pl.pallas_call(
        kernel,
        out_shape=(
            jax.ShapeDtypeStruct((256, 512), F32),
            jax.ShapeDtypeStruct((1, 4), F32),
        ),
        in_specs=[vmem, pl.BlockSpec(memory_space=pltpu.SMEM), vmem],
        out_specs=(vmem, vmem),
        scratch_shapes=[
            pltpu.VMEM((8, 4, 128, 256), BF),
            pltpu.VMEM((8, 4, 128, 256), BF),
            pltpu.VMEM((8, 4, 32, 256), BF),
            pltpu.VMEM((8, 4, 32, 256), BF),
            pltpu.VMEM((8, 4, 32, 256), BF),
            pltpu.VMEM((4, 128, 256), BF),
            pltpu.VMEM((4, 128, 256), BF),
            pltpu.VMEM((3, 4, 128, 512), BF),
            pltpu.VMEM((4, 128, 512), BF),
            pltpu.VMEM((4, 128, 512), F32),
            pltpu.VMEM((512, 512), F32),
            pltpu.VMEM((512, 512), F32),
            pltpu.VMEM((512, 512), BF),
            pltpu.VMEM((512, 512), BF),
            pltpu.VMEM((512, 256), F32),
            pltpu.VMEM((512, 256), F32),
            pltpu.VMEM((512, 256), F32),
            pltpu.VMEM((3, 512, 256), BF),
            pltpu.VMEM((3, 512, 256), BF),
            pltpu.VMEM((4, 8, 512), F32),
            pltpu.VMEM((4, 8, 512), F32),
            pltpu.VMEM((2, 8, 128), F32),
            pltpu.SemaphoreType.DMA((COPIES,)),
            pltpu.SemaphoreType.DMA((COPIES,)),
        ],
        compiler_params=pltpu.CompilerParams(
            collective_id=0, has_side_effects=True, vmem_limit_bytes=44 << 20
        ),
        name="pairs",
    )(factors.reshape(256, 512), occ_energy, vir_energy.reshape(1, 512))
    return energy, gamma.reshape(256, 1, 512)


def solution(mesh):
    return jax.shard_map(
        per_device,
        mesh=mesh,
        in_specs=(P("aux", "blk", None), P("blk"), P()),
        out_specs=(P("blk", None), P("aux", "blk", None)),
        check_vma=False,
    )
```

```python
import jax
import jax.numpy as jnp
from jax import lax
from jax.experimental import pallas as pl
from jax.experimental.pallas import tpu as pltpu
from jax.sharding import PartitionSpec as P

MESH = pl.DeviceIdType.MESH
BF = jnp.bfloat16
F32 = jnp.float32
NX = 4
NU = 64
HALF = NU // 2
COPIES = 128


def place(x, u, k):
    u = lax.rem(u, NU)
    return lax.rem(u, HALF) * 2 + k, lax.div(u, HALF) * NX + lax.rem(x, NX)


def nt(lhs, rhs):
    return lax.dot_general(lhs, rhs, (((1,), (1,)), ((), ())), preferred_element_type=F32)


def kernel(
    f_ref, occ_ref, vir_ref, gamma_ref, energy_ref,
    bo, bx, sf, sg, sv, rf, rg, t, a0, vv, acc, acc2, w, wt,
    gown, goth, gf, out3, in3, eps, esum, en, send, recv,
):
    b = lax.axis_index("blk")
    a = lax.axis_index("aux")
    k = lax.rem(b, 2)
    h = lax.div(a, NX)
    x = lax.rem(a, NX)
    u = HALF * h + lax.div(b, 2)
    y = lax.rem(u, 4)
    g = NX * h + x
    near = NX * h
    far = NX * (1 - h)
    gfar = far + x
    xs = [place(x + d, u, k) for d in (1, 2, 3)]
    partner = place(x, u + HALF, k)
    twin = place(x, u, 1 - k)
    down1, down2 = place(x, u + NU - 1, k), place(x, u + NU - 2, k)
    up1, up2 = place(x, u + 1, k), place(x, u + 2, k)
    h_down1 = lax.div(lax.rem(u + NU - 1, NU), HALF)
    h_down2 = lax.div(lax.rem(u + NU - 2, NU), HALF)
    g_up1 = NX * lax.div(lax.rem(u + 1, NU), HALF) + x
    g_up2 = NX * lax.div(lax.rem(u + 2, NU), HALF) + x
    mine = pl.ds(pl.multiple_of(32 * x, 32), 32)

    barrier = pltpu.get_barrier_semaphore()
    detour, undetour = place(x, u + 3, k), place(x, u + NU - 3, k)
    down4, up4 = place(x, u + NU - 4, k), place(x, u + 4, k)
    others = xs + [partner, twin, down1, down2, up1, up2, detour, undetour, down4, up4]
    for device in others:
        pl.semaphore_signal(barrier, inc=1, device_id=device, device_id_type=MESH)

    who = {
        "all": None,
        "even": k == 0,
        "skip": (k == 0) & (y > 0),
        "round": (k == 0) & (y == 0),
        "rounded": (k == 0) & (y == 2),
        "direct": (k == 0) | (y > 0),
        "detour": (k == 1) & (y == 0),
        "detoured": (k == 1) & (y == 3),
    }
    used, done = [], []

    def copy(src, dst, device, sender="all", lands_as=None):
        n = len(used)
        made = pltpu.make_async_remote_copy(
            src_ref=src, dst_ref=dst, send_sem=send.at[n],
            recv_sem=recv.at[n if lands_as is None else slot_of[id(lands_as)]],
            device_id=device, device_id_type=MESH,
        )
        slot_of[id(made)] = n
        used.append((made, sender))
        return made

    slot_of = {}

    def only(sender, body):
        pl.when(who[sender])(body)

    def sent(*copies):
        for c in copies:
            c.wait_send()
            done.append(c)

    def even(body):
        pl.when(k == 0)(body)

    def odd(body):
        pl.when(k == 1)(body)

    bo[g] = f_ref[...].T.reshape(4, 128, 256)
    eps[0] = jnp.full((8, 512), occ_ref[0], F32)
    row = jnp.broadcast_to(vir_ref[...], (128, 512))
    for q in range(4):
        column = jnp.broadcast_to(row[:, 128 * q:128 * q + 128].T[:, 0:1], (128, 512))
        vv[q] = column + row
    esum[...] = jnp.zeros_like(esum)

    pl.semaphore_wait(barrier, len(others))

    def chunk(group, c):
        q, first, rows = ((0, 0, 128), (1, 0, 128), (2, 0, 128), (3, 0, 64), (3, 64, 64))[c]
        return bo.at[group, q, pl.ds(first, rows)]

    cz = [copy(chunk(g, c), chunk(g, c), partner) for c in range(5)]
    cx = [copy(bo.at[g], bo.at[g], xs[d]) for d in range(3)]
    ce = [copy(eps.at[0], eps.at[n], device) for n, device in ((1, twin), (2, down1), (3, down2))]
    cr_f = copy(bo.at[NX * h_down1 + x], rf, down1)
    cr_g = copy(bo.at[NX * h_down2 + x], rg, down2, "even")
    for c in cz[:2] + cx + ce:
        c.start()
    pl.when(y > 0)(cr_f.start)
    pl.when((y > 1) & (k == 0))(cr_g.start)
    near4, far4 = pl.ds(near, NX), pl.ds(far, NX)
    ct_near = copy(bo.at[near4], bx.at[near4], twin)

    def slices(groups, q):
        own = bo.at[groups, q, mine]
        there = sv.at[groups, q]
        f = copy(own, sf.at[groups, q], down1, "direct")
        f_out = copy(own, there, detour, "detour")
        f_in = copy(there, sf.at[groups, q], down4, "detoured", f)
        g = copy(own, sg.at[groups, q], down2, "skip")
        g_out = copy(own, there, up2, "round")
        g_in = copy(there, sg.at[groups, q], down4, "rounded", g)

        def first():
            only("direct", f.start)
            only("detour", f_out.start)
            only("skip", g.start)
            only("round", g_out.start)

        def second():
            @pl.when(who["detoured"])
            def _():
                f_out.wait_recv()
                f_in.start()

            @pl.when(who["rounded"])
            def _():
                g_out.wait_recv()
                g_in.start()

        return first, second, f, g

    to_near = slices(near4, slice(None))
    sent(cz[0])
    cz[2].start()
    for c in cx:
        c.wait_recv()
    ct_near.start()
    to_near[0]()
    sent(cz[1])
    cz[3].start()
    cz[4].start()

    def gram(dst, lhs, rhs, base, init):
        @pl.loop(0, 2)
        def _(c):
            total = None
            for n in range(NX):
                part = nt(lhs[base + n].reshape(512, 256), rhs[base + n, pl.ds(2 * c, 2)].reshape(256, 256))
                total = part if total is None else total + part
            cols = pl.ds(pl.multiple_of(256 * c, 256), 256)
            dst[:, cols] = total if init else dst[:, cols] + total

    gram(acc, bo, bo, near, True)
    to_near[1]()
    ct_near.wait_recv()
    odd(lambda: gram(acc2, bo, bx, near, True))

    cxf = [[copy(chunk(gfar, c), chunk(gfar, c), xs[d]) for d in range(3)] for c in range(5)]
    ct_far = [copy(bo.at[far4, q], bx.at[far4, q], twin) for q in range(4)]
    to_far = [slices(far4, q) for q in range(4)]
    for step in range(6):
        if step < 5:
            cz[step].wait_recv()
            for c in cxf[step]:
                c.start()
        if step > 0:
            for c in cxf[step - 1]:
                c.wait_recv()
        if step in (1, 2, 3, 5):
            q = min(step, 4) - 1
            to_far[q][0]()
            ct_far[q].start()
        if step in (2, 3, 4):
            to_far[step - 2][1]()
    to_far[3][1]()
    pl.when(y == 0)(cr_f.start)
    pl.when((y < 2) & (k == 0))(cr_g.start)

    def amplitude(integral, first, second, q, rows, cols=slice(None)):
        gap = vv[q, rows, cols] - eps[first, 0:1, cols] - eps[second, 0:1, cols]
        return (-integral / gap).astype(BF)

    def tile(piece, pq, whole, wq):
        halves = []
        for half in range(2):
            total = None
            for n in range(NX):
                lhs, rhs = piece[NX * half + n, pq], whole[NX * half + n, wq]
                part = nt(lhs.reshape(-1, 256), rhs.reshape(-1, 256))
                total = part if total is None else total + part
            halves.append(total)
        return halves[0] + halves[1]

    head, tail = slice(0, 384), slice(384, 512)
    early = [[copy(t.at[p, 0:3, mine, head], t.at[p, 0:3, mine, head], xs[d], "even" if p == 2 else "all")
              for d in range(3)] for p in range(3)]
    late = [[copy(src, src, xs[d], "even" if p == 2 else "all") for d in range(3)
             for src in (t.at[p, 3, mine], t.at[p, 0:3, mine, tail])] for p in range(3)]

    def begin(copies):
        for c in copies:
            c.start()

    def arrive(copies):
        for c in copies:
            c.wait_recv()

    def first_batch(p, piece, whole, first, second):
        total = tile(piece, slice(0, 3), whole, slice(0, 3))
        for q in range(3):
            t[p, q, mine, head] = amplitude(total[32 * q:32 * q + 32], first, second, q, mine, head)
        begin(early[p])

    def second_batch(p, piece, whole, first, second):
        t[p, 3, mine] = amplitude(tile(piece, slice(3, 4), whole, slice(0, 4)), first, second, 3, mine)
        total = tile(piece, slice(0, 3), whole, slice(3, 4))
        for q in range(3):
            t[p, q, mine, tail] = amplitude(total[32 * q:32 * q + 32], first, second, q, mine, tail)
        begin(late[p])

    arrive(ce + [to_near[2]] + [part[2] for part in to_far[:3]] + ct_far[:3])
    first_batch(0, sf, bo, 0, 2)
    first_batch(1, sf, bx, 1, 2)

    @even
    def _():
        arrive([to_near[3]] + [part[3] for part in to_far[:3]])
        first_batch(2, sg, bx, 1, 3)

    def pair(read, first, second, slot, both):
        @pl.loop(0, 4)
        def _(q):
            rows = pl.ds(pl.multiple_of(128 * q, 128), 128)
            tq = read(q, slice(None)).astype(F32)
            turned = jnp.concatenate([read(n, rows).T for n in range(4)], axis=1).astype(F32)
            wide = 2.0 * tq - turned
            gap = vv[q] - eps[first, 0:1, :] - eps[second, 0:1, :]
            esum[slot, 0:1] += jnp.sum(gap * tq * wide, axis=0, keepdims=True)
            if both:
                wt[rows] = wide.astype(BF)
            w[rows] = (2.0 * turned - tq).astype(BF)

    def times(weight, factor):
        return jnp.dot(weight[...], factor, preferred_element_type=F32)

    gram(acc, bo, bo, far, False)

    @pl.loop(0, 4)
    def _(q):
        rows = pl.ds(pl.multiple_of(128 * q, 128), 128)
        a0[q] = amplitude(acc[rows], 0, 0, q, slice(None))

    pair(lambda q, cols: a0[q, :, cols], 0, 0, 0, False)
    gown[...] = times(w, bo[g].reshape(512, 256))

    arrive([to_far[3][2], ct_far[3]])
    second_batch(0, sf, bo, 0, 2)
    second_batch(1, sf, bx, 1, 2)

    @even
    def _():
        to_far[3][3].wait_recv()
        second_batch(2, sg, bx, 1, 3)

    @odd
    def _():
        gram(acc2, bo, bx, far, False)

        @pl.loop(0, 4)
        def _(q):
            rows = pl.ds(pl.multiple_of(128 * q, 128), 128)
            t[2, q] = amplitude(acc2[rows], 1, 0, q, slice(None))
        pair(lambda q, cols: t[2, q, :, cols], 1, 0, 3, True)
        gown[...] += times(wt, bx[g].reshape(512, 256))
        goth[...] = times(w, bo[g].reshape(512, 256))

    c_f = copy(out3.at[0], in3.at[0], up1)
    c_g = copy(out3.at[1], in3.at[1], up2, "even")
    c_x = copy(out3.at[2], in3.at[2], twin)
    cr_f.wait_recv()
    arrive(early[0] + late[0])
    pair(lambda q, cols: t[0, q, :, cols], 0, 2, 2, True)
    gf[...] = times(wt, bo[g_up1].reshape(512, 256))
    gown[...] += times(w, rf[...].reshape(512, 256))
    arrive(early[1] + late[1])
    pair(lambda q, cols: t[1, q, :, cols], 1, 2, 1, True)
    out3[0] = (gf[...] + times(wt, bx[g_up1].reshape(512, 256))).astype(BF)
    c_f.start()
    part = times(w, rf[...].reshape(512, 256))

    @odd
    def _():
        out3[2] = (goth[...] + part).astype(BF)
        c_x.start()

    @even
    def _():
        goth[...] = part
        cr_g.wait_recv()
        arrive(early[2] + late[2])
        pair(lambda q, cols: t[2, q, :, cols], 1, 3, 3, True)
        out3[1] = times(wt, bx[g_up2].reshape(512, 256)).astype(BF)
        c_g.start()
        out3[2] = (goth[...] + times(w, rg[...].reshape(512, 256))).astype(BF)
        c_x.start()

    lane = lax.broadcasted_iota(jnp.int32, (8, 128), 1)
    total = [-jnp.sum(esum[n, 0:1], axis=1, keepdims=True) for n in range(4)]
    first_at = 1 + 2 * k
    en[0] = jnp.where(lane == first_at, total[1], jnp.where(lane == 4 - first_at, total[3], 0.0))
    c_e = copy(en.at[0], en.at[1], twin)
    c_e.start()
    kept = jnp.where(lane == 0, total[0], jnp.where(lane == 2, total[2], 0.0))
    c_e.wait_recv()
    energy_ref[...] = (kept + en[1])[0:1, 0:4]

    c_x.wait_recv()
    gown[...] += in3[2].astype(F32)
    c_f.wait_recv()
    gown[...] += in3[0].astype(F32)

    @even
    def _():
        c_g.wait_recv()
        gown[...] += in3[1].astype(F32)

    for n in range(4):
        gamma_ref[:, 128 * n:128 * n + 128] = gown[128 * n:128 * n + 128].T

    for name, sender in who.items():
        left = [c for c, n in used if n == name and all(c is not d for d in done)]

        def finish(left=left):
            for c in left:
                c.wait_send()
        finish() if sender is None else pl.when(sender)(finish)


def per_device(factors, occ_energy, vir_energy):
    vmem = pl.BlockSpec(memory_space=pltpu.VMEM)
    gamma, energy = pl.pallas_call(
        kernel,
        out_shape=(
            jax.ShapeDtypeStruct((256, 512), F32),
            jax.ShapeDtypeStruct((1, 4), F32),
        ),
        in_specs=[vmem, pl.BlockSpec(memory_space=pltpu.SMEM), vmem],
        out_specs=(vmem, vmem),
        scratch_shapes=[
            pltpu.VMEM((8, 4, 128, 256), BF),
            pltpu.VMEM((8, 4, 128, 256), BF),
            pltpu.VMEM((8, 4, 32, 256), BF),
            pltpu.VMEM((8, 4, 32, 256), BF),
            pltpu.VMEM((8, 4, 32, 256), BF),
            pltpu.VMEM((4, 128, 256), BF),
            pltpu.VMEM((4, 128, 256), BF),
            pltpu.VMEM((3, 4, 128, 512), BF),
            pltpu.VMEM((4, 128, 512), BF),
            pltpu.VMEM((4, 128, 512), F32),
            pltpu.VMEM((512, 512), F32),
            pltpu.VMEM((512, 512), F32),
            pltpu.VMEM((512, 512), BF),
            pltpu.VMEM((512, 512), BF),
            pltpu.VMEM((512, 256), F32),
            pltpu.VMEM((512, 256), F32),
            pltpu.VMEM((512, 256), F32),
            pltpu.VMEM((3, 512, 256), BF),
            pltpu.VMEM((3, 512, 256), BF),
            pltpu.VMEM((4, 8, 512), F32),
            pltpu.VMEM((4, 8, 512), F32),
            pltpu.VMEM((2, 8, 128), F32),
            pltpu.SemaphoreType.DMA((COPIES,)),
            pltpu.SemaphoreType.DMA((COPIES,)),
        ],
        compiler_params=pltpu.CompilerParams(
            collective_id=0, has_side_effects=True, vmem_limit_bytes=44 << 20
        ),
        name="pairs",
    )(factors.reshape(256, 512), occ_energy, vir_energy.reshape(1, 512))
    return energy, gamma.reshape(256, 1, 512)


def solution(mesh):
    return jax.shard_map(
        per_device,
        mesh=mesh,
        in_specs=(P("aux", "blk", None), P("blk"), P()),
        out_specs=(P("blk", None), P("aux", "blk", None)),
        check_vma=False,
    )
```

```python
import jax
import jax.numpy as jnp
from jax import lax
from jax.experimental import pallas as pl
from jax.experimental.pallas import tpu as pltpu
from jax.sharding import PartitionSpec as P

MESH = pl.DeviceIdType.MESH
BF = jnp.bfloat16
F32 = jnp.float32
NX = 4
NU = 64
HALF = NU // 2
COPIES = 128


def place(x, u, k):
    u = lax.rem(u, NU)
    return lax.rem(u, HALF) * 2 + k, lax.div(u, HALF) * NX + lax.rem(x, NX)


def nt(lhs, rhs):
    return lax.dot_general(lhs, rhs, (((1,), (1,)), ((), ())), preferred_element_type=F32)


def kernel(
    f_ref, occ_ref, vir_ref, gamma_ref, energy_ref,
    bo, bx, sf, sg, sv, rf, rg, t, a0, vv, acc, acc2, w, wt,
    gown, goth, gf, out3, in3, eps, esum, en, f_own, vir, local, send, recv,
):
    b = lax.axis_index("blk")
    a = lax.axis_index("aux")
    k = lax.rem(b, 2)
    h = lax.div(a, NX)
    x = lax.rem(a, NX)
    u = HALF * h + lax.div(b, 2)
    y = lax.rem(u, 4)
    g = NX * h + x
    near = NX * h
    far = NX * (1 - h)
    gfar = far + x
    xs = [place(x + d, u, k) for d in (1, 2, 3)]
    partner = place(x, u + HALF, k)
    twin = place(x, u, 1 - k)
    down1, down2 = place(x, u + NU - 1, k), place(x, u + NU - 2, k)
    up1, up2 = place(x, u + 1, k), place(x, u + 2, k)
    h_down1 = lax.div(lax.rem(u + NU - 1, NU), HALF)
    h_down2 = lax.div(lax.rem(u + NU - 2, NU), HALF)
    g_up1 = NX * lax.div(lax.rem(u + 1, NU), HALF) + x
    g_up2 = NX * lax.div(lax.rem(u + 2, NU), HALF) + x
    mine = pl.ds(pl.multiple_of(32 * x, 32), 32)

    barrier = pltpu.get_barrier_semaphore()
    down4, up4 = place(x, u + NU - 4, k), place(x, u + 4, k)
    others = xs + [partner, twin, down1, down2, up1, up2, down4, up4]
    for device in others:
        pl.semaphore_signal(barrier, inc=1, device_id=device, device_id_type=MESH)

    who = {
        "all": None,
        "even": k == 0,
        "skip": (k == 0) & (y > 0),
        "round": (k == 0) & (y == 0),
        "rounded": (k == 0) & (y == 2),
    }
    used, done = [], []

    def copy(src, dst, device, sender="all", lands_as=None):
        n = len(used)
        made = pltpu.make_async_remote_copy(
            src_ref=src, dst_ref=dst, send_sem=send.at[n],
            recv_sem=recv.at[n if lands_as is None else slot_of[id(lands_as)]],
            device_id=device, device_id_type=MESH,
        )
        slot_of[id(made)] = n
        used.append((made, sender))
        return made

    slot_of = {}

    def only(sender, body):
        pl.when(who[sender])(body)

    def sent(*copies):
        for c in copies:
            c.wait_send()
            done.append(c)

    def even(body):
        pl.when(k == 0)(body)

    def odd(body):
        pl.when(k == 1)(body)

    reads = [pltpu.make_async_copy(f_ref, f_own, local.at[0]), pltpu.make_async_copy(vir_ref, vir, local.at[1])]
    for c in reads:
        c.start()
    for c in reads:
        c.wait()

    bo[g] = f_own[...].T.reshape(4, 128, 256)
    eps[0] = jnp.full((8, 512), occ_ref[0], F32)
    row = jnp.broadcast_to(vir[...], (128, 512))
    for q in range(4):
        column = jnp.broadcast_to(row[:, 128 * q:128 * q + 128].T[:, 0:1], (128, 512))
        vv[q] = column + row
    esum[...] = jnp.zeros_like(esum)

    pl.semaphore_wait(barrier, len(others))

    def chunk(group, c):
        q, first, rows = ((0, 0, 128), (1, 0, 128), (2, 0, 128), (3, 0, 64), (3, 64, 64))[c]
        return bo.at[group, q, pl.ds(first, rows)]

    cz = [copy(chunk(g, c), chunk(g, c), partner) for c in range(5)]
    cx = [copy(bo.at[g], bo.at[g], xs[d]) for d in range(3)]
    ce = [copy(eps.at[0], eps.at[n], device) for n, device in ((1, twin), (2, down1), (3, down2))]
    cr_f = copy(bo.at[NX * h_down1 + x], rf, down1)
    cr_g = copy(bo.at[NX * h_down2 + x], rg, down2, "even")
    for c in cz[:2] + cx + ce:
        c.start()
    pl.when(y > 0)(cr_f.start)
    pl.when((y > 1) & (k == 0))(cr_g.start)
    near4, far4 = pl.ds(near, NX), pl.ds(far, NX)
    ct_near = copy(bo.at[near4], bx.at[near4], twin)

    def slices(groups, q):
        own = bo.at[groups, q, mine]
        there = sv.at[groups, q]
        f = copy(own, sf.at[groups, q], down1)
        g = copy(own, sg.at[groups, q], down2, "skip")
        g_out = copy(own, there, up2, "round")
        g_in = copy(there, sg.at[groups, q], down4, "rounded", g)

        def first():
            f.start()
            only("skip", g.start)
            only("round", g_out.start)

        def second():
            @pl.when(who["rounded"])
            def _():
                g_out.wait_recv()
                g_in.start()

        return first, second, f, g

    to_near = slices(near4, slice(None))
    sent(cz[0])
    cz[2].start()
    for c in cx:
        c.wait_recv()
    ct_near.start()
    to_near[0]()
    sent(cz[1])
    cz[3].start()
    cz[4].start()

    def gram(dst, lhs, rhs, base, init):
        @pl.loop(0, 2)
        def _(c):
            total = None
            for n in range(NX):
                part = nt(lhs[base + n].reshape(512, 256), rhs[base + n, pl.ds(2 * c, 2)].reshape(256, 256))
                total = part if total is None else total + part
            cols = pl.ds(pl.multiple_of(256 * c, 256), 256)
            dst[:, cols] = total if init else dst[:, cols] + total

    gram(acc, bo, bo, near, True)
    to_near[1]()
    ct_near.wait_recv()
    odd(lambda: gram(acc2, bo, bx, near, True))

    cxf = [[copy(chunk(gfar, c), chunk(gfar, c), xs[d]) for d in range(3)] for c in range(5)]
    ct_far = [copy(bo.at[far4, q], bx.at[far4, q], twin) for q in range(4)]
    to_far = [slices(far4, q) for q in range(4)]
    for step in range(6):
        if step < 5:
            cz[step].wait_recv()
            for c in cxf[step]:
                c.start()
        if step in (2, 3, 4):
            to_far[step - 2][1]()
        if step > 0:
            for c in cxf[step - 1]:
                c.wait_recv()
        if step in (1, 2, 3, 5):
            q = min(step, 4) - 1
            to_far[q][0]()
            ct_far[q].start()
    to_far[3][1]()
    pl.when(y == 0)(cr_f.start)
    pl.when((y < 2) & (k == 0))(cr_g.start)

    def amplitude(integral, first, second, q, rows, cols=slice(None)):
        gap = vv[q, rows, cols] - eps[first, 0:1, cols] - eps[second, 0:1, cols]
        return (-integral / gap).astype(BF)

    def tile(piece, pq, whole, wq):
        halves = []
        for half in range(2):
            total = None
            for n in range(NX):
                lhs, rhs = piece[NX * half + n, pq], whole[NX * half + n, wq]
                part = nt(lhs.reshape(-1, 256), rhs.reshape(-1, 256))
                total = part if total is None else total + part
            halves.append(total)
        return halves[0] + halves[1]

    head, tail = slice(0, 384), slice(384, 512)
    early = [[copy(t.at[p, 0:3, mine, head], t.at[p, 0:3, mine, head], xs[d], "even" if p == 2 else "all")
              for d in range(3)] for p in range(3)]
    late = [[copy(src, src, xs[d], "even" if p == 2 else "all") for d in range(3)
             for src in (t.at[p, 3, mine], t.at[p, 0:3, mine, tail])] for p in range(3)]

    def begin(copies):
        for c in copies:
            c.start()

    def arrive(copies):
        for c in copies:
            c.wait_recv()

    def first_batch(p, piece, whole, first, second):
        total = tile(piece, slice(0, 3), whole, slice(0, 3))
        for q in range(3):
            t[p, q, mine, head] = amplitude(total[32 * q:32 * q + 32], first, second, q, mine, head)
        begin(early[p])

    def second_batch(p, piece, whole, first, second):
        t[p, 3, mine] = amplitude(tile(piece, slice(3, 4), whole, slice(0, 4)), first, second, 3, mine)
        total = tile(piece, slice(0, 3), whole, slice(3, 4))
        for q in range(3):
            t[p, q, mine, tail] = amplitude(total[32 * q:32 * q + 32], first, second, q, mine, tail)
        begin(late[p])

    arrive(ce + [to_near[2]] + [part[2] for part in to_far[:3]] + ct_far[:3])
    first_batch(0, sf, bo, 0, 2)
    first_batch(1, sf, bx, 1, 2)

    @even
    def _():
        arrive([to_near[3]] + [part[3] for part in to_far[:3]])
        first_batch(2, sg, bx, 1, 3)

    def pair(read, first, second, slot, both):
        @pl.loop(0, 4)
        def _(q):
            rows = pl.ds(pl.multiple_of(128 * q, 128), 128)
            tq = read(q, slice(None)).astype(F32)
            turned = jnp.concatenate([read(n, rows).T for n in range(4)], axis=1).astype(F32)
            wide = 2.0 * tq - turned
            gap = vv[q] - eps[first, 0:1, :] - eps[second, 0:1, :]
            esum[slot, 0:1] += jnp.sum(gap * tq * wide, axis=0, keepdims=True)
            if both:
                wt[rows] = wide.astype(BF)
            w[rows] = (2.0 * turned - tq).astype(BF)

    def times(weight, factor):
        return jnp.dot(weight[...], factor, preferred_element_type=F32)

    arrive([to_far[3][2], ct_far[3]])

    @even
    def _():
        to_far[3][3].wait_recv()
        second_batch(2, sg, bx, 1, 3)

    second_batch(0, sf, bo, 0, 2)
    second_batch(1, sf, bx, 1, 2)

    gram(acc, bo, bo, far, False)

    @pl.loop(0, 4)
    def _(q):
        rows = pl.ds(pl.multiple_of(128 * q, 128), 128)
        a0[q] = amplitude(acc[rows], 0, 0, q, slice(None))

    pair(lambda q, cols: a0[q, :, cols], 0, 0, 0, False)
    gown[...] = times(w, bo[g].reshape(512, 256))

    @odd
    def _():
        gram(acc2, bo, bx, far, False)

        @pl.loop(0, 4)
        def _(q):
            rows = pl.ds(pl.multiple_of(128 * q, 128), 128)
            t[2, q] = amplitude(acc2[rows], 1, 0, q, slice(None))
        pair(lambda q, cols: t[2, q, :, cols], 1, 0, 3, True)
        gown[...] += times(wt, bx[g].reshape(512, 256))
        goth[...] = times(w, bo[g].reshape(512, 256))

    c_f = copy(out3.at[0], in3.at[0], up1)
    c_g = copy(out3.at[1], in3.at[1], up2, "even")
    c_x = copy(out3.at[2], in3.at[2], twin)

    @even
    def _():
        arrive(early[2] + late[2])
        pair(lambda q, cols: t[2, q, :, cols], 1, 3, 3, True)
        out3[1] = times(wt, bx[g_up2].reshape(512, 256)).astype(BF)
        c_g.start()
        cr_g.wait_recv()
        goth[...] = times(w, rg[...].reshape(512, 256))

    cr_f.wait_recv()
    arrive(early[0] + late[0])
    pair(lambda q, cols: t[0, q, :, cols], 0, 2, 2, True)
    gf[...] = times(wt, bo[g_up1].reshape(512, 256))
    gown[...] += times(w, rf[...].reshape(512, 256))
    arrive(early[1] + late[1])
    pair(lambda q, cols: t[1, q, :, cols], 1, 2, 1, True)
    out3[0] = (gf[...] + times(wt, bx[g_up1].reshape(512, 256))).astype(BF)
    c_f.start()
    out3[2] = (goth[...] + times(w, rf[...].reshape(512, 256))).astype(BF)
    c_x.start()

    lane = lax.broadcasted_iota(jnp.int32, (8, 128), 1)
    total = [-jnp.sum(esum[n, 0:1], axis=1, keepdims=True) for n in range(4)]
    first_at = 1 + 2 * k
    en[0] = jnp.where(lane == first_at, total[1], jnp.where(lane == 4 - first_at, total[3], 0.0))
    c_e = copy(en.at[0], en.at[1], twin)
    c_e.start()
    kept = jnp.where(lane == 0, total[0], jnp.where(lane == 2, total[2], 0.0))
    c_e.wait_recv()
    energy_ref[...] = (kept + en[1])[0:1, 0:4]

    c_x.wait_recv()
    gown[...] += in3[2].astype(F32)
    c_f.wait_recv()
    gown[...] += in3[0].astype(F32)

    @even
    def _():
        c_g.wait_recv()
        gown[...] += in3[1].astype(F32)

    for n in range(4):
        gamma_ref[:, 128 * n:128 * n + 128] = gown[128 * n:128 * n + 128].T

    for name, sender in who.items():
        left = [c for c, n in used if n == name and all(c is not d for d in done)]

        def finish(left=left):
            for c in left:
                c.wait_send()
        finish() if sender is None else pl.when(sender)(finish)


def per_device(factors, occ_energy, vir_energy):
    vmem = pl.BlockSpec(memory_space=pltpu.VMEM)
    hbm = pl.BlockSpec(memory_space=pl.ANY)
    gamma, energy = pl.pallas_call(
        kernel,
        out_shape=(
            jax.ShapeDtypeStruct((256, 512), F32),
            jax.ShapeDtypeStruct((1, 4), F32),
        ),
        in_specs=[hbm, pl.BlockSpec(memory_space=pltpu.SMEM), hbm],
        out_specs=(vmem, vmem),
        scratch_shapes=[
            pltpu.VMEM((8, 4, 128, 256), BF),
            pltpu.VMEM((8, 4, 128, 256), BF),
            pltpu.VMEM((8, 4, 32, 256), BF),
            pltpu.VMEM((8, 4, 32, 256), BF),
            pltpu.VMEM((8, 4, 32, 256), BF),
            pltpu.VMEM((4, 128, 256), BF),
            pltpu.VMEM((4, 128, 256), BF),
            pltpu.VMEM((3, 4, 128, 512), BF),
            pltpu.VMEM((4, 128, 512), BF),
            pltpu.VMEM((4, 128, 512), F32),
            pltpu.VMEM((512, 512), F32),
            pltpu.VMEM((512, 512), F32),
            pltpu.VMEM((512, 512), BF),
            pltpu.VMEM((512, 512), BF),
            pltpu.VMEM((512, 256), F32),
            pltpu.VMEM((512, 256), F32),
            pltpu.VMEM((512, 256), F32),
            pltpu.VMEM((3, 512, 256), BF),
            pltpu.VMEM((3, 512, 256), BF),
            pltpu.VMEM((4, 8, 512), F32),
            pltpu.VMEM((4, 8, 512), F32),
            pltpu.VMEM((2, 8, 128), F32),
            pltpu.VMEM((256, 512), BF),
            pltpu.VMEM((1, 512), F32),
            pltpu.SemaphoreType.DMA((2,)),
            pltpu.SemaphoreType.DMA((COPIES,)),
            pltpu.SemaphoreType.DMA((COPIES,)),
        ],
        compiler_params=pltpu.CompilerParams(
            collective_id=0, has_side_effects=True, vmem_limit_bytes=60 << 20
        ),
        name="pairs",
    )(factors.reshape(256, 512), occ_energy, vir_energy.reshape(1, 512))
    return energy, gamma.reshape(256, 1, 512)


def solution(mesh):
    return jax.shard_map(
        per_device,
        mesh=mesh,
        in_specs=(P("aux", "blk", None), P("blk"), P()),
        out_specs=(P("blk", None), P("aux", "blk", None)),
        check_vma=False,
    )
```

```python
import jax
import jax.numpy as jnp
from jax import lax
from jax.experimental import pallas as pl
from jax.experimental.pallas import tpu as pltpu
from jax.sharding import PartitionSpec as P

MESH = pl.DeviceIdType.MESH
BF = jnp.bfloat16
F32 = jnp.float32
NX = 4
NU = 64
HALF = NU // 2
COPIES = 128


def place(x, u, k):
    u = lax.rem(u, NU)
    return lax.rem(u, HALF) * 2 + k, lax.div(u, HALF) * NX + lax.rem(x, NX)


def nt(lhs, rhs):
    return lax.dot_general(lhs, rhs, (((1,), (1,)), ((), ())), preferred_element_type=F32)


def kernel(
    f_ref, occ_ref, vir_ref, gamma_ref, energy_ref,
    bo, bx, sf, sg, sv, rf, rg, t, a0, vv, acc, acc2, nacc, w, wt, tt,
    gown, goth, gf, out3, in3, eps, esum, en, f_own, vir, local, send, recv,
):
    b = lax.axis_index("blk")
    a = lax.axis_index("aux")
    k = lax.rem(b, 2)
    h = lax.div(a, NX)
    x = lax.rem(a, NX)
    u = HALF * h + lax.div(b, 2)
    y = lax.rem(u, 4)
    g = NX * h + x
    near = NX * h
    far = NX * (1 - h)
    gfar = far + x
    xs = [place(x + d, u, k) for d in (1, 2, 3)]
    partner = place(x, u + HALF, k)
    twin = place(x, u, 1 - k)
    down1, down2 = place(x, u + NU - 1, k), place(x, u + NU - 2, k)
    up1, up2 = place(x, u + 1, k), place(x, u + 2, k)
    h_down1 = lax.div(lax.rem(u + NU - 1, NU), HALF)
    h_down2 = lax.div(lax.rem(u + NU - 2, NU), HALF)
    h_up1, h_up2 = lax.div(lax.rem(u + 1, NU), HALF), lax.div(lax.rem(u + 2, NU), HALF)
    g_up1, g_up2 = NX * h_up1 + x, NX * h_up2 + x
    mine = pl.ds(pl.multiple_of(32 * x, 32), 32)

    barrier = pltpu.get_barrier_semaphore()
    down4, up4 = place(x, u + NU - 4, k), place(x, u + 4, k)
    others = xs + [partner, twin, down1, down2, up1, up2, down4, up4]
    for device in others:
        pl.semaphore_signal(barrier, inc=1, device_id=device, device_id_type=MESH)

    who = {
        "all": None,
        "even": k == 0,
        "skip": (k == 0) & (y > 0),
        "round": (k == 0) & (y == 0),
        "rounded": (k == 0) & (y == 2),
    }
    used, done = [], []

    def copy(src, dst, device, sender="all", lands_as=None):
        n = len(used)
        made = pltpu.make_async_remote_copy(
            src_ref=src, dst_ref=dst, send_sem=send.at[n],
            recv_sem=recv.at[n if lands_as is None else slot_of[id(lands_as)]],
            device_id=device, device_id_type=MESH,
        )
        slot_of[id(made)] = n
        used.append((made, sender))
        return made

    slot_of = {}

    def only(sender, body):
        pl.when(who[sender])(body)

    def sent(*copies):
        for c in copies:
            c.wait_send()
            done.append(c)

    def even(body):
        pl.when(k == 0)(body)

    def odd(body):
        pl.when(k == 1)(body)

    reads = [pltpu.make_async_copy(f_ref, f_own, local.at[0]), pltpu.make_async_copy(vir_ref, vir, local.at[1])]
    for c in reads:
        c.start()
    for c in reads:
        c.wait()

    bo[g] = f_own[...].T.reshape(4, 128, 256)
    eps[0] = jnp.full((8, 512), occ_ref[0], F32)
    row = jnp.broadcast_to(vir[...], (128, 512))
    for q in range(4):
        column = jnp.broadcast_to(row[:, 128 * q:128 * q + 128].T[:, 0:1], (128, 512))
        vv[q] = column + row
    esum[...] = jnp.zeros_like(esum)

    pl.semaphore_wait(barrier, len(others))

    def chunk(group, c):
        q, first, rows = ((0, 0, 128), (1, 0, 128), (2, 0, 128), (3, 0, 64), (3, 64, 64))[c]
        return bo.at[group, q, pl.ds(first, rows)]

    cz = [copy(chunk(g, c), chunk(g, c), partner) for c in range(5)]
    cx = [copy(bo.at[g], bo.at[g], xs[d]) for d in range(3)]
    ce = [copy(eps.at[0], eps.at[n], device) for n, device in ((1, twin), (2, down1), (3, down2))]
    cr_f = copy(bo.at[NX * h_down1 + x], rf, down1)
    cr_g = copy(bo.at[NX * h_down2 + x], rg, down2, "even")
    for c in cz[:2] + cx + ce:
        c.start()
    pl.when(y > 0)(cr_f.start)
    pl.when((y > 1) & (k == 0))(cr_g.start)
    near4, far4 = pl.ds(near, NX), pl.ds(far, NX)
    ct_near = copy(bo.at[near4], bx.at[near4], twin)

    def slices(groups, q):
        own = bo.at[groups, q, mine]
        there = sv.at[groups, q]
        f = copy(own, sf.at[groups, q], down1)
        g = copy(own, sg.at[groups, q], down2, "skip")
        g_out = copy(own, there, up2, "round")
        g_in = copy(there, sg.at[groups, q], down4, "rounded", g)

        def first():
            f.start()
            only("skip", g.start)
            only("round", g_out.start)

        def second():
            @pl.when(who["rounded"])
            def _():
                g_out.wait_recv()
                g_in.start()

        return first, second, f, g

    to_near = slices(near4, slice(None))
    for n in range(2):
        sent(cz[n])
        cz[n + 2].start()
    for c in cx:
        c.wait_recv()
    ct_near.start()
    to_near[0]()
    sent(cz[2])
    cz[4].start()

    def gram(dst, lhs, rhs, base, init):
        @pl.loop(0, 2)
        def _(c):
            total = None
            for n in range(NX):
                part = nt(lhs[base + n].reshape(512, 256), rhs[base + n, pl.ds(2 * c, 2)].reshape(256, 256))
                total = part if total is None else total + part
            cols = pl.ds(pl.multiple_of(256 * c, 256), 256)
            dst[:, cols] = total if init else dst[:, cols] + total

    gram(acc, bo, bo, near, True)
    ct_near.wait_recv()
    odd(lambda: gram(acc2, bo, bx, near, True))

    def tile(piece, pq, whole, wq, base):
        total = None
        for n in range(NX):
            lhs, rhs = piece[base + n, pq], whole[base + n, wq]
            part = nt(lhs.reshape(-1, 256), rhs.reshape(-1, 256))
            total = part if total is None else total + part
        return total

    every = slice(0, 4)
    first_1, first_2 = NX * h_up1, NX * h_up2
    last_1, last_2 = NX - first_1, NX - first_2

    def half(p, piece, whole, base):
        nacc[p] = tile(piece, every, whole, every, base).reshape(4, 32, 512)

    def halves():
        half(0, sf, bo, first_1)
        half(1, sf, bx, first_1)

    def arrive(copies):
        for c in copies:
            c.wait_recv()

    cxf = [[copy(chunk(gfar, c), chunk(gfar, c), xs[d]) for d in range(3)] for c in range(5)]
    ct_far = [copy(bo.at[far4, q], bx.at[far4, q], twin) for q in range(4)]
    to_far = [slices(far4, q) for q in range(4)]
    for step in range(6):
        if step < 5:
            cz[step].wait_recv()
            for c in cxf[step]:
                c.start()
        if step == 3:
            to_near[1]()
        if step == 4:
            to_near[2].wait_recv()
            pl.when(h_up1 == h)(halves)
        if step > 0:
            arrive(cxf[step - 1])
        if step in (1, 2, 3, 5):
            q = min(step, 4) - 1
            to_far[q][0]()
            ct_far[q].start()
    for part in to_far:
        part[1]()
    pl.when(y == 0)(cr_f.start)
    pl.when((y < 2) & (k == 0))(cr_g.start)

    def amplitude(integral, first, second, q, rows, cols=slice(None)):
        gap = vv[q, rows, cols] - eps[first, 0:1, cols] - eps[second, 0:1, cols]
        return (-integral / gap).astype(BF)

    head, tail = slice(0, 384), slice(384, 512)
    early = [[copy(t.at[p, 0:3, mine, head], t.at[p, 0:3, mine, head], xs[d], "even" if p == 2 else "all")
              for d in range(3)] for p in range(3)]
    late = [[copy(src, src, xs[d], "even" if p == 2 else "all") for d in range(3)
             for src in (t.at[p, 3, mine], t.at[p, 0:3, mine, tail])] for p in range(3)]

    def begin(copies):
        for c in copies:
            c.start()

    def first_batch(p, piece, whole, base, first, second):
        total = tile(piece, slice(0, 3), whole, slice(0, 3), base)
        for q in range(3):
            whole_sum = nacc[p, q, :, head] + total[32 * q:32 * q + 32]
            t[p, q, mine, head] = amplitude(whole_sum, first, second, q, mine, head)
        begin(early[p])

    def second_batch(p, piece, whole, base, first, second):
        total = nacc[p, 3] + tile(piece, slice(3, 4), whole, every, base)
        t[p, 3, mine] = amplitude(total, first, second, 3, mine)
        total = tile(piece, slice(0, 3), whole, slice(3, 4), base)
        for q in range(3):
            whole_sum = nacc[p, q, :, tail] + total[32 * q:32 * q + 32]
            t[p, q, mine, tail] = amplitude(whole_sum, first, second, q, mine, tail)
        begin(late[p])

    @even
    def _():
        to_near[3].wait_recv()
        pl.when(h_up2 == h)(lambda: half(2, sg, bx, first_2))

    gram(acc, bo, bo, far, False)

    @pl.loop(0, 4)
    def _(q):
        rows = pl.ds(pl.multiple_of(128 * q, 128), 128)
        a0[q] = amplitude(acc[rows], 0, 0, q, slice(None))

    arrive(ce + [part[2] for part in to_far[:3]] + ct_far)
    pl.when(h_up1 != h)(halves)
    first_batch(0, sf, bo, last_1, 0, 2)
    first_batch(1, sf, bx, last_1, 1, 2)

    @even
    def _():
        arrive([part[3] for part in to_far[:3]])
        pl.when(h_up2 != h)(lambda: half(2, sg, bx, first_2))
        first_batch(2, sg, bx, last_2, 1, 3)

    to_far[3][2].wait_recv()
    second_batch(0, sf, bo, last_1, 0, 2)
    second_batch(1, sf, bx, last_1, 1, 2)

    @even
    def _():
        to_far[3][3].wait_recv()
        second_batch(2, sg, bx, last_2, 1, 3)

    def weights(p, read, both):
        @pl.loop(0, 4)
        def _(q):
            rows = pl.ds(pl.multiple_of(128 * q, 128), 128)
            turned = jnp.concatenate([read(n, rows).T for n in range(4)], axis=1)
            tt[p, rows] = turned
            tq, turned = read(q, slice(None)).astype(F32), turned.astype(F32)
            if both:
                wt[rows] = (2.0 * tq - turned).astype(BF)
            w[p, rows] = (2.0 * turned - tq).astype(BF)

    def energy(p, read, first, second, slot):
        @pl.loop(0, 4)
        def _(q):
            rows = pl.ds(pl.multiple_of(128 * q, 128), 128)
            tq = read(q, slice(None)).astype(F32)
            gap = vv[q] - eps[first, 0:1, :] - eps[second, 0:1, :]
            wide = 2.0 * tq - tt[p, rows].astype(F32)
            esum[slot, 0:1] += jnp.sum(gap * tq * wide, axis=0, keepdims=True)

    def times(weight, factor):
        return jnp.dot(weight, factor.reshape(512, 256), preferred_element_type=F32)

    def amplitudes(p):
        return lambda q, cols: t[p, q, :, cols]

    def own_amplitudes(q, cols):
        return a0[q, :, cols]

    weights(3, own_amplitudes, False)
    gown[...] = times(w[3], bo[g])

    @odd
    def _():
        gram(acc2, bo, bx, far, False)

        @pl.loop(0, 4)
        def _(q):
            rows = pl.ds(pl.multiple_of(128 * q, 128), 128)
            t[2, q] = amplitude(acc2[rows], 1, 0, q, slice(None))
        weights(2, amplitudes(2), True)
        gown[...] += times(wt[...], bx[g])
        goth[...] = times(w[2], bo[g])

    c_f = copy(out3.at[0], in3.at[0], up1)
    c_g = copy(out3.at[1], in3.at[1], up2, "even")
    c_x = copy(out3.at[2], in3.at[2], twin)

    @even
    def _():
        arrive(early[2] + late[2])
        weights(2, amplitudes(2), True)
        out3[1] = times(wt[...], bx[g_up2]).astype(BF)
        c_g.start()

    arrive(early[0] + late[0])
    weights(0, amplitudes(0), True)
    gf[...] = times(wt[...], bo[g_up1])
    arrive(early[1] + late[1])
    weights(1, amplitudes(1), True)
    out3[0] = (gf[...] + times(wt[...], bx[g_up1])).astype(BF)
    c_f.start()

    @even
    def _():
        cr_g.wait_recv()
        goth[...] = times(w[2], rg[...])

    cr_f.wait_recv()
    out3[2] = (goth[...] + times(w[1], rf[...])).astype(BF)
    c_x.start()
    gown[...] += times(w[0], rf[...])
    energy(3, own_amplitudes, 0, 0, 0)
    energy(0, amplitudes(0), 0, 2, 2)
    energy(1, amplitudes(1), 1, 2, 1)
    energy(2, amplitudes(2), 1, 3 * (1 - k), 3)

    lane = lax.broadcasted_iota(jnp.int32, (8, 128), 1)
    total = [-jnp.sum(esum[n, 0:1], axis=1, keepdims=True) for n in range(4)]
    first_at = 1 + 2 * k
    en[0] = jnp.where(lane == first_at, total[1], jnp.where(lane == 4 - first_at, total[3], 0.0))
    c_e = copy(en.at[0], en.at[1], twin)
    c_e.start()
    kept = jnp.where(lane == 0, total[0], jnp.where(lane == 2, total[2], 0.0))
    c_e.wait_recv()
    energy_ref[...] = (kept + en[1])[0:1, 0:4]

    c_x.wait_recv()
    gown[...] += in3[2].astype(F32)
    c_f.wait_recv()
    gown[...] += in3[0].astype(F32)

    @even
    def _():
        c_g.wait_recv()
        gown[...] += in3[1].astype(F32)

    for n in range(4):
        gamma_ref[:, 128 * n:128 * n + 128] = gown[128 * n:128 * n + 128].T

    for name, sender in who.items():
        left = [c for c, n in used if n == name and all(c is not d for d in done)]

        def finish(left=left):
            for c in left:
                c.wait_send()
        finish() if sender is None else pl.when(sender)(finish)


def per_device(factors, occ_energy, vir_energy):
    vmem = pl.BlockSpec(memory_space=pltpu.VMEM)
    hbm = pl.BlockSpec(memory_space=pl.ANY)
    gamma, energy = pl.pallas_call(
        kernel,
        out_shape=(
            jax.ShapeDtypeStruct((256, 512), F32),
            jax.ShapeDtypeStruct((1, 4), F32),
        ),
        in_specs=[hbm, pl.BlockSpec(memory_space=pltpu.SMEM), hbm],
        out_specs=(vmem, vmem),
        scratch_shapes=[
            pltpu.VMEM((8, 4, 128, 256), BF),
            pltpu.VMEM((8, 4, 128, 256), BF),
            pltpu.VMEM((8, 4, 32, 256), BF),
            pltpu.VMEM((8, 4, 32, 256), BF),
            pltpu.VMEM((8, 4, 32, 256), BF),
            pltpu.VMEM((4, 128, 256), BF),
            pltpu.VMEM((4, 128, 256), BF),
            pltpu.VMEM((3, 4, 128, 512), BF),
            pltpu.VMEM((4, 128, 512), BF),
            pltpu.VMEM((4, 128, 512), F32),
            pltpu.VMEM((512, 512), F32),
            pltpu.VMEM((512, 512), F32),
            pltpu.VMEM((3, 4, 32, 512), F32),
            pltpu.VMEM((4, 512, 512), BF),
            pltpu.VMEM((512, 512), BF),
            pltpu.VMEM((4, 512, 512), BF),
            pltpu.VMEM((512, 256), F32),
            pltpu.VMEM((512, 256), F32),
            pltpu.VMEM((512, 256), F32),
            pltpu.VMEM((3, 512, 256), BF),
            pltpu.VMEM((3, 512, 256), BF),
            pltpu.VMEM((4, 8, 512), F32),
            pltpu.VMEM((4, 8, 512), F32),
            pltpu.VMEM((2, 8, 128), F32),
            pltpu.VMEM((256, 512), BF),
            pltpu.VMEM((1, 512), F32),
            pltpu.SemaphoreType.DMA((2,)),
            pltpu.SemaphoreType.DMA((COPIES,)),
            pltpu.SemaphoreType.DMA((COPIES,)),
        ],
        compiler_params=pltpu.CompilerParams(
            collective_id=0, has_side_effects=True, vmem_limit_bytes=60 << 20
        ),
        name="pairs",
    )(factors.reshape(256, 512), occ_energy, vir_energy.reshape(1, 512))
    return energy, gamma.reshape(256, 1, 512)


def solution(mesh):
    return jax.shard_map(
        per_device,
        mesh=mesh,
        in_specs=(P("aux", "blk", None), P("blk"), P()),
        out_specs=(P("blk", None), P("aux", "blk", None)),
        check_vma=False,
    )
```

```python
import jax
import jax.numpy as jnp
from jax import lax
from jax.experimental import pallas as pl
from jax.experimental.pallas import tpu as pltpu
from jax.sharding import PartitionSpec as P

MESH = pl.DeviceIdType.MESH
BF = jnp.bfloat16
F32 = jnp.float32
NX = 4
NU = 64
HALF = NU // 2
COPIES = 144


def place(x, u, k):
    u = lax.rem(u, NU)
    return lax.rem(u, HALF) * 2 + k, lax.div(u, HALF) * NX + lax.rem(x, NX)


def nt(lhs, rhs):
    return lax.dot_general(lhs, rhs, (((1,), (1,)), ((), ())), preferred_element_type=F32)


def kernel(
    f_ref, occ_ref, vir_ref, gamma_ref, energy_ref,
    bo, bx, sf, sg, sv, rf, rg, t, a0, vv, acc, acc2, nacc, w, wt, tt,
    gown, goth, gf, out3, in3, eps, esum, en, f_own, vir, local, send, recv,
):
    b = lax.axis_index("blk")
    a = lax.axis_index("aux")
    k = lax.rem(b, 2)
    h = lax.div(a, NX)
    x = lax.rem(a, NX)
    u = HALF * h + lax.div(b, 2)
    y = lax.rem(u, 4)
    g = NX * h + x
    near = NX * h
    far = NX * (1 - h)
    gfar = far + x
    xs = [place(x + d, u, k) for d in (1, 2, 3)]
    partner = place(x, u + HALF, k)
    twin = place(x, u, 1 - k)
    down1, down2 = place(x, u + NU - 1, k), place(x, u + NU - 2, k)
    up1, up2 = place(x, u + 1, k), place(x, u + 2, k)
    h_down1 = lax.div(lax.rem(u + NU - 1, NU), HALF)
    h_down2 = lax.div(lax.rem(u + NU - 2, NU), HALF)
    h_up1, h_up2 = lax.div(lax.rem(u + 1, NU), HALF), lax.div(lax.rem(u + 2, NU), HALF)
    g_up1, g_up2 = NX * h_up1 + x, NX * h_up2 + x
    mine = pl.ds(pl.multiple_of(32 * x, 32), 32)

    barrier = pltpu.get_barrier_semaphore()
    down4, up4 = place(x, u + NU - 4, k), place(x, u + 4, k)
    others = xs + [partner, twin, down1, down2, up1, up2, down4, up4]
    for device in others:
        pl.semaphore_signal(barrier, inc=1, device_id=device, device_id_type=MESH)

    who = {
        "all": None,
        "even": k == 0,
        "skip": (k == 0) & (y > 0),
        "round": (k == 0) & (y == 0),
        "rounded": (k == 0) & (y == 2),
    }
    used, done = [], []

    def copy(src, dst, device, sender="all", lands_as=None):
        n = len(used)
        made = pltpu.make_async_remote_copy(
            src_ref=src, dst_ref=dst, send_sem=send.at[n],
            recv_sem=recv.at[n if lands_as is None else slot_of[id(lands_as)]],
            device_id=device, device_id_type=MESH,
        )
        slot_of[id(made)] = n
        used.append((made, sender))
        return made

    slot_of = {}

    def only(sender, body):
        pl.when(who[sender])(body)

    def sent(*copies):
        for c in copies:
            c.wait_send()
            done.append(c)

    def even(body):
        pl.when(k == 0)(body)

    def odd(body):
        pl.when(k == 1)(body)

    reads = [pltpu.make_async_copy(f_ref, f_own, local.at[0]), pltpu.make_async_copy(vir_ref, vir, local.at[1])]
    for c in reads:
        c.start()
    for c in reads:
        c.wait()

    bo[g] = f_own[...].T.reshape(4, 128, 256)
    eps[0] = jnp.full((8, 512), occ_ref[0], F32)
    row = jnp.broadcast_to(vir[...], (128, 512))
    for q in range(4):
        column = jnp.broadcast_to(row[:, 128 * q:128 * q + 128].T[:, 0:1], (128, 512))
        vv[q] = column + row
    esum[...] = jnp.zeros_like(esum)

    pl.semaphore_wait(barrier, len(others))

    def chunk(group, c):
        q, first, rows = ((0, 0, 128), (1, 0, 128), (2, 0, 128), (3, 0, 64), (3, 64, 64))[c]
        return bo.at[group, q, pl.ds(first, rows)]

    cz = [copy(chunk(g, c), chunk(g, c), partner) for c in range(5)]
    cx = [copy(bo.at[g], bo.at[g], xs[d]) for d in range(3)]
    ce = [copy(eps.at[0], eps.at[n], device) for n, device in ((1, twin), (2, down1), (3, down2))]
    cr_f = copy(bo.at[NX * h_down1 + x], rf, down1)
    cr_g = copy(bo.at[NX * h_down2 + x], rg, down2, "even")
    for c in cz[:2] + cx + ce:
        c.start()
    pl.when(y > 0)(cr_f.start)
    pl.when((y > 1) & (k == 0))(cr_g.start)
    near4, far4 = pl.ds(near, NX), pl.ds(far, NX)
    ct_near = copy(bo.at[near4], bx.at[near4], twin)

    def slices(groups, q):
        own = bo.at[groups, q, mine]
        there = sv.at[groups, q]
        f = copy(own, sf.at[groups, q], down1)
        g = copy(own, sg.at[groups, q], down2, "skip")
        g_out = copy(own, there, up2, "round")
        g_in = copy(there, sg.at[groups, q], down4, "rounded", g)

        def first():
            f.start()
            only("skip", g.start)
            only("round", g_out.start)

        def second():
            @pl.when(who["rounded"])
            def _():
                g_out.wait_recv()
                g_in.start()

        return first, second, f, g

    to_near = slices(near4, slice(None))
    sent(cz[0])
    cz[2].start()
    for c in cx:
        c.wait_recv()
    ct_near.start()
    to_near[0]()
    sent(cz[1])
    cz[3].start()
    cz[4].start()

    def gram(dst, lhs, rhs, base, init):
        @pl.loop(0, 2)
        def _(c):
            total = None
            for n in range(NX):
                part = nt(lhs[base + n].reshape(512, 256), rhs[base + n, pl.ds(2 * c, 2)].reshape(256, 256))
                total = part if total is None else total + part
            cols = pl.ds(pl.multiple_of(256 * c, 256), 256)
            dst[:, cols] = total if init else dst[:, cols] + total

    gram(acc, bo, bo, near, True)
    ct_near.wait_recv()
    odd(lambda: gram(acc2, bo, bx, near, True))

    def tile(piece, pq, whole, wq, base):
        total = None
        for n in range(NX):
            lhs, rhs = piece[base + n, pq], whole[base + n, wq]
            part = nt(lhs.reshape(-1, 256), rhs.reshape(-1, 256))
            total = part if total is None else total + part
        return total

    every = slice(0, 4)
    first_1, first_2 = NX * h_up1, NX * h_up2
    last_1, last_2 = NX - first_1, NX - first_2

    def half(p, piece, whole, base):
        nacc[p] = tile(piece, every, whole, every, base).reshape(4, 32, 512)

    def halves():
        half(0, sf, bo, first_1)
        half(1, sf, bx, first_1)

    def arrive(copies):
        for c in copies:
            c.wait_recv()

    cxf = [[copy(chunk(gfar, c), chunk(gfar, c), xs[d]) for d in range(3)] for c in range(5)]
    ct_far = [copy(bo.at[far4, q], bx.at[far4, q], twin) for q in range(4)]
    to_far = [slices(far4, q) for q in range(4)]
    for step in range(6):
        if step < 5:
            cz[step].wait_recv()
            for c in cxf[step]:
                c.start()
        if step == 3:
            to_near[1]()
        if step == 4:
            to_near[2].wait_recv()
            pl.when(h_up1 == h)(halves)
        if step > 0:
            arrive(cxf[step - 1])
        if step in (1, 2, 3, 5):
            q = min(step, 4) - 1
            to_far[q][0]()
            ct_far[q].start()
    for part in to_far[:3]:
        part[1]()
    pl.when(y == 0)(cr_f.start)
    pl.when((y < 2) & (k == 0))(cr_g.start)

    def amplitude(integral, first, second, q, rows, cols=slice(None)):
        gap = vv[q, rows, cols] - eps[first, 0:1, cols] - eps[second, 0:1, cols]
        return (-integral / gap).astype(BF)

    def parts(p, n):
        if n == 1:
            return [t.at[p, 0:2, mine, 0:256]]
        upto, new = slice(0, 128 * n + 128), slice(128 * n, 128 * n + 128)
        return [t.at[p, n, mine, upto], t.at[p, 0:n, mine, new]]

    gather = [
        [[copy(src, src, xs[d], "even" if p == 2 else "all") for d in range(3) for src in parts(p, n)] for n in (1, 2, 3)]
        for p in range(3)
    ]

    def batch(p, n, piece, whole, base, first, second):
        def block(rows, cols):
            total = tile(piece, slice(*rows), whole, slice(*cols), base)
            lanes = slice(128 * cols[0], 128 * cols[1])
            for q in range(*rows):
                start = 32 * (q - rows[0])
                whole_sum = nacc[p, q, :, lanes] + total[start:start + 32]
                t[p, q, mine, lanes] = amplitude(whole_sum, first, second, q, mine, lanes)

        if n == 1:
            block((0, 2), (0, 2))
        else:
            block((n, n + 1), (0, n + 1))
            block((0, n), (n, n + 1))
        for c in gather[p][n - 1]:
            c.start()

    def next_chip(n):
        batch(0, n, sf, bo, last_1, 0, 2)
        batch(1, n, sf, bx, last_1, 1, 2)

    def chip_after(n):
        batch(2, n, sg, bx, last_2, 1, 3)

    arrive(ce + [part[2] for part in to_far[:2]] + ct_far[:2])

    @pl.when(h_up1 != h)
    def _():
        arrive(ct_far[2:])
        halves()

    next_chip(1)
    pl.when(h_up1 == h)(lambda: arrive(ct_far[2:]))
    to_far[3][1]()

    @even
    def _():
        arrive([to_near[3]] + [part[3] for part in to_far[:2]])
        half(2, sg, bx, first_2)
        chip_after(1)

    to_far[2][2].wait_recv()
    next_chip(2)

    @even
    def _():
        to_far[2][3].wait_recv()
        chip_after(2)

    gram(acc, bo, bo, far, False)

    @pl.loop(0, 4)
    def _(q):
        rows = pl.ds(pl.multiple_of(128 * q, 128), 128)
        a0[q] = amplitude(acc[rows], 0, 0, q, slice(None))

    to_far[3][2].wait_recv()
    next_chip(3)

    @even
    def _():
        to_far[3][3].wait_recv()
        chip_after(3)

    def weights(p, read, both):
        @pl.loop(0, 4)
        def _(q):
            rows = pl.ds(pl.multiple_of(128 * q, 128), 128)
            turned = jnp.concatenate([read(n, rows).T for n in range(4)], axis=1)
            tt[p, rows] = turned
            tq, turned = read(q, slice(None)).astype(F32), turned.astype(F32)
            if both:
                wt[rows] = (2.0 * tq - turned).astype(BF)
            w[p, rows] = (2.0 * turned - tq).astype(BF)

    def energy(p, read, first, second, slot):
        @pl.loop(0, 4)
        def _(q):
            rows = pl.ds(pl.multiple_of(128 * q, 128), 128)
            tq = read(q, slice(None)).astype(F32)
            gap = vv[q] - eps[first, 0:1, :] - eps[second, 0:1, :]
            wide = 2.0 * tq - tt[p, rows].astype(F32)
            esum[slot, 0:1] += jnp.sum(gap * tq * wide, axis=0, keepdims=True)

    def times(weight, factor):
        return jnp.dot(weight, factor.reshape(512, 256), preferred_element_type=F32)

    def amplitudes(p):
        return lambda q, cols: t[p, q, :, cols]

    def own_amplitudes(q, cols):
        return a0[q, :, cols]

    weights(3, own_amplitudes, False)
    gown[...] = times(w[3], bo[g])

    @odd
    def _():
        gram(acc2, bo, bx, far, False)

        @pl.loop(0, 4)
        def _(q):
            rows = pl.ds(pl.multiple_of(128 * q, 128), 128)
            t[2, q] = amplitude(acc2[rows], 1, 0, q, slice(None))
        weights(2, amplitudes(2), True)
        gown[...] += times(wt[...], bx[g])
        goth[...] = times(w[2], bo[g])

    c_f = copy(out3.at[0], in3.at[0], up1)
    c_g = copy(out3.at[1], in3.at[1], up2, "even")
    c_x = copy(out3.at[2], in3.at[2], twin)

    @even
    def _():
        arrive(sum(gather[2], []))
        weights(2, amplitudes(2), True)
        out3[1] = times(wt[...], bx[g_up2]).astype(BF)
        c_g.start()

    arrive(sum(gather[0], []))
    weights(0, amplitudes(0), True)
    gf[...] = times(wt[...], bo[g_up1])
    arrive(sum(gather[1], []))
    weights(1, amplitudes(1), True)
    out3[0] = (gf[...] + times(wt[...], bx[g_up1])).astype(BF)
    c_f.start()

    @even
    def _():
        cr_g.wait_recv()
        goth[...] = times(w[2], rg[...])

    cr_f.wait_recv()
    out3[2] = (goth[...] + times(w[1], rf[...])).astype(BF)
    c_x.start()
    gown[...] += times(w[0], rf[...])
    energy(3, own_amplitudes, 0, 0, 0)
    energy(0, amplitudes(0), 0, 2, 2)
    energy(1, amplitudes(1), 1, 2, 1)
    energy(2, amplitudes(2), 1, 3 * (1 - k), 3)

    lane = lax.broadcasted_iota(jnp.int32, (8, 128), 1)
    total = [-jnp.sum(esum[n, 0:1], axis=1, keepdims=True) for n in range(4)]
    first_at = 1 + 2 * k
    en[0] = jnp.where(lane == first_at, total[1], jnp.where(lane == 4 - first_at, total[3], 0.0))
    c_e = copy(en.at[0], en.at[1], twin)
    c_e.start()
    kept = jnp.where(lane == 0, total[0], jnp.where(lane == 2, total[2], 0.0))
    c_e.wait_recv()
    energy_ref[...] = (kept + en[1])[0:1, 0:4]

    c_x.wait_recv()
    gown[...] += in3[2].astype(F32)
    c_f.wait_recv()
    gown[...] += in3[0].astype(F32)

    @even
    def _():
        c_g.wait_recv()
        gown[...] += in3[1].astype(F32)

    for n in range(4):
        gamma_ref[:, 128 * n:128 * n + 128] = gown[128 * n:128 * n + 128].T

    for name, sender in who.items():
        left = [c for c, n in used if n == name and all(c is not d for d in done)]

        def finish(left=left):
            for c in left:
                c.wait_send()
        finish() if sender is None else pl.when(sender)(finish)


def per_device(factors, occ_energy, vir_energy):
    vmem = pl.BlockSpec(memory_space=pltpu.VMEM)
    hbm = pl.BlockSpec(memory_space=pl.ANY)
    gamma, energy = pl.pallas_call(
        kernel,
        out_shape=(
            jax.ShapeDtypeStruct((256, 512), F32),
            jax.ShapeDtypeStruct((1, 4), F32),
        ),
        in_specs=[hbm, pl.BlockSpec(memory_space=pltpu.SMEM), hbm],
        out_specs=(vmem, vmem),
        scratch_shapes=[
            pltpu.VMEM((8, 4, 128, 256), BF),
            pltpu.VMEM((8, 4, 128, 256), BF),
            pltpu.VMEM((8, 4, 32, 256), BF),
            pltpu.VMEM((8, 4, 32, 256), BF),
            pltpu.VMEM((8, 4, 32, 256), BF),
            pltpu.VMEM((4, 128, 256), BF),
            pltpu.VMEM((4, 128, 256), BF),
            pltpu.VMEM((3, 4, 128, 512), BF),
            pltpu.VMEM((4, 128, 512), BF),
            pltpu.VMEM((4, 128, 512), F32),
            pltpu.VMEM((512, 512), F32),
            pltpu.VMEM((512, 512), F32),
            pltpu.VMEM((3, 4, 32, 512), F32),
            pltpu.VMEM((4, 512, 512), BF),
            pltpu.VMEM((512, 512), BF),
            pltpu.VMEM((4, 512, 512), BF),
            pltpu.VMEM((512, 256), F32),
            pltpu.VMEM((512, 256), F32),
            pltpu.VMEM((512, 256), F32),
            pltpu.VMEM((3, 512, 256), BF),
            pltpu.VMEM((3, 512, 256), BF),
            pltpu.VMEM((4, 8, 512), F32),
            pltpu.VMEM((4, 8, 512), F32),
            pltpu.VMEM((2, 8, 128), F32),
            pltpu.VMEM((256, 512), BF),
            pltpu.VMEM((1, 512), F32),
            pltpu.SemaphoreType.DMA((2,)),
            pltpu.SemaphoreType.DMA((COPIES,)),
            pltpu.SemaphoreType.DMA((COPIES,)),
        ],
        compiler_params=pltpu.CompilerParams(
            collective_id=0, has_side_effects=True, vmem_limit_bytes=60 << 20
        ),
        name="pairs",
    )(factors.reshape(256, 512), occ_energy, vir_energy.reshape(1, 512))
    return energy, gamma.reshape(256, 1, 512)


def solution(mesh):
    return jax.shard_map(
        per_device,
        mesh=mesh,
        in_specs=(P("aux", "blk", None), P("blk"), P()),
        out_specs=(P("blk", None), P("aux", "blk", None)),
        check_vma=False,
    )
```

```python
import jax
import jax.numpy as jnp
from jax import lax
from jax.experimental import pallas as pl
from jax.experimental.pallas import tpu as pltpu
from jax.sharding import PartitionSpec as P

MESH = pl.DeviceIdType.MESH
BF = jnp.bfloat16
F32 = jnp.float32
NX = 4
NU = 64
HALF = NU // 2
COPIES = 144


def place(x, u, k):
    u = lax.rem(u, NU)
    return lax.rem(u, HALF) * 2 + k, lax.div(u, HALF) * NX + lax.rem(x, NX)


def nt(lhs, rhs):
    return lax.dot_general(lhs, rhs, (((1,), (1,)), ((), ())), preferred_element_type=F32)


def kernel(
    f_ref, occ_ref, vir_ref, gamma_ref, energy_ref,
    bo, bx, sf, sg, sv, rf, rg, t, a0, vv, acc, acc2, nacc, w, wt, tt,
    gown, goth, gf, out3, in3, eps, esum, en, f_own, vir, local, send, recv,
):
    b = lax.axis_index("blk")
    a = lax.axis_index("aux")
    k = lax.rem(b, 2)
    h = lax.div(a, NX)
    x = lax.rem(a, NX)
    u = HALF * h + lax.div(b, 2)
    y = lax.rem(u, 4)
    g = NX * h + x
    near = NX * h
    far = NX * (1 - h)
    gfar = far + x
    xs = [place(x + d, u, k) for d in (1, 2, 3)]
    partner = place(x, u + HALF, k)
    twin = place(x, u, 1 - k)
    down1, down2 = place(x, u + NU - 1, k), place(x, u + NU - 2, k)
    up1, up2 = place(x, u + 1, k), place(x, u + 2, k)
    h_down1 = lax.div(lax.rem(u + NU - 1, NU), HALF)
    h_down2 = lax.div(lax.rem(u + NU - 2, NU), HALF)
    h_up1, h_up2 = lax.div(lax.rem(u + 1, NU), HALF), lax.div(lax.rem(u + 2, NU), HALF)
    g_up1, g_up2 = NX * h_up1 + x, NX * h_up2 + x
    mine = pl.ds(pl.multiple_of(32 * x, 32), 32)

    barrier = pltpu.get_barrier_semaphore()
    down4, up4 = place(x, u + NU - 4, k), place(x, u + 4, k)
    others = xs + [partner, twin, down1, down2, up1, up2, down4, up4]
    for device in others:
        pl.semaphore_signal(barrier, inc=1, device_id=device, device_id_type=MESH)

    who = {
        "all": None,
        "even": k == 0,
        "skip": (k == 0) & (y > 0),
        "round": (k == 0) & (y == 0),
        "rounded": (k == 0) & (y == 2),
    }
    used, done = [], []

    def copy(src, dst, device, sender="all", lands_as=None):
        n = len(used)
        made = pltpu.make_async_remote_copy(
            src_ref=src, dst_ref=dst, send_sem=send.at[n],
            recv_sem=recv.at[n if lands_as is None else slot_of[id(lands_as)]],
            device_id=device, device_id_type=MESH,
        )
        slot_of[id(made)] = n
        used.append((made, sender))
        return made

    slot_of = {}

    def only(sender, body):
        pl.when(who[sender])(body)

    def sent(*copies):
        for c in copies:
            c.wait_send()
            done.append(c)

    def even(body):
        pl.when(k == 0)(body)

    def odd(body):
        pl.when(k == 1)(body)

    reads = [pltpu.make_async_copy(f_ref, f_own, local.at[0]), pltpu.make_async_copy(vir_ref, vir, local.at[1])]
    for c in reads:
        c.start()
    for c in reads:
        c.wait()

    bo[g] = f_own[...].T.reshape(4, 128, 256)
    eps[0] = jnp.full((8, 512), occ_ref[0], F32)
    row = jnp.broadcast_to(vir[...], (128, 512))
    for q in range(4):
        column = jnp.broadcast_to(row[:, 128 * q:128 * q + 128].T[:, 0:1], (128, 512))
        vv[q] = column + row
    esum[...] = jnp.zeros_like(esum)

    pl.semaphore_wait(barrier, len(others))

    def chunk(group, c):
        q, first, rows = ((0, 0, 128), (1, 0, 128), (2, 0, 128), (3, 0, 64), (3, 64, 64))[c]
        return bo.at[group, q, pl.ds(first, rows)]

    cz = [copy(chunk(g, c), chunk(g, c), partner) for c in range(5)]
    cx = [copy(bo.at[g], bo.at[g], xs[d]) for d in range(3)]
    ce = [copy(eps.at[0], eps.at[n], device) for n, device in ((1, twin), (2, down1), (3, down2))]
    cr_f = copy(bo.at[NX * h_down1 + x], rf, down1)
    cr_g = copy(bo.at[NX * h_down2 + x], rg, down2, "even")
    for c in cz[:2] + cx + ce:
        c.start()
    pl.when(y > 0)(cr_f.start)
    pl.when((y > 1) & (k == 0))(cr_g.start)
    near4, far4 = pl.ds(near, NX), pl.ds(far, NX)
    ct_near = copy(bo.at[near4], bx.at[near4], twin)

    def slices(groups, q):
        own = bo.at[groups, q, mine]
        there = sv.at[groups, q]
        f = copy(own, sf.at[groups, q], down1)
        g = copy(own, sg.at[groups, q], down2, "skip")
        g_out = copy(own, there, up2, "round")
        g_in = copy(there, sg.at[groups, q], down4, "rounded", g)

        def first():
            f.start()
            only("skip", g.start)
            only("round", g_out.start)

        def second():
            @pl.when(who["rounded"])
            def _():
                g_out.wait_recv()
                g_in.start()

        return first, second, f, g

    to_near = slices(near4, slice(None))
    sent(cz[0])
    cz[2].start()
    for c in cx:
        c.wait_recv()
    ct_near.start()
    to_near[0]()
    sent(cz[1])
    cz[3].start()
    cz[4].start()

    def gram(dst, lhs, rhs, base, init):
        @pl.loop(0, 2)
        def _(c):
            total = None
            for n in range(NX):
                part = nt(lhs[base + n].reshape(512, 256), rhs[base + n, pl.ds(2 * c, 2)].reshape(256, 256))
                total = part if total is None else total + part
            cols = pl.ds(pl.multiple_of(256 * c, 256), 256)
            dst[:, cols] = total if init else dst[:, cols] + total

    gram(acc, bo, bo, near, True)
    ct_near.wait_recv()
    odd(lambda: gram(acc2, bo, bx, near, True))

    def tile(piece, pq, whole, wq, base):
        total = None
        for n in range(NX):
            lhs, rhs = piece[base + n, pq], whole[base + n, wq]
            part = nt(lhs.reshape(-1, 256), rhs.reshape(-1, 256))
            total = part if total is None else total + part
        return total

    every = slice(0, 4)
    first_1, first_2 = NX * h_up1, NX * h_up2
    last_1, last_2 = NX - first_1, NX - first_2

    def half(p, piece, whole, base):
        nacc[p] = tile(piece, every, whole, every, base).reshape(4, 32, 512)

    def halves():
        half(0, sf, bo, first_1)
        half(1, sf, bx, first_1)

    def arrive(copies):
        for c in copies:
            c.wait_recv()

    cxf = [[copy(chunk(gfar, c), chunk(gfar, c), xs[d]) for d in range(3)] for c in range(5)]
    ct_far = [copy(bo.at[far4, q], bx.at[far4, q], twin) for q in range(4)]
    to_far = [slices(far4, q) for q in range(4)]
    for step in range(6):
        if step < 5:
            cz[step].wait_recv()
            for c in cxf[step]:
                c.start()
        if step == 3:
            to_near[1]()
        if step == 4:
            to_near[2].wait_recv()
            pl.when(h_up1 == h)(halves)
        if step > 0:
            arrive(cxf[step - 1])
        if step in (1, 2, 3, 5):
            q = min(step, 4) - 1
            to_far[q][0]()
            ct_far[q].start()
    for part in to_far[:3]:
        part[1]()
    pl.when(y == 0)(cr_f.start)
    pl.when((y < 2) & (k == 0))(cr_g.start)

    def amplitude(integral, first, second, q, rows, cols=slice(None)):
        gap = vv[q, rows, cols] - eps[first, 0:1, cols] - eps[second, 0:1, cols]
        return (-integral / gap).astype(BF)

    def parts(p, n, rows):
        if n == 1:
            return [t.at[p, 0:2, rows, 0:256]]
        upto, new = slice(0, 128 * n + 128), slice(128 * n, 128 * n + 128)
        return [t.at[p, n, rows, upto], t.at[p, 0:n, rows, new]]

    step_x = 1 - 2 * k
    ahead, behind = place(x + NX + step_x, u, k), place(x + NX - step_x, u, k)
    theirs = pl.ds(pl.multiple_of(32 * lax.rem(x + NX - step_x, NX), 32), 32)
    by_core = ["all", "all", "even"]
    to_ahead, to_behind, passed = [
        [[[copy(src, src, device, by_core[p]) for src in parts(p, n, rows)] for n in (1, 2, 3)] for p in range(3)]
        for device, rows in ((ahead, mine), (behind, mine), (ahead, theirs))
    ]

    def pass_on(p, n):
        for got, on in zip(to_ahead[p][n - 1], passed[p][n - 1]):
            got.wait_recv()
            on.start()

    def pass_all(n):
        pass_on(0, n)
        pass_on(1, n)
        even(lambda: pass_on(2, n))

    def gathered(p):
        for n in range(3):
            arrive(to_behind[p][n] + passed[p][n])

    def batch(p, n, piece, whole, base, first, second):
        def block(rows, cols):
            total = tile(piece, slice(*rows), whole, slice(*cols), base)
            lanes = slice(128 * cols[0], 128 * cols[1])
            for q in range(*rows):
                start = 32 * (q - rows[0])
                whole_sum = nacc[p, q, :, lanes] + total[start:start + 32]
                t[p, q, mine, lanes] = amplitude(whole_sum, first, second, q, mine, lanes)

        if n == 1:
            block((0, 2), (0, 2))
        else:
            block((n, n + 1), (0, n + 1))
            block((0, n), (n, n + 1))
        for c in to_ahead[p][n - 1] + to_behind[p][n - 1]:
            c.start()

    def next_chip(n):
        batch(0, n, sf, bo, last_1, 0, 2)
        batch(1, n, sf, bx, last_1, 1, 2)

    def chip_after(n):
        batch(2, n, sg, bx, last_2, 1, 3)

    arrive(ce + [part[2] for part in to_far[:2]] + ct_far[:2])

    @pl.when(h_up1 != h)
    def _():
        arrive(ct_far[2:])
        halves()

    next_chip(1)
    pl.when(h_up1 == h)(lambda: arrive(ct_far[2:]))
    to_far[3][1]()

    @even
    def _():
        arrive([to_near[3]] + [part[3] for part in to_far[:2]])
        half(2, sg, bx, first_2)
        chip_after(1)

    to_far[2][2].wait_recv()
    next_chip(2)

    @even
    def _():
        to_far[2][3].wait_recv()
        chip_after(2)

    pass_all(1)

    gram(acc, bo, bo, far, False)

    @pl.loop(0, 4)
    def _(q):
        rows = pl.ds(pl.multiple_of(128 * q, 128), 128)
        a0[q] = amplitude(acc[rows], 0, 0, q, slice(None))

    to_far[3][2].wait_recv()
    next_chip(3)

    @even
    def _():
        to_far[3][3].wait_recv()
        chip_after(3)

    pass_all(2)

    def weights(p, read, both):
        @pl.loop(0, 4)
        def _(q):
            rows = pl.ds(pl.multiple_of(128 * q, 128), 128)
            turned = jnp.concatenate([read(n, rows).T for n in range(4)], axis=1)
            tt[p, rows] = turned
            tq, turned = read(q, slice(None)).astype(F32), turned.astype(F32)
            if both:
                wt[rows] = (2.0 * tq - turned).astype(BF)
            w[p, rows] = (2.0 * turned - tq).astype(BF)

    def energy(p, read, first, second, slot):
        @pl.loop(0, 4)
        def _(q):
            rows = pl.ds(pl.multiple_of(128 * q, 128), 128)
            tq = read(q, slice(None)).astype(F32)
            gap = vv[q] - eps[first, 0:1, :] - eps[second, 0:1, :]
            wide = 2.0 * tq - tt[p, rows].astype(F32)
            esum[slot, 0:1] += jnp.sum(gap * tq * wide, axis=0, keepdims=True)

    def times(weight, factor):
        return jnp.dot(weight, factor.reshape(512, 256), preferred_element_type=F32)

    def amplitudes(p):
        return lambda q, cols: t[p, q, :, cols]

    def own_amplitudes(q, cols):
        return a0[q, :, cols]

    weights(3, own_amplitudes, False)
    gown[...] = times(w[3], bo[g])

    pass_all(3)

    @odd
    def _():
        gram(acc2, bo, bx, far, False)

        @pl.loop(0, 4)
        def _(q):
            rows = pl.ds(pl.multiple_of(128 * q, 128), 128)
            t[2, q] = amplitude(acc2[rows], 1, 0, q, slice(None))
        weights(2, amplitudes(2), True)
        gown[...] += times(wt[...], bx[g])
        goth[...] = times(w[2], bo[g])

    c_f = copy(out3.at[0], in3.at[0], up1)
    c_g = copy(out3.at[1], in3.at[1], up1, "even")
    c_x = copy(out3.at[2], in3.at[2], twin)

    @even
    def _():
        gathered(2)
        weights(2, amplitudes(2), True)
        out3[1] = times(wt[...], bx[g_up2]).astype(BF)
        c_g.start()

    gathered(0)
    weights(0, amplitudes(0), True)
    gf[...] = times(wt[...], bo[g_up1])
    gathered(1)
    weights(1, amplitudes(1), True)
    gf[...] += times(wt[...], bx[g_up1])

    @even
    def _():
        c_g.wait_recv()
        gf[...] += in3[1].astype(F32)

    out3[0] = gf[...].astype(BF)
    c_f.start()

    @even
    def _():
        cr_g.wait_recv()
        goth[...] = times(w[2], rg[...])

    cr_f.wait_recv()
    out3[2] = (goth[...] + times(w[1], rf[...])).astype(BF)
    c_x.start()
    gown[...] += times(w[0], rf[...])
    energy(3, own_amplitudes, 0, 0, 0)
    energy(0, amplitudes(0), 0, 2, 2)
    energy(1, amplitudes(1), 1, 2, 1)
    energy(2, amplitudes(2), 1, 3 * (1 - k), 3)

    lane = lax.broadcasted_iota(jnp.int32, (8, 128), 1)
    total = [-jnp.sum(esum[n, 0:1], axis=1, keepdims=True) for n in range(4)]
    first_at = 1 + 2 * k
    en[0] = jnp.where(lane == first_at, total[1], jnp.where(lane == 4 - first_at, total[3], 0.0))
    c_e = copy(en.at[0], en.at[1], twin)
    c_e.start()
    kept = jnp.where(lane == 0, total[0], jnp.where(lane == 2, total[2], 0.0))
    c_e.wait_recv()
    energy_ref[...] = (kept + en[1])[0:1, 0:4]

    c_x.wait_recv()
    gown[...] += in3[2].astype(F32)
    c_f.wait_recv()
    gown[...] += in3[0].astype(F32)

    for n in range(4):
        gamma_ref[:, 128 * n:128 * n + 128] = gown[128 * n:128 * n + 128].T

    for name, sender in who.items():
        left = [c for c, n in used if n == name and all(c is not d for d in done)]

        def finish(left=left):
            for c in left:
                c.wait_send()
        finish() if sender is None else pl.when(sender)(finish)


def per_device(factors, occ_energy, vir_energy):
    vmem = pl.BlockSpec(memory_space=pltpu.VMEM)
    hbm = pl.BlockSpec(memory_space=pl.ANY)
    gamma, energy = pl.pallas_call(
        kernel,
        out_shape=(
            jax.ShapeDtypeStruct((256, 512), F32),
            jax.ShapeDtypeStruct((1, 4), F32),
        ),
        in_specs=[hbm, pl.BlockSpec(memory_space=pltpu.SMEM), hbm],
        out_specs=(vmem, vmem),
        scratch_shapes=[
            pltpu.VMEM((8, 4, 128, 256), BF),
            pltpu.VMEM((8, 4, 128, 256), BF),
            pltpu.VMEM((8, 4, 32, 256), BF),
            pltpu.VMEM((8, 4, 32, 256), BF),
            pltpu.VMEM((8, 4, 32, 256), BF),
            pltpu.VMEM((4, 128, 256), BF),
            pltpu.VMEM((4, 128, 256), BF),
            pltpu.VMEM((3, 4, 128, 512), BF),
            pltpu.VMEM((4, 128, 512), BF),
            pltpu.VMEM((4, 128, 512), F32),
            pltpu.VMEM((512, 512), F32),
            pltpu.VMEM((512, 512), F32),
            pltpu.VMEM((3, 4, 32, 512), F32),
            pltpu.VMEM((4, 512, 512), BF),
            pltpu.VMEM((512, 512), BF),
            pltpu.VMEM((4, 512, 512), BF),
            pltpu.VMEM((512, 256), F32),
            pltpu.VMEM((512, 256), F32),
            pltpu.VMEM((512, 256), F32),
            pltpu.VMEM((3, 512, 256), BF),
            pltpu.VMEM((3, 512, 256), BF),
            pltpu.VMEM((4, 8, 512), F32),
            pltpu.VMEM((4, 8, 512), F32),
            pltpu.VMEM((2, 8, 128), F32),
            pltpu.VMEM((256, 512), BF),
            pltpu.VMEM((1, 512), F32),
            pltpu.SemaphoreType.DMA((2,)),
            pltpu.SemaphoreType.DMA((COPIES,)),
            pltpu.SemaphoreType.DMA((COPIES,)),
        ],
        compiler_params=pltpu.CompilerParams(
            collective_id=0, has_side_effects=True, vmem_limit_bytes=60 << 20
        ),
        name="pairs",
    )(factors.reshape(256, 512), occ_energy, vir_energy.reshape(1, 512))
    return energy, gamma.reshape(256, 1, 512)


def solution(mesh):
    return jax.shard_map(
        per_device,
        mesh=mesh,
        in_specs=(P("aux", "blk", None), P("blk"), P()),
        out_specs=(P("blk", None), P("aux", "blk", None)),
        check_vma=False,
    )
```

```python
import jax
import jax.numpy as jnp
from jax import lax
from jax.experimental import pallas as pl
from jax.experimental.pallas import tpu as pltpu
from jax.sharding import PartitionSpec as P

MESH = pl.DeviceIdType.MESH
BF = jnp.bfloat16
F32 = jnp.float32
NX = 4
NU = 64
HALF = NU // 2
COPIES = 144


def place(x, u, k):
    u = lax.rem(u, NU)
    return lax.rem(u, HALF) * 2 + k, lax.div(u, HALF) * NX + lax.rem(x, NX)


def nt(lhs, rhs):
    return lax.dot_general(lhs, rhs, (((1,), (1,)), ((), ())), preferred_element_type=F32)


def kernel(
    f_ref, occ_ref, vir_ref, gamma_ref, energy_ref,
    bo, bx, sf, sg, sv, rf, rg, t, a0, vv, acc, acc2, nacc, w, wt, tt,
    gown, goth, gf, out3, in3, eps, esum, en, f_own, vir, local, send, recv,
):
    b = lax.axis_index("blk")
    a = lax.axis_index("aux")
    k = lax.rem(b, 2)
    h = lax.div(a, NX)
    x = lax.rem(a, NX)
    u = HALF * h + lax.div(b, 2)
    y = lax.rem(u, 4)
    g = NX * h + x
    near = NX * h
    far = NX * (1 - h)
    gfar = far + x
    xs = [place(x + d, u, k) for d in (1, 2, 3)]
    partner = place(x, u + HALF, k)
    twin = place(x, u, 1 - k)
    down1, down2 = place(x, u + NU - 1, k), place(x, u + NU - 2, k)
    up1, up2 = place(x, u + 1, k), place(x, u + 2, k)
    h_down1 = lax.div(lax.rem(u + NU - 1, NU), HALF)
    h_down2 = lax.div(lax.rem(u + NU - 2, NU), HALF)
    h_up1, h_up2 = lax.div(lax.rem(u + 1, NU), HALF), lax.div(lax.rem(u + 2, NU), HALF)
    g_up1, g_up2 = NX * h_up1 + x, NX * h_up2 + x
    mine = pl.ds(pl.multiple_of(32 * x, 32), 32)

    barrier = pltpu.get_barrier_semaphore()
    down4, up4 = place(x, u + NU - 4, k), place(x, u + 4, k)
    others = xs + [partner, twin, down1, down2, up1, up2, down4, up4]
    for device in others:
        pl.semaphore_signal(barrier, inc=1, device_id=device, device_id_type=MESH)

    who = {
        "all": None,
        "even": k == 0,
        "skip": (k == 0) & (y > 0),
        "round": (k == 0) & (y == 0),
        "rounded": (k == 0) & (y == 2),
    }
    used, done = [], []

    def copy(src, dst, device, sender="all", lands_as=None):
        n = len(used)
        made = pltpu.make_async_remote_copy(
            src_ref=src, dst_ref=dst, send_sem=send.at[n],
            recv_sem=recv.at[n if lands_as is None else slot_of[id(lands_as)]],
            device_id=device, device_id_type=MESH,
        )
        slot_of[id(made)] = n
        used.append((made, sender))
        return made

    slot_of = {}

    def only(sender, body):
        pl.when(who[sender])(body)

    def sent(*copies):
        for c in copies:
            c.wait_send()
            done.append(c)

    def even(body):
        pl.when(k == 0)(body)

    def odd(body):
        pl.when(k == 1)(body)

    reads = [pltpu.make_async_copy(f_ref, f_own, local.at[0]), pltpu.make_async_copy(vir_ref, vir, local.at[1])]
    for c in reads:
        c.start()
    for c in reads:
        c.wait()

    bo[g] = f_own[...].T.reshape(4, 128, 256)
    eps[0] = jnp.full((8, 512), occ_ref[0], F32)
    row = jnp.broadcast_to(vir[...], (128, 512))
    for q in range(4):
        column = jnp.broadcast_to(row[:, 128 * q:128 * q + 128].T[:, 0:1], (128, 512))
        vv[q] = column + row
    esum[...] = jnp.zeros_like(esum)

    pl.semaphore_wait(barrier, len(others))

    def chunk(group, c):
        q, first, rows = ((0, 0, 128), (1, 0, 128), (2, 0, 128), (3, 0, 64), (3, 64, 64))[c]
        return bo.at[group, q, pl.ds(first, rows)]

    cz = [copy(chunk(g, c), chunk(g, c), partner) for c in range(5)]
    cx = [copy(bo.at[g], bo.at[g], xs[d]) for d in range(3)]
    ce = [copy(eps.at[0], eps.at[n], device) for n, device in ((1, twin), (2, down1), (3, down2))]
    cr_f = copy(bo.at[NX * h_down1 + x], rf, down1)
    cr_g = copy(bo.at[NX * h_down2 + x], rg, down2, "even")
    for c in cz[:2] + cx + ce:
        c.start()
    pl.when(y > 0)(cr_f.start)
    pl.when((y > 1) & (k == 0))(cr_g.start)
    near4, far4 = pl.ds(near, NX), pl.ds(far, NX)
    ct_near = copy(bo.at[near4], bx.at[near4], twin)

    def slices(groups, q):
        own = bo.at[groups, q, mine]
        there = sv.at[groups, q]
        f = copy(own, sf.at[groups, q], down1)
        g = copy(own, sg.at[groups, q], down2, "skip")
        g_out = copy(own, there, up2, "round")
        g_in = copy(there, sg.at[groups, q], down4, "rounded", g)

        def first():
            f.start()
            only("skip", g.start)
            only("round", g_out.start)

        def second():
            @pl.when(who["rounded"])
            def _():
                g_out.wait_recv()
                g_in.start()

        return first, second, f, g

    to_near = slices(near4, slice(None))
    sent(cz[0])
    cz[2].start()
    for c in cx:
        c.wait_recv()
    ct_near.start()
    to_near[0]()
    sent(cz[1])
    cz[3].start()
    cz[4].start()

    def gram(dst, lhs, rhs, base, init):
        @pl.loop(0, 2)
        def _(c):
            total = None
            for n in range(NX):
                part = nt(lhs[base + n].reshape(512, 256), rhs[base + n, pl.ds(2 * c, 2)].reshape(256, 256))
                total = part if total is None else total + part
            cols = pl.ds(pl.multiple_of(256 * c, 256), 256)
            dst[:, cols] = total if init else dst[:, cols] + total

    gram(acc, bo, bo, near, True)
    ct_near.wait_recv()
    odd(lambda: gram(acc2, bo, bx, near, True))

    def tile(piece, pq, whole, wq, base):
        total = None
        for n in range(NX):
            lhs, rhs = piece[base + n, pq], whole[base + n, wq]
            part = nt(lhs.reshape(-1, 256), rhs.reshape(-1, 256))
            total = part if total is None else total + part
        return total

    every = slice(0, 4)
    first_1, first_2 = NX * h_up1, NX * h_up2
    last_1, last_2 = NX - first_1, NX - first_2

    def half(p, piece, whole, base):
        nacc[p] = tile(piece, every, whole, every, base).reshape(4, 32, 512)

    def halves():
        half(0, sf, bo, first_1)
        half(1, sf, bx, first_1)

    def arrive(copies):
        for c in copies:
            c.wait_recv()

    cxf = [[copy(chunk(gfar, c), chunk(gfar, c), xs[d]) for d in range(3)] for c in range(5)]
    ct_far = [copy(bo.at[far4, q], bx.at[far4, q], twin) for q in range(4)]
    to_far = [slices(far4, q) for q in range(4)]
    for step in range(6):
        if step < 5:
            cz[step].wait_recv()
            for c in cxf[step]:
                c.start()
        if step == 3:
            to_near[1]()
        if step == 4:
            to_near[2].wait_recv()
            pl.when(h_up1 == h)(halves)
        if step > 0:
            arrive(cxf[step - 1])
        if step in (1, 2, 3, 5):
            q = min(step, 4) - 1
            to_far[q][0]()
            ct_far[q].start()
    for part in to_far[:3]:
        part[1]()
    pl.when(y == 0)(cr_f.start)
    pl.when((y < 2) & (k == 0))(cr_g.start)

    def amplitude(integral, first, second, q, rows, cols=slice(None)):
        gap = vv[q, rows, cols] - eps[first, 0:1, cols] - eps[second, 0:1, cols]
        return (-integral / gap).astype(BF)

    def parts(p, n):
        if n == 1:
            return [t.at[p, 0:2, mine, 0:256]]
        upto, new = slice(0, 128 * n + 128), slice(128 * n, 128 * n + 128)
        return [t.at[p, n, mine, upto], t.at[p, 0:n, mine, new]]

    gather = [
        [[copy(src, src, xs[d], "even" if p == 2 else "all") for d in range(3) for src in parts(p, n)] for n in (1, 2, 3)]
        for p in range(3)
    ]

    def batch(p, n, piece, whole, base, first, second):
        def block(rows, cols):
            total = tile(piece, slice(*rows), whole, slice(*cols), base)
            lanes = slice(128 * cols[0], 128 * cols[1])
            for q in range(*rows):
                start = 32 * (q - rows[0])
                whole_sum = nacc[p, q, :, lanes] + total[start:start + 32]
                t[p, q, mine, lanes] = amplitude(whole_sum, first, second, q, mine, lanes)

        if n == 1:
            block((0, 2), (0, 2))
        else:
            block((n, n + 1), (0, n + 1))
            block((0, n), (n, n + 1))
        for c in gather[p][n - 1]:
            c.start()

    def next_chip(n):
        batch(0, n, sf, bo, last_1, 0, 2)
        batch(1, n, sf, bx, last_1, 1, 2)

    def chip_after(n):
        batch(2, n, sg, bx, last_2, 1, 3)

    arrive(ce + [part[2] for part in to_far[:2]] + ct_far[:2])

    @pl.when(h_up1 != h)
    def _():
        arrive(ct_far[2:])
        halves()

    next_chip(1)
    pl.when(h_up1 == h)(lambda: arrive(ct_far[2:]))
    to_far[3][1]()

    @even
    def _():
        arrive([to_near[3]] + [part[3] for part in to_far[:2]])
        half(2, sg, bx, first_2)
        chip_after(1)

    to_far[2][2].wait_recv()
    next_chip(2)

    @even
    def _():
        to_far[2][3].wait_recv()
        chip_after(2)

    gram(acc, bo, bo, far, False)

    @pl.loop(0, 4)
    def _(q):
        rows = pl.ds(pl.multiple_of(128 * q, 128), 128)
        a0[q] = amplitude(acc[rows], 0, 0, q, slice(None))

    to_far[3][2].wait_recv()
    next_chip(3)

    @even
    def _():
        to_far[3][3].wait_recv()
        chip_after(3)

    def weights(p, read, both):
        @pl.loop(0, 4)
        def _(q):
            rows = pl.ds(pl.multiple_of(128 * q, 128), 128)
            turned = jnp.concatenate([read(n, rows).T for n in range(4)], axis=1)
            tt[p, rows] = turned
            tq, turned = read(q, slice(None)).astype(F32), turned.astype(F32)
            if both:
                wt[rows] = (2.0 * tq - turned).astype(BF)
            w[p, rows] = (2.0 * turned - tq).astype(BF)

    def energy(p, read, first, second, slot):
        @pl.loop(0, 4)
        def _(q):
            rows = pl.ds(pl.multiple_of(128 * q, 128), 128)
            tq = read(q, slice(None)).astype(F32)
            gap = vv[q] - eps[first, 0:1, :] - eps[second, 0:1, :]
            wide = 2.0 * tq - tt[p, rows].astype(F32)
            esum[slot, 0:1] += jnp.sum(gap * tq * wide, axis=0, keepdims=True)

    def times(weight, factor):
        return jnp.dot(weight, factor.reshape(512, 256), preferred_element_type=F32)

    def amplitudes(p):
        return lambda q, cols: t[p, q, :, cols]

    def own_amplitudes(q, cols):
        return a0[q, :, cols]

    weights(3, own_amplitudes, False)
    gown[...] = times(w[3], bo[g])

    @odd
    def _():
        gram(acc2, bo, bx, far, False)

        @pl.loop(0, 4)
        def _(q):
            rows = pl.ds(pl.multiple_of(128 * q, 128), 128)
            t[2, q] = amplitude(acc2[rows], 1, 0, q, slice(None))
        weights(2, amplitudes(2), True)
        gown[...] += times(wt[...], bx[g])
        goth[...] = times(w[2], bo[g])

    c_f = copy(out3.at[0], in3.at[0], up1)
    c_g = copy(out3.at[1], in3.at[1], up1, "even")
    c_x = copy(out3.at[2], in3.at[2], twin)

    @even
    def _():
        arrive(sum(gather[2], []))
        weights(2, amplitudes(2), True)
        out3[1] = times(wt[...], bx[g_up2]).astype(BF)
        c_g.start()

    arrive(sum(gather[0], []))
    weights(0, amplitudes(0), True)
    gf[...] = times(wt[...], bo[g_up1])
    arrive(sum(gather[1], []))
    weights(1, amplitudes(1), True)
    gf[...] += times(wt[...], bx[g_up1])

    @even
    def _():
        c_g.wait_recv()
        gf[...] += in3[1].astype(F32)

    out3[0] = gf[...].astype(BF)
    c_f.start()

    @even
    def _():
        cr_g.wait_recv()
        goth[...] = times(w[2], rg[...])

    cr_f.wait_recv()
    out3[2] = (goth[...] + times(w[1], rf[...])).astype(BF)
    c_x.start()
    gown[...] += times(w[0], rf[...])
    energy(3, own_amplitudes, 0, 0, 0)
    energy(0, amplitudes(0), 0, 2, 2)
    energy(1, amplitudes(1), 1, 2, 1)
    energy(2, amplitudes(2), 1, 3 * (1 - k), 3)

    lane = lax.broadcasted_iota(jnp.int32, (8, 128), 1)
    total = [-jnp.sum(esum[n, 0:1], axis=1, keepdims=True) for n in range(4)]
    first_at = 1 + 2 * k
    en[0] = jnp.where(lane == first_at, total[1], jnp.where(lane == 4 - first_at, total[3], 0.0))
    c_e = copy(en.at[0], en.at[1], twin)
    c_e.start()
    kept = jnp.where(lane == 0, total[0], jnp.where(lane == 2, total[2], 0.0))
    c_e.wait_recv()
    energy_ref[...] = (kept + en[1])[0:1, 0:4]

    c_x.wait_recv()
    gown[...] += in3[2].astype(F32)
    c_f.wait_recv()
    gown[...] += in3[0].astype(F32)

    for n in range(4):
        gamma_ref[:, 128 * n:128 * n + 128] = gown[128 * n:128 * n + 128].T

    for name, sender in who.items():
        left = [c for c, n in used if n == name and all(c is not d for d in done)]

        def finish(left=left):
            for c in left:
                c.wait_send()
        finish() if sender is None else pl.when(sender)(finish)


def per_device(factors, occ_energy, vir_energy):
    vmem = pl.BlockSpec(memory_space=pltpu.VMEM)
    hbm = pl.BlockSpec(memory_space=pl.ANY)
    gamma, energy = pl.pallas_call(
        kernel,
        out_shape=(
            jax.ShapeDtypeStruct((256, 512), F32),
            jax.ShapeDtypeStruct((1, 4), F32),
        ),
        in_specs=[hbm, pl.BlockSpec(memory_space=pltpu.SMEM), hbm],
        out_specs=(vmem, vmem),
        scratch_shapes=[
            pltpu.VMEM((8, 4, 128, 256), BF),
            pltpu.VMEM((8, 4, 128, 256), BF),
            pltpu.VMEM((8, 4, 32, 256), BF),
            pltpu.VMEM((8, 4, 32, 256), BF),
            pltpu.VMEM((8, 4, 32, 256), BF),
            pltpu.VMEM((4, 128, 256), BF),
            pltpu.VMEM((4, 128, 256), BF),
            pltpu.VMEM((3, 4, 128, 512), BF),
            pltpu.VMEM((4, 128, 512), BF),
            pltpu.VMEM((4, 128, 512), F32),
            pltpu.VMEM((512, 512), F32),
            pltpu.VMEM((512, 512), F32),
            pltpu.VMEM((3, 4, 32, 512), F32),
            pltpu.VMEM((4, 512, 512), BF),
            pltpu.VMEM((512, 512), BF),
            pltpu.VMEM((4, 512, 512), BF),
            pltpu.VMEM((512, 256), F32),
            pltpu.VMEM((512, 256), F32),
            pltpu.VMEM((512, 256), F32),
            pltpu.VMEM((3, 512, 256), BF),
            pltpu.VMEM((3, 512, 256), BF),
            pltpu.VMEM((4, 8, 512), F32),
            pltpu.VMEM((4, 8, 512), F32),
            pltpu.VMEM((2, 8, 128), F32),
            pltpu.VMEM((256, 512), BF),
            pltpu.VMEM((1, 512), F32),
            pltpu.SemaphoreType.DMA((2,)),
            pltpu.SemaphoreType.DMA((COPIES,)),
            pltpu.SemaphoreType.DMA((COPIES,)),
        ],
        compiler_params=pltpu.CompilerParams(
            collective_id=0, has_side_effects=True, vmem_limit_bytes=60 << 20
        ),
        name="pairs",
    )(factors.reshape(256, 512), occ_energy, vir_energy.reshape(1, 512))
    return energy, gamma.reshape(256, 1, 512)


def solution(mesh):
    return jax.shard_map(
        per_device,
        mesh=mesh,
        in_specs=(P("aux", "blk", None), P("blk"), P()),
        out_specs=(P("blk", None), P("aux", "blk", None)),
        check_vma=False,
    )
```

```python
import jax
import jax.numpy as jnp
from jax import lax
from jax.experimental import pallas as pl
from jax.experimental.pallas import tpu as pltpu
from jax.sharding import PartitionSpec as P

MESH = pl.DeviceIdType.MESH
BF = jnp.bfloat16
F32 = jnp.float32
NX = 4
NU = 64
HALF = NU // 2
COPIES = 144


def place(x, u, k):
    u = lax.rem(u, NU)
    return lax.rem(u, HALF) * 2 + k, lax.div(u, HALF) * NX + lax.rem(x, NX)


def nt(lhs, rhs):
    return lax.dot_general(lhs, rhs, (((1,), (1,)), ((), ())), preferred_element_type=F32)


def kernel(
    f_ref, occ_ref, vir_ref, gamma_ref, energy_ref,
    bo, bx, sf, sg, sv, rf, rg, t, a0, vv, acc, acc2, nacc, w, wt, tt,
    gown, goth, gf, out3, in3, eps, esum, en, f_own, vir, local, send, recv,
):
    b = lax.axis_index("blk")
    a = lax.axis_index("aux")
    k = lax.rem(b, 2)
    h = lax.div(a, NX)
    x = lax.rem(a, NX)
    u = HALF * h + lax.div(b, 2)
    y = lax.rem(u, 4)
    g = NX * h + x
    near = NX * h
    far = NX * (1 - h)
    gfar = far + x
    xs = [place(x + d, u, k) for d in (1, 2, 3)]
    partner = place(x, u + HALF, k)
    twin = place(x, u, 1 - k)
    down1, down2 = place(x, u + NU - 1, k), place(x, u + NU - 2, k)
    up1, up2 = place(x, u + 1, k), place(x, u + 2, k)
    h_down1 = lax.div(lax.rem(u + NU - 1, NU), HALF)
    h_down2 = lax.div(lax.rem(u + NU - 2, NU), HALF)
    h_up1, h_up2 = lax.div(lax.rem(u + 1, NU), HALF), lax.div(lax.rem(u + 2, NU), HALF)
    g_up1, g_up2 = NX * h_up1 + x, NX * h_up2 + x
    mine = pl.ds(pl.multiple_of(32 * x, 32), 32)

    barrier = pltpu.get_barrier_semaphore()
    down4, up4 = place(x, u + NU - 4, k), place(x, u + 4, k)
    others = xs + [partner, twin, down1, down2, up1, up2, down4, up4]
    for device in others:
        pl.semaphore_signal(barrier, inc=1, device_id=device, device_id_type=MESH)

    who = {
        "all": None,
        "even": k == 0,
        "skip": (k == 0) & (y > 0),
        "round": (k == 0) & (y == 0),
        "rounded": (k == 0) & (y == 2),
    }
    used, done = [], []

    def copy(src, dst, device, sender="all", lands_as=None):
        n = len(used)
        made = pltpu.make_async_remote_copy(
            src_ref=src, dst_ref=dst, send_sem=send.at[n],
            recv_sem=recv.at[n if lands_as is None else slot_of[id(lands_as)]],
            device_id=device, device_id_type=MESH,
        )
        slot_of[id(made)] = n
        used.append((made, sender))
        return made

    slot_of = {}

    def only(sender, body):
        pl.when(who[sender])(body)

    def sent(*copies):
        for c in copies:
            c.wait_send()
            done.append(c)

    def even(body):
        pl.when(k == 0)(body)

    def odd(body):
        pl.when(k == 1)(body)

    reads = [pltpu.make_async_copy(f_ref, f_own, local.at[0]), pltpu.make_async_copy(vir_ref, vir, local.at[1])]
    for c in reads:
        c.start()
    for c in reads:
        c.wait()

    bo[g] = f_own[...].T.reshape(4, 128, 256)
    eps[0] = jnp.full((8, 512), occ_ref[0], F32)
    row = jnp.broadcast_to(vir[...], (128, 512))
    for q in range(4):
        column = jnp.broadcast_to(row[:, 128 * q:128 * q + 128].T[:, 0:1], (128, 512))
        vv[q] = column + row
    esum[...] = jnp.zeros_like(esum)

    pl.semaphore_wait(barrier, len(others))

    def chunk(group, c):
        q, first, rows = ((0, 0, 128), (1, 0, 128), (2, 0, 128), (3, 0, 64), (3, 64, 64))[c]
        return bo.at[group, q, pl.ds(first, rows)]

    cz = [copy(chunk(g, c), chunk(g, c), partner) for c in range(5)]
    cx = [copy(bo.at[g], bo.at[g], xs[d]) for d in range(3)]
    ce = [copy(eps.at[0], eps.at[n], device) for n, device in ((1, twin), (2, down1), (3, down2))]
    cr_f = copy(bo.at[NX * h_down1 + x], rf, down1)
    cr_g = copy(bo.at[NX * h_down2 + x], rg, down2, "even")
    for c in cz[:2] + cx + ce:
        c.start()
    pl.when(y > 0)(cr_f.start)
    pl.when((y > 1) & (k == 0))(cr_g.start)
    near4, far4 = pl.ds(near, NX), pl.ds(far, NX)
    ct_near = copy(bo.at[near4], bx.at[near4], twin)

    def slices(groups, q):
        own = bo.at[groups, q, mine]
        there = sv.at[groups, q]
        f = copy(own, sf.at[groups, q], down1)
        g = copy(own, sg.at[groups, q], down2, "skip")
        g_out = copy(own, there, up2, "round")
        g_in = copy(there, sg.at[groups, q], down4, "rounded", g)

        def first():
            f.start()
            only("skip", g.start)
            only("round", g_out.start)

        def second():
            @pl.when(who["rounded"])
            def _():
                g_out.wait_recv()
                g_in.start()

        return first, second, f, g

    to_near = slices(near4, slice(None))
    sent(cz[0])
    cz[2].start()
    for c in cx:
        c.wait_recv()
    ct_near.start()
    to_near[0]()
    sent(cz[1])
    cz[3].start()
    cz[4].start()

    def gram(dst, lhs, rhs, base, init):
        @pl.loop(0, 2)
        def _(c):
            total = None
            for n in range(NX):
                part = nt(lhs[base + n].reshape(512, 256), rhs[base + n, pl.ds(2 * c, 2)].reshape(256, 256))
                total = part if total is None else total + part
            cols = pl.ds(pl.multiple_of(256 * c, 256), 256)
            dst[:, cols] = total if init else dst[:, cols] + total

    gram(acc, bo, bo, near, True)
    ct_near.wait_recv()
    odd(lambda: gram(acc2, bo, bx, near, True))

    def tile(piece, pq, whole, wq, base):
        total = None
        for n in range(NX):
            lhs, rhs = piece[base + n, pq], whole[base + n, wq]
            part = nt(lhs.reshape(-1, 256), rhs.reshape(-1, 256))
            total = part if total is None else total + part
        return total

    every = slice(0, 4)
    first_1, first_2 = NX * h_up1, NX * h_up2
    last_1, last_2 = NX - first_1, NX - first_2

    def half(p, piece, whole, base):
        nacc[p] = tile(piece, every, whole, every, base).reshape(4, 32, 512)

    def halves():
        half(0, sf, bo, first_1)
        half(1, sf, bx, first_1)

    def arrive(copies):
        for c in copies:
            c.wait_recv()

    cxf = [[copy(chunk(gfar, c), chunk(gfar, c), xs[d]) for d in range(3)] for c in range(5)]
    ct_far = [copy(bo.at[far4, q], bx.at[far4, q], twin) for q in range(4)]
    to_far = [slices(far4, q) for q in range(4)]
    for step in range(6):
        if step < 5:
            cz[step].wait_recv()
            for c in cxf[step]:
                c.start()
        if step == 3:
            to_near[1]()
        if step == 4:
            to_near[2].wait_recv()
            pl.when(h_up1 == h)(halves)
        if step > 0:
            arrive(cxf[step - 1])
        if step in (1, 2, 3, 5):
            q = min(step, 4) - 1
            to_far[q][0]()
            ct_far[q].start()
    for part in to_far[:3]:
        part[1]()
    pl.when(y == 0)(cr_f.start)
    pl.when((y < 2) & (k == 0))(cr_g.start)

    def amplitude(integral, first, second, q, rows, cols=slice(None)):
        gap = vv[q, rows, cols] - eps[first, 0:1, cols] - eps[second, 0:1, cols]
        return (-integral / gap).astype(BF)

    def parts(p, n):
        if n == 1:
            return [t.at[p, 0:2, mine, 0:256]]
        upto, new = slice(0, 128 * n + 128), slice(128 * n, 128 * n + 128)
        return [t.at[p, n, mine, upto], t.at[p, 0:n, mine, new]]

    gather = [
        [[copy(src, src, xs[d], "even" if p == 2 else "all") for d in range(3) for src in parts(p, n)] for n in (1, 2, 3)]
        for p in range(3)
    ]

    def batch(p, n, piece, whole, base, first, second):
        def block(rows, cols):
            total = tile(piece, slice(*rows), whole, slice(*cols), base)
            lanes = slice(128 * cols[0], 128 * cols[1])
            for q in range(*rows):
                start = 32 * (q - rows[0])
                whole_sum = nacc[p, q, :, lanes] + total[start:start + 32]
                t[p, q, mine, lanes] = amplitude(whole_sum, first, second, q, mine, lanes)

        if n == 1:
            block((0, 2), (0, 2))
        else:
            block((n, n + 1), (0, n + 1))
            block((0, n), (n, n + 1))
        for c in gather[p][n - 1]:
            c.start()

    def next_chip(n):
        batch(0, n, sf, bo, last_1, 0, 2)
        batch(1, n, sf, bx, last_1, 1, 2)

    def chip_after(n):
        batch(2, n, sg, bx, last_2, 1, 3)

    arrive(ce + [part[2] for part in to_far[:2]] + ct_far[:2])

    @pl.when(h_up1 != h)
    def _():
        arrive(ct_far[2:])
        halves()

    next_chip(1)
    pl.when(h_up1 == h)(lambda: arrive(ct_far[2:]))
    to_far[3][1]()

    @even
    def _():
        arrive([to_near[3]] + [part[3] for part in to_far[:2]])
        half(2, sg, bx, first_2)
        chip_after(1)

    to_far[2][2].wait_recv()
    next_chip(2)

    @even
    def _():
        to_far[2][3].wait_recv()
        chip_after(2)

    gram(acc, bo, bo, far, False)

    @pl.loop(0, 4)
    def _(q):
        rows = pl.ds(pl.multiple_of(128 * q, 128), 128)
        a0[q] = amplitude(acc[rows], 0, 0, q, slice(None))

    def weights(p, read, both):
        @pl.loop(0, 4)
        def _(q):
            rows = pl.ds(pl.multiple_of(128 * q, 128), 128)
            turned = jnp.concatenate([read(n, rows).T for n in range(4)], axis=1)
            tt[p, rows] = turned
            tq, turned = read(q, slice(None)).astype(F32), turned.astype(F32)
            if both:
                wt[rows] = (2.0 * tq - turned).astype(BF)
            w[p, rows] = (2.0 * turned - tq).astype(BF)

    def energy(p, read, first, second, slot):
        @pl.loop(0, 4)
        def _(q):
            rows = pl.ds(pl.multiple_of(128 * q, 128), 128)
            tq = read(q, slice(None)).astype(F32)
            gap = vv[q] - eps[first, 0:1, :] - eps[second, 0:1, :]
            wide = 2.0 * tq - tt[p, rows].astype(F32)
            esum[slot, 0:1] += jnp.sum(gap * tq * wide, axis=0, keepdims=True)

    def times(weight, factor):
        return jnp.dot(weight, factor.reshape(512, 256), preferred_element_type=F32)

    def amplitudes(p):
        return lambda q, cols: t[p, q, :, cols]

    def own_amplitudes(q, cols):
        return a0[q, :, cols]

    def own_pair():
        weights(3, own_amplitudes, False)
        gown[...] = times(w[3], bo[g])

    def chip_pair():
        gram(acc2, bo, bx, far, False)

        @pl.loop(0, 4)
        def _(q):
            rows = pl.ds(pl.multiple_of(128 * q, 128), 128)
            t[2, q] = amplitude(acc2[rows], 1, 0, q, slice(None))
        weights(2, amplitudes(2), True)
        gown[...] += times(wt[...], bx[g])
        goth[...] = times(w[2], bo[g])

    @odd
    def _():
        own_pair()
        chip_pair()

    @even
    def _():
        to_far[3][3].wait_recv()
        chip_after(3)

    to_far[3][2].wait_recv()
    next_chip(3)
    even(own_pair)

    c_f = copy(out3.at[0], in3.at[0], up1)
    c_g = copy(out3.at[1], in3.at[1], up2, "even")
    c_x = copy(out3.at[2], in3.at[2], twin)

    @even
    def _():
        arrive(sum(gather[2], []))
        weights(2, amplitudes(2), True)
        out3[1] = times(wt[...], bx[g_up2]).astype(BF)
        c_g.start()

    arrive(sum(gather[0], []))
    weights(0, amplitudes(0), True)
    gf[...] = times(wt[...], bo[g_up1])
    arrive(sum(gather[1], []))
    weights(1, amplitudes(1), True)
    out3[0] = (gf[...] + times(wt[...], bx[g_up1])).astype(BF)
    c_f.start()

    @even
    def _():
        cr_g.wait_recv()
        goth[...] = times(w[2], rg[...])

    cr_f.wait_recv()
    out3[2] = (goth[...] + times(w[1], rf[...])).astype(BF)
    c_x.start()
    gown[...] += times(w[0], rf[...])
    energy(3, own_amplitudes, 0, 0, 0)
    energy(0, amplitudes(0), 0, 2, 2)
    energy(1, amplitudes(1), 1, 2, 1)
    energy(2, amplitudes(2), 1, 3 * (1 - k), 3)

    lane = lax.broadcasted_iota(jnp.int32, (8, 128), 1)
    total = [-jnp.sum(esum[n, 0:1], axis=1, keepdims=True) for n in range(4)]
    first_at = 1 + 2 * k
    en[0] = jnp.where(lane == first_at, total[1], jnp.where(lane == 4 - first_at, total[3], 0.0))
    c_e = copy(en.at[0], en.at[1], twin)
    c_e.start()
    kept = jnp.where(lane == 0, total[0], jnp.where(lane == 2, total[2], 0.0))
    c_e.wait_recv()
    energy_ref[...] = (kept + en[1])[0:1, 0:4]

    c_x.wait_recv()
    gown[...] += in3[2].astype(F32)
    c_f.wait_recv()
    gown[...] += in3[0].astype(F32)

    @even
    def _():
        c_g.wait_recv()
        gown[...] += in3[1].astype(F32)

    for n in range(4):
        gamma_ref[:, 128 * n:128 * n + 128] = gown[128 * n:128 * n + 128].T

    for name, sender in who.items():
        left = [c for c, n in used if n == name and all(c is not d for d in done)]

        def finish(left=left):
            for c in left:
                c.wait_send()
        finish() if sender is None else pl.when(sender)(finish)


def per_device(factors, occ_energy, vir_energy):
    vmem = pl.BlockSpec(memory_space=pltpu.VMEM)
    hbm = pl.BlockSpec(memory_space=pl.ANY)
    gamma, energy = pl.pallas_call(
        kernel,
        out_shape=(
            jax.ShapeDtypeStruct((256, 512), F32),
            jax.ShapeDtypeStruct((1, 4), F32),
        ),
        in_specs=[hbm, pl.BlockSpec(memory_space=pltpu.SMEM), hbm],
        out_specs=(vmem, vmem),
        scratch_shapes=[
            pltpu.VMEM((8, 4, 128, 256), BF),
            pltpu.VMEM((8, 4, 128, 256), BF),
            pltpu.VMEM((8, 4, 32, 256), BF),
            pltpu.VMEM((8, 4, 32, 256), BF),
            pltpu.VMEM((8, 4, 32, 256), BF),
            pltpu.VMEM((4, 128, 256), BF),
            pltpu.VMEM((4, 128, 256), BF),
            pltpu.VMEM((3, 4, 128, 512), BF),
            pltpu.VMEM((4, 128, 512), BF),
            pltpu.VMEM((4, 128, 512), F32),
            pltpu.VMEM((512, 512), F32),
            pltpu.VMEM((512, 512), F32),
            pltpu.VMEM((3, 4, 32, 512), F32),
            pltpu.VMEM((4, 512, 512), BF),
            pltpu.VMEM((512, 512), BF),
            pltpu.VMEM((4, 512, 512), BF),
            pltpu.VMEM((512, 256), F32),
            pltpu.VMEM((512, 256), F32),
            pltpu.VMEM((512, 256), F32),
            pltpu.VMEM((3, 512, 256), BF),
            pltpu.VMEM((3, 512, 256), BF),
            pltpu.VMEM((4, 8, 512), F32),
            pltpu.VMEM((4, 8, 512), F32),
            pltpu.VMEM((2, 8, 128), F32),
            pltpu.VMEM((256, 512), BF),
            pltpu.VMEM((1, 512), F32),
            pltpu.SemaphoreType.DMA((2,)),
            pltpu.SemaphoreType.DMA((COPIES,)),
            pltpu.SemaphoreType.DMA((COPIES,)),
        ],
        compiler_params=pltpu.CompilerParams(
            collective_id=0, has_side_effects=True, vmem_limit_bytes=60 << 20
        ),
        name="pairs",
    )(factors.reshape(256, 512), occ_energy, vir_energy.reshape(1, 512))
    return energy, gamma.reshape(256, 1, 512)


def solution(mesh):
    return jax.shard_map(
        per_device,
        mesh=mesh,
        in_specs=(P("aux", "blk", None), P("blk"), P()),
        out_specs=(P("blk", None), P("aux", "blk", None)),
        check_vma=False,
    )
```

```python
import jax
import jax.numpy as jnp
from jax import lax
from jax.experimental import pallas as pl
from jax.experimental.pallas import tpu as pltpu
from jax.sharding import PartitionSpec as P

MESH = pl.DeviceIdType.MESH
BF = jnp.bfloat16
F32 = jnp.float32
NX = 4
NU = 64
HALF = NU // 2
COPIES = 144


def place(x, u, k):
    u = lax.rem(u, NU)
    return lax.rem(u, HALF) * 2 + k, lax.div(u, HALF) * NX + lax.rem(x, NX)


def nt(lhs, rhs):
    return lax.dot_general(lhs, rhs, (((1,), (1,)), ((), ())), preferred_element_type=F32)


def kernel(
    f_ref, occ_ref, vir_ref, gamma_ref, energy_ref,
    bo, bx, sf, sg, sv, rf, rg, t, a0, vv, acc, acc2, nacc, w, wt, tt,
    gown, goth, gf, out3, in3, between, eps, esum, en, f_own, vir, local, send, recv,
):
    b = lax.axis_index("blk")
    a = lax.axis_index("aux")
    k = lax.rem(b, 2)
    h = lax.div(a, NX)
    x = lax.rem(a, NX)
    u = HALF * h + lax.div(b, 2)
    y = lax.rem(u, 4)
    g = NX * h + x
    near = NX * h
    far = NX * (1 - h)
    gfar = far + x
    xs = [place(x + d, u, k) for d in (1, 2, 3)]
    partner = place(x, u + HALF, k)
    twin = place(x, u, 1 - k)
    down1, down2 = place(x, u + NU - 1, k), place(x, u + NU - 2, k)
    up1, up2 = place(x, u + 1, k), place(x, u + 2, k)
    h_down1 = lax.div(lax.rem(u + NU - 1, NU), HALF)
    h_down2 = lax.div(lax.rem(u + NU - 2, NU), HALF)
    h_up1, h_up2 = lax.div(lax.rem(u + 1, NU), HALF), lax.div(lax.rem(u + 2, NU), HALF)
    g_up1, g_up2 = NX * h_up1 + x, NX * h_up2 + x
    mine = pl.ds(pl.multiple_of(32 * x, 32), 32)

    barrier = pltpu.get_barrier_semaphore()
    down4, up4 = place(x, u + NU - 4, k), place(x, u + 4, k)
    down3, up3 = place(x, u + NU - 3, k), place(x, u + 3, k)
    way_back = place(x, u + NU - 1 + 4 * lax.div(3 - y, 3), k)
    passed_to = place(x, u + NU + 3 - 4 * lax.div(y, 3), k)
    others = xs + [partner, twin, down1, down2, up1, up2, down4, up4, down3, up3]
    for device in others:
        pl.semaphore_signal(barrier, inc=1, device_id=device, device_id_type=MESH)

    who = {
        "all": None,
        "even": k == 0,
        "skip": (k == 0) & (y > 0),
        "round": (k == 0) & (y == 0),
        "rounded": (k == 0) & (y == 2),
    }
    used, done = [], []

    def copy(src, dst, device, sender="all", lands_as=None):
        n = len(used)
        made = pltpu.make_async_remote_copy(
            src_ref=src, dst_ref=dst, send_sem=send.at[n],
            recv_sem=recv.at[n if lands_as is None else slot_of[id(lands_as)]],
            device_id=device, device_id_type=MESH,
        )
        slot_of[id(made)] = n
        used.append((made, sender))
        return made

    slot_of = {}

    def only(sender, body):
        pl.when(who[sender])(body)

    def sent(*copies):
        for c in copies:
            c.wait_send()
            done.append(c)

    def even(body):
        pl.when(k == 0)(body)

    def odd(body):
        pl.when(k == 1)(body)

    reads = [pltpu.make_async_copy(f_ref, f_own, local.at[0]), pltpu.make_async_copy(vir_ref, vir, local.at[1])]
    for c in reads:
        c.start()
    for c in reads:
        c.wait()

    bo[g] = f_own[...].T.reshape(4, 128, 256)
    eps[0] = jnp.full((8, 512), occ_ref[0], F32)
    row = jnp.broadcast_to(vir[...], (128, 512))
    for q in range(4):
        column = jnp.broadcast_to(row[:, 128 * q:128 * q + 128].T[:, 0:1], (128, 512))
        vv[q] = column + row
    esum[...] = jnp.zeros_like(esum)

    pl.semaphore_wait(barrier, len(others))

    def chunk(group, c):
        q, first, rows = ((0, 0, 128), (1, 0, 128), (2, 0, 128), (3, 0, 64), (3, 64, 64))[c]
        return bo.at[group, q, pl.ds(first, rows)]

    cz = [copy(chunk(g, c), chunk(g, c), partner) for c in range(5)]
    cx = [copy(bo.at[g], bo.at[g], xs[d]) for d in range(3)]
    ce = [copy(eps.at[0], eps.at[n], device) for n, device in ((1, twin), (2, down1), (3, down2))]
    cr_f = copy(bo.at[NX * h_down1 + x], rf, down1)
    cr_g = copy(bo.at[NX * h_down2 + x], rg, down2, "even")
    for c in cz[:2] + cx + ce:
        c.start()
    pl.when(y > 0)(cr_f.start)
    pl.when((y > 1) & (k == 0))(cr_g.start)
    near4, far4 = pl.ds(near, NX), pl.ds(far, NX)
    ct_near = copy(bo.at[near4], bx.at[near4], twin)

    def slices(groups, q):
        own = bo.at[groups, q, mine]
        there = sv.at[groups, q]
        f = copy(own, sf.at[groups, q], down1)
        g = copy(own, sg.at[groups, q], down2, "skip")
        g_out = copy(own, there, up2, "round")
        g_in = copy(there, sg.at[groups, q], down4, "rounded", g)

        def first():
            f.start()
            only("skip", g.start)
            only("round", g_out.start)

        def second():
            @pl.when(who["rounded"])
            def _():
                g_out.wait_recv()
                g_in.start()

        return first, second, f, g

    to_near = slices(near4, slice(None))
    sent(cz[0])
    cz[2].start()
    for c in cx:
        c.wait_recv()
    ct_near.start()
    to_near[0]()
    sent(cz[1])
    cz[3].start()
    cz[4].start()

    def gram(dst, lhs, rhs, base, init):
        @pl.loop(0, 2)
        def _(c):
            total = None
            for n in range(NX):
                part = nt(lhs[base + n].reshape(512, 256), rhs[base + n, pl.ds(2 * c, 2)].reshape(256, 256))
                total = part if total is None else total + part
            cols = pl.ds(pl.multiple_of(256 * c, 256), 256)
            dst[:, cols] = total if init else dst[:, cols] + total

    gram(acc, bo, bo, near, True)
    ct_near.wait_recv()
    odd(lambda: gram(acc2, bo, bx, near, True))

    def tile(piece, pq, whole, wq, base):
        total = None
        for n in range(NX):
            lhs, rhs = piece[base + n, pq], whole[base + n, wq]
            part = nt(lhs.reshape(-1, 256), rhs.reshape(-1, 256))
            total = part if total is None else total + part
        return total

    every = slice(0, 4)
    first_1, first_2 = NX * h_up1, NX * h_up2
    last_1, last_2 = NX - first_1, NX - first_2

    def half(p, piece, whole, base):
        nacc[p] = tile(piece, every, whole, every, base).reshape(4, 32, 512)

    def halves():
        half(0, sf, bo, first_1)
        half(1, sf, bx, first_1)

    def arrive(copies):
        for c in copies:
            c.wait_recv()

    cxf = [[copy(chunk(gfar, c), chunk(gfar, c), xs[d]) for d in range(3)] for c in range(5)]
    ct_far = [copy(bo.at[far4, q], bx.at[far4, q], twin) for q in range(4)]
    to_far = [slices(far4, q) for q in range(4)]
    for step in range(6):
        if step < 5:
            cz[step].wait_recv()
            for c in cxf[step]:
                c.start()
        if step == 3:
            to_near[1]()
        if step == 4:
            to_near[2].wait_recv()
            pl.when(h_up1 == h)(halves)
        if step > 0:
            arrive(cxf[step - 1])
        if step in (1, 2, 3, 5):
            q = min(step, 4) - 1
            to_far[q][0]()
            ct_far[q].start()
    for part in to_far[:3]:
        part[1]()
    pl.when(y == 0)(cr_f.start)
    pl.when((y < 2) & (k == 0))(cr_g.start)

    def amplitude(integral, first, second, q, rows, cols=slice(None)):
        gap = vv[q, rows, cols] - eps[first, 0:1, cols] - eps[second, 0:1, cols]
        return (-integral / gap).astype(BF)

    def parts(p, n):
        if n == 1:
            return [t.at[p, 0:2, mine, 0:256]]
        upto, new = slice(0, 128 * n + 128), slice(128 * n, 128 * n + 128)
        return [t.at[p, n, mine, upto], t.at[p, 0:n, mine, new]]

    gather = [
        [[copy(src, src, xs[d], "even" if p == 2 else "all") for d in range(3) for src in parts(p, n)] for n in (1, 2, 3)]
        for p in range(3)
    ]

    def batch(p, n, piece, whole, base, first, second):
        def block(rows, cols):
            total = tile(piece, slice(*rows), whole, slice(*cols), base)
            lanes = slice(128 * cols[0], 128 * cols[1])
            for q in range(*rows):
                start = 32 * (q - rows[0])
                whole_sum = nacc[p, q, :, lanes] + total[start:start + 32]
                t[p, q, mine, lanes] = amplitude(whole_sum, first, second, q, mine, lanes)

        if n == 1:
            block((0, 2), (0, 2))
        else:
            block((n, n + 1), (0, n + 1))
            block((0, n), (n, n + 1))
        for c in gather[p][n - 1]:
            c.start()

    def next_chip(n):
        batch(0, n, sf, bo, last_1, 0, 2)
        batch(1, n, sf, bx, last_1, 1, 2)

    def chip_after(n):
        batch(2, n, sg, bx, last_2, 1, 3)

    arrive(ce + [part[2] for part in to_far[:2]] + ct_far[:2])

    @pl.when(h_up1 != h)
    def _():
        arrive(ct_far[2:])
        halves()

    next_chip(1)
    pl.when(h_up1 == h)(lambda: arrive(ct_far[2:]))
    to_far[3][1]()

    @even
    def _():
        arrive([to_near[3]] + [part[3] for part in to_far[:2]])
        half(2, sg, bx, first_2)
        chip_after(1)

    to_far[2][2].wait_recv()
    next_chip(2)

    @even
    def _():
        to_far[2][3].wait_recv()
        chip_after(2)

    gram(acc, bo, bo, far, False)

    @pl.loop(0, 4)
    def _(q):
        rows = pl.ds(pl.multiple_of(128 * q, 128), 128)
        a0[q] = amplitude(acc[rows], 0, 0, q, slice(None))

    def weights(p, read, both):
        @pl.loop(0, 4)
        def _(q):
            rows = pl.ds(pl.multiple_of(128 * q, 128), 128)
            turned = jnp.concatenate([read(n, rows).T for n in range(4)], axis=1)
            tt[p, rows] = turned
            tq, turned = read(q, slice(None)).astype(F32), turned.astype(F32)
            if both:
                wt[rows] = (2.0 * tq - turned).astype(BF)
            w[p, rows] = (2.0 * turned - tq).astype(BF)

    def energy(p, read, first, second, slot):
        @pl.loop(0, 4)
        def _(q):
            rows = pl.ds(pl.multiple_of(128 * q, 128), 128)
            tq = read(q, slice(None)).astype(F32)
            gap = vv[q] - eps[first, 0:1, :] - eps[second, 0:1, :]
            wide = 2.0 * tq - tt[p, rows].astype(F32)
            esum[slot, 0:1] += jnp.sum(gap * tq * wide, axis=0, keepdims=True)

    def times(weight, factor):
        return jnp.dot(weight, factor.reshape(512, 256), preferred_element_type=F32)

    def amplitudes(p):
        return lambda q, cols: t[p, q, :, cols]

    def own_amplitudes(q, cols):
        return a0[q, :, cols]

    def own_pair():
        weights(3, own_amplitudes, False)
        gown[...] = times(w[3], bo[g])

    def chip_pair():
        gram(acc2, bo, bx, far, False)

        @pl.loop(0, 4)
        def _(q):
            rows = pl.ds(pl.multiple_of(128 * q, 128), 128)
            t[2, q] = amplitude(acc2[rows], 1, 0, q, slice(None))
        weights(2, amplitudes(2), True)
        gown[...] += times(wt[...], bx[g])
        goth[...] = times(w[2], bo[g])

    @odd
    def _():
        own_pair()
        chip_pair()

    @even
    def _():
        to_far[3][3].wait_recv()
        chip_after(3)

    to_far[3][2].wait_recv()
    next_chip(3)
    even(own_pair)

    c_f = copy(out3.at[0], in3.at[0], up1)
    c_g = copy(out3.at[1], between, way_back, "even")
    c_g_on = copy(between, in3.at[1], passed_to, "even")
    c_x = copy(out3.at[2], in3.at[2], twin)

    @even
    def _():
        arrive(sum(gather[2], []))
        weights(2, amplitudes(2), True)
        out3[1] = times(wt[...], bx[g_up2]).astype(BF)
        c_g.start()

    arrive(sum(gather[0], []))
    weights(0, amplitudes(0), True)
    gf[...] = times(wt[...], bo[g_up1])
    arrive(sum(gather[1], []))
    weights(1, amplitudes(1), True)
    out3[0] = (gf[...] + times(wt[...], bx[g_up1])).astype(BF)
    c_f.start()

    @even
    def _():
        cr_g.wait_recv()
        goth[...] = times(w[2], rg[...])

    cr_f.wait_recv()
    out3[2] = (goth[...] + times(w[1], rf[...])).astype(BF)
    c_x.start()

    @even
    def _():
        c_g.wait_recv()
        c_g_on.start()

    gown[...] += times(w[0], rf[...])
    energy(3, own_amplitudes, 0, 0, 0)
    energy(0, amplitudes(0), 0, 2, 2)
    energy(1, amplitudes(1), 1, 2, 1)
    energy(2, amplitudes(2), 1, 3 * (1 - k), 3)

    lane = lax.broadcasted_iota(jnp.int32, (8, 128), 1)
    total = [-jnp.sum(esum[n, 0:1], axis=1, keepdims=True) for n in range(4)]
    first_at = 1 + 2 * k
    en[0] = jnp.where(lane == first_at, total[1], jnp.where(lane == 4 - first_at, total[3], 0.0))
    c_e = copy(en.at[0], en.at[1], twin)
    c_e.start()
    kept = jnp.where(lane == 0, total[0], jnp.where(lane == 2, total[2], 0.0))
    c_e.wait_recv()
    energy_ref[...] = (kept + en[1])[0:1, 0:4]

    c_x.wait_recv()
    gown[...] += in3[2].astype(F32)
    c_f.wait_recv()
    gown[...] += in3[0].astype(F32)

    @even
    def _():
        c_g_on.wait_recv()
        gown[...] += in3[1].astype(F32)

    for n in range(4):
        gamma_ref[:, 128 * n:128 * n + 128] = gown[128 * n:128 * n + 128].T

    for name, sender in who.items():
        left = [c for c, n in used if n == name and all(c is not d for d in done)]

        def finish(left=left):
            for c in left:
                c.wait_send()
        finish() if sender is None else pl.when(sender)(finish)


def per_device(factors, occ_energy, vir_energy):
    vmem = pl.BlockSpec(memory_space=pltpu.VMEM)
    hbm = pl.BlockSpec(memory_space=pl.ANY)
    gamma, energy = pl.pallas_call(
        kernel,
        out_shape=(
            jax.ShapeDtypeStruct((256, 512), F32),
            jax.ShapeDtypeStruct((1, 4), F32),
        ),
        in_specs=[hbm, pl.BlockSpec(memory_space=pltpu.SMEM), hbm],
        out_specs=(vmem, vmem),
        scratch_shapes=[
            pltpu.VMEM((8, 4, 128, 256), BF),
            pltpu.VMEM((8, 4, 128, 256), BF),
            pltpu.VMEM((8, 4, 32, 256), BF),
            pltpu.VMEM((8, 4, 32, 256), BF),
            pltpu.VMEM((8, 4, 32, 256), BF),
            pltpu.VMEM((4, 128, 256), BF),
            pltpu.VMEM((4, 128, 256), BF),
            pltpu.VMEM((3, 4, 128, 512), BF),
            pltpu.VMEM((4, 128, 512), BF),
            pltpu.VMEM((4, 128, 512), F32),
            pltpu.VMEM((512, 512), F32),
            pltpu.VMEM((512, 512), F32),
            pltpu.VMEM((3, 4, 32, 512), F32),
            pltpu.VMEM((4, 512, 512), BF),
            pltpu.VMEM((512, 512), BF),
            pltpu.VMEM((4, 512, 512), BF),
            pltpu.VMEM((512, 256), F32),
            pltpu.VMEM((512, 256), F32),
            pltpu.VMEM((512, 256), F32),
            pltpu.VMEM((3, 512, 256), BF),
            pltpu.VMEM((3, 512, 256), BF),
            pltpu.VMEM((512, 256), BF),
            pltpu.VMEM((4, 8, 512), F32),
            pltpu.VMEM((4, 8, 512), F32),
            pltpu.VMEM((2, 8, 128), F32),
            pltpu.VMEM((256, 512), BF),
            pltpu.VMEM((1, 512), F32),
            pltpu.SemaphoreType.DMA((2,)),
            pltpu.SemaphoreType.DMA((COPIES,)),
            pltpu.SemaphoreType.DMA((COPIES,)),
        ],
        compiler_params=pltpu.CompilerParams(
            collective_id=0, has_side_effects=True, vmem_limit_bytes=60 << 20
        ),
        name="pairs",
    )(factors.reshape(256, 512), occ_energy, vir_energy.reshape(1, 512))
    return energy, gamma.reshape(256, 1, 512)


def solution(mesh):
    return jax.shard_map(
        per_device,
        mesh=mesh,
        in_specs=(P("aux", "blk", None), P("blk"), P()),
        out_specs=(P("blk", None), P("aux", "blk", None)),
        check_vma=False,
    )
```

```python
import jax
import jax.numpy as jnp
from jax import lax
from jax.experimental import pallas as pl
from jax.experimental.pallas import tpu as pltpu
from jax.sharding import PartitionSpec as P

MESH = pl.DeviceIdType.MESH
BF = jnp.bfloat16
F32 = jnp.float32
NX = 4
NU = 64
HALF = NU // 2
COPIES = 144


def place(x, u, k):
    u = lax.rem(u, NU)
    return lax.rem(u, HALF) * 2 + k, lax.div(u, HALF) * NX + lax.rem(x, NX)


def nt(lhs, rhs):
    return lax.dot_general(lhs, rhs, (((1,), (1,)), ((), ())), preferred_element_type=F32)


def kernel(
    f_ref, occ_ref, vir_ref, gamma_ref, energy_ref,
    bo, bx, sf, sg, sv, rf, rg, t, a0, vv, acc, acc2, nacc, w, wt, tt,
    gown, goth, gf, out3, in3, eps, esum, en, f_own, vir, local, send, recv,
):
    b = lax.axis_index("blk")
    a = lax.axis_index("aux")
    k = lax.rem(b, 2)
    h = lax.div(a, NX)
    x = lax.rem(a, NX)
    u = HALF * h + lax.div(b, 2)
    y = lax.rem(u, 4)
    g = NX * h + x
    near = NX * h
    far = NX * (1 - h)
    gfar = far + x
    xs = [place(x + d, u, k) for d in (1, 2, 3)]
    partner = place(x, u + HALF, k)
    twin = place(x, u, 1 - k)
    down1, down2 = place(x, u + NU - 1, k), place(x, u + NU - 2, k)
    up1, up2 = place(x, u + 1, k), place(x, u + 2, k)
    h_down1 = lax.div(lax.rem(u + NU - 1, NU), HALF)
    h_down2 = lax.div(lax.rem(u + NU - 2, NU), HALF)
    h_up1, h_up2 = lax.div(lax.rem(u + 1, NU), HALF), lax.div(lax.rem(u + 2, NU), HALF)
    g_up1, g_up2 = NX * h_up1 + x, NX * h_up2 + x
    mine = pl.ds(pl.multiple_of(32 * x, 32), 32)

    barrier = pltpu.get_barrier_semaphore()
    down4, up4 = place(x, u + NU - 4, k), place(x, u + 4, k)
    others = xs + [partner, twin, down1, down2, up1, up2, down4, up4]
    for device in others:
        pl.semaphore_signal(barrier, inc=1, device_id=device, device_id_type=MESH)

    who = {
        "all": None,
        "even": k == 0,
        "skip": (k == 0) & (y > 0),
        "round": (k == 0) & (y == 0),
        "rounded": (k == 0) & (y == 2),
    }
    used, done = [], []

    def copy(src, dst, device, sender="all", lands_as=None):
        n = len(used)
        made = pltpu.make_async_remote_copy(
            src_ref=src, dst_ref=dst, send_sem=send.at[n],
            recv_sem=recv.at[n if lands_as is None else slot_of[id(lands_as)]],
            device_id=device, device_id_type=MESH,
        )
        slot_of[id(made)] = n
        used.append((made, sender))
        return made

    slot_of = {}

    def only(sender, body):
        pl.when(who[sender])(body)

    def sent(*copies):
        for c in copies:
            c.wait_send()
            done.append(c)

    def even(body):
        pl.when(k == 0)(body)

    def odd(body):
        pl.when(k == 1)(body)

    reads = [pltpu.make_async_copy(f_ref, f_own, local.at[0]), pltpu.make_async_copy(vir_ref, vir, local.at[1])]
    for c in reads:
        c.start()
    for c in reads:
        c.wait()

    bo[g] = f_own[...].T.reshape(4, 128, 256)
    eps[0] = jnp.full((8, 512), occ_ref[0], F32)
    row = jnp.broadcast_to(vir[...], (128, 512))
    for q in range(4):
        column = jnp.broadcast_to(row[:, 128 * q:128 * q + 128].T[:, 0:1], (128, 512))
        vv[q] = column + row
    esum[...] = jnp.zeros_like(esum)

    pl.semaphore_wait(barrier, len(others))

    def chunk(group, c):
        q, first, rows = ((0, 0, 128), (1, 0, 128), (2, 0, 128), (3, 0, 64), (3, 64, 64))[c]
        return bo.at[group, q, pl.ds(first, rows)]

    cz = [copy(chunk(g, c), chunk(g, c), partner) for c in range(5)]
    cx = [copy(bo.at[g], bo.at[g], xs[d]) for d in range(3)]
    ce = [copy(eps.at[0], eps.at[n], device) for n, device in ((1, twin), (2, down1), (3, down2))]
    cr_f = copy(bo.at[NX * h_down1 + x], rf, down1)
    cr_g = copy(bo.at[NX * h_down2 + x], rg, down2, "even")
    for c in cz[:2] + cx + ce:
        c.start()
    pl.when(y > 0)(cr_f.start)
    pl.when((y > 1) & (k == 0))(cr_g.start)
    near4, far4 = pl.ds(near, NX), pl.ds(far, NX)
    ct_near = copy(bo.at[near4], bx.at[near4], twin)

    def slices(groups, q):
        own = bo.at[groups, q, mine]
        there = sv.at[groups, q]
        f = copy(own, sf.at[groups, q], down1)
        g = copy(own, sg.at[groups, q], down2, "skip")
        g_out = copy(own, there, up2, "round")
        g_in = copy(there, sg.at[groups, q], down4, "rounded", g)

        def first():
            f.start()
            only("skip", g.start)
            only("round", g_out.start)

        def second():
            @pl.when(who["rounded"])
            def _():
                g_out.wait_recv()
                g_in.start()

        return first, second, f, g

    to_near = slices(near4, slice(None))
    sent(cz[0])
    cz[2].start()
    for c in cx:
        c.wait_recv()
    ct_near.start()
    to_near[0]()
    sent(cz[1])
    cz[3].start()
    cz[4].start()

    def gram(dst, lhs, rhs, base, init):
        @pl.loop(0, 2)
        def _(c):
            total = None
            for n in range(NX):
                part = nt(lhs[base + n].reshape(512, 256), rhs[base + n, pl.ds(2 * c, 2)].reshape(256, 256))
                total = part if total is None else total + part
            cols = pl.ds(pl.multiple_of(256 * c, 256), 256)
            dst[:, cols] = total if init else dst[:, cols] + total

    gram(acc, bo, bo, near, True)
    ct_near.wait_recv()
    odd(lambda: gram(acc2, bo, bx, near, True))

    def tile(piece, pq, whole, wq, base):
        total = None
        for n in range(NX):
            lhs, rhs = piece[base + n, pq], whole[base + n, wq]
            part = nt(lhs.reshape(-1, 256), rhs.reshape(-1, 256))
            total = part if total is None else total + part
        return total

    every = slice(0, 4)
    first_1, first_2 = NX * h_up1, NX * h_up2
    last_1, last_2 = NX - first_1, NX - first_2

    def half(p, piece, whole, base):
        nacc[p] = tile(piece, every, whole, every, base).reshape(4, 32, 512)

    def halves():
        half(0, sf, bo, first_1)
        half(1, sf, bx, first_1)

    def arrive(copies):
        for c in copies:
            c.wait_recv()

    cxf = [[copy(chunk(gfar, c), chunk(gfar, c), xs[d]) for d in range(3)] for c in range(5)]
    ct_far = [copy(bo.at[far4, q], bx.at[far4, q], twin) for q in range(4)]
    to_far = [slices(far4, q) for q in range(4)]
    for step in range(6):
        if step < 5:
            cz[step].wait_recv()
            for c in cxf[step]:
                c.start()
        if step == 3:
            to_near[1]()
        if step == 4:
            to_near[2].wait_recv()
            pl.when(h_up1 == h)(halves)
        if step > 0:
            arrive(cxf[step - 1])
        if step in (1, 2, 3, 5):
            q = min(step, 4) - 1
            to_far[q][0]()
            ct_far[q].start()
    for part in to_far[:3]:
        part[1]()

    def amplitude(integral, first, second, q, rows, cols=slice(None)):
        gap = vv[q, rows, cols] - eps[first, 0:1, cols] - eps[second, 0:1, cols]
        return (-integral / gap).astype(BF)

    def parts(p, n):
        if n == 1:
            return [t.at[p, 0:2, mine, 0:256]]
        upto, new = slice(0, 128 * n + 128), slice(128 * n, 128 * n + 128)
        return [t.at[p, n, mine, upto], t.at[p, 0:n, mine, new]]

    gather = [
        [[copy(src, src, xs[d], "even" if p == 2 else "all") for d in range(3) for src in parts(p, n)] for n in (1, 2, 3)]
        for p in range(3)
    ]

    def batch(p, n, piece, whole, base, first, second):
        def block(rows, cols):
            total = tile(piece, slice(*rows), whole, slice(*cols), base)
            lanes = slice(128 * cols[0], 128 * cols[1])
            for q in range(*rows):
                start = 32 * (q - rows[0])
                whole_sum = nacc[p, q, :, lanes] + total[start:start + 32]
                t[p, q, mine, lanes] = amplitude(whole_sum, first, second, q, mine, lanes)

        if n == 1:
            block((0, 2), (0, 2))
        else:
            block((n, n + 1), (0, n + 1))
            block((0, n), (n, n + 1))
        for c in gather[p][n - 1]:
            c.start()

    def next_chip(n):
        batch(0, n, sf, bo, last_1, 0, 2)
        batch(1, n, sf, bx, last_1, 1, 2)

    def chip_after(n):
        batch(2, n, sg, bx, last_2, 1, 3)

    arrive(ce + [part[2] for part in to_far[:2]] + ct_far[:2])

    @pl.when(h_up1 != h)
    def _():
        arrive(ct_far[2:])
        halves()

    next_chip(1)
    pl.when(h_up1 == h)(lambda: arrive(ct_far[2:]))
    to_far[3][1]()

    @even
    def _():
        arrive([to_near[3]] + [part[3] for part in to_far[:2]])
        half(2, sg, bx, first_2)
        chip_after(1)

    to_far[2][2].wait_recv()
    next_chip(2)

    @even
    def _():
        to_far[2][3].wait_recv()
        chip_after(2)

    gram(acc, bo, bo, far, False)

    @pl.loop(0, 4)
    def _(q):
        rows = pl.ds(pl.multiple_of(128 * q, 128), 128)
        a0[q] = amplitude(acc[rows], 0, 0, q, slice(None))

    def weights(p, read, both):
        @pl.loop(0, 4)
        def _(q):
            rows = pl.ds(pl.multiple_of(128 * q, 128), 128)
            turned = jnp.concatenate([read(n, rows).T for n in range(4)], axis=1)
            tt[p, rows] = turned
            tq, turned = read(q, slice(None)).astype(F32), turned.astype(F32)
            if both:
                wt[rows] = (2.0 * tq - turned).astype(BF)
            w[p, rows] = (2.0 * turned - tq).astype(BF)

    def energy(p, read, first, second, slot):
        @pl.loop(0, 4)
        def _(q):
            rows = pl.ds(pl.multiple_of(128 * q, 128), 128)
            tq = read(q, slice(None)).astype(F32)
            gap = vv[q] - eps[first, 0:1, :] - eps[second, 0:1, :]
            wide = 2.0 * tq - tt[p, rows].astype(F32)
            esum[slot, 0:1] += jnp.sum(gap * tq * wide, axis=0, keepdims=True)

    def times(weight, factor):
        return jnp.dot(weight, factor.reshape(512, 256), preferred_element_type=F32)

    def amplitudes(p):
        return lambda q, cols: t[p, q, :, cols]

    def own_amplitudes(q, cols):
        return a0[q, :, cols]

    def own_pair():
        weights(3, own_amplitudes, False)
        gown[...] = times(w[3], bo[g])

    def chip_pair():
        gram(acc2, bo, bx, far, False)

        @pl.loop(0, 4)
        def _(q):
            rows = pl.ds(pl.multiple_of(128 * q, 128), 128)
            t[2, q] = amplitude(acc2[rows], 1, 0, q, slice(None))
        weights(2, amplitudes(2), True)
        gown[...] += times(wt[...], bx[g])
        goth[...] = times(w[2], bo[g])

    @odd
    def _():
        own_pair()
        chip_pair()

    @even
    def _():
        to_far[3][3].wait_recv()
        chip_after(3)

    to_far[3][2].wait_recv()
    next_chip(3)
    pl.when(y == 0)(cr_f.start)
    pl.when((y < 2) & (k == 0))(cr_g.start)
    even(own_pair)

    c_f = copy(out3.at[0], in3.at[0], up1)
    c_g = copy(out3.at[1], in3.at[1], up2, "even")
    c_x = copy(out3.at[2], in3.at[2], twin)

    @even
    def _():
        arrive(sum(gather[2], []))
        weights(2, amplitudes(2), True)
        out3[1] = times(wt[...], bx[g_up2]).astype(BF)
        c_g.start()

    arrive(sum(gather[0], []))
    weights(0, amplitudes(0), True)
    gf[...] = times(wt[...], bo[g_up1])
    arrive(sum(gather[1], []))
    weights(1, amplitudes(1), True)
    out3[0] = (gf[...] + times(wt[...], bx[g_up1])).astype(BF)
    c_f.start()

    @even
    def _():
        cr_g.wait_recv()
        goth[...] = times(w[2], rg[...])

    cr_f.wait_recv()
    out3[2] = (goth[...] + times(w[1], rf[...])).astype(BF)
    c_x.start()
    gown[...] += times(w[0], rf[...])
    energy(3, own_amplitudes, 0, 0, 0)
    energy(0, amplitudes(0), 0, 2, 2)
    energy(1, amplitudes(1), 1, 2, 1)
    energy(2, amplitudes(2), 1, 3 * (1 - k), 3)

    lane = lax.broadcasted_iota(jnp.int32, (8, 128), 1)
    total = [-jnp.sum(esum[n, 0:1], axis=1, keepdims=True) for n in range(4)]
    first_at = 1 + 2 * k
    en[0] = jnp.where(lane == first_at, total[1], jnp.where(lane == 4 - first_at, total[3], 0.0))
    c_e = copy(en.at[0], en.at[1], twin)
    c_e.start()
    kept = jnp.where(lane == 0, total[0], jnp.where(lane == 2, total[2], 0.0))
    c_e.wait_recv()
    energy_ref[...] = (kept + en[1])[0:1, 0:4]

    c_x.wait_recv()
    gown[...] += in3[2].astype(F32)
    c_f.wait_recv()
    gown[...] += in3[0].astype(F32)

    @even
    def _():
        c_g.wait_recv()
        gown[...] += in3[1].astype(F32)

    for n in range(4):
        gamma_ref[:, 128 * n:128 * n + 128] = gown[128 * n:128 * n + 128].T

    for name, sender in who.items():
        left = [c for c, n in used if n == name and all(c is not d for d in done)]

        def finish(left=left):
            for c in left:
                c.wait_send()
        finish() if sender is None else pl.when(sender)(finish)


def per_device(factors, occ_energy, vir_energy):
    vmem = pl.BlockSpec(memory_space=pltpu.VMEM)
    hbm = pl.BlockSpec(memory_space=pl.ANY)
    gamma, energy = pl.pallas_call(
        kernel,
        out_shape=(
            jax.ShapeDtypeStruct((256, 512), F32),
            jax.ShapeDtypeStruct((1, 4), F32),
        ),
        in_specs=[hbm, pl.BlockSpec(memory_space=pltpu.SMEM), hbm],
        out_specs=(vmem, vmem),
        scratch_shapes=[
            pltpu.VMEM((8, 4, 128, 256), BF),
            pltpu.VMEM((8, 4, 128, 256), BF),
            pltpu.VMEM((8, 4, 32, 256), BF),
            pltpu.VMEM((8, 4, 32, 256), BF),
            pltpu.VMEM((8, 4, 32, 256), BF),
            pltpu.VMEM((4, 128, 256), BF),
            pltpu.VMEM((4, 128, 256), BF),
            pltpu.VMEM((3, 4, 128, 512), BF),
            pltpu.VMEM((4, 128, 512), BF),
            pltpu.VMEM((4, 128, 512), F32),
            pltpu.VMEM((512, 512), F32),
            pltpu.VMEM((512, 512), F32),
            pltpu.VMEM((3, 4, 32, 512), F32),
            pltpu.VMEM((4, 512, 512), BF),
            pltpu.VMEM((512, 512), BF),
            pltpu.VMEM((4, 512, 512), BF),
            pltpu.VMEM((512, 256), F32),
            pltpu.VMEM((512, 256), F32),
            pltpu.VMEM((512, 256), F32),
            pltpu.VMEM((3, 512, 256), BF),
            pltpu.VMEM((3, 512, 256), BF),
            pltpu.VMEM((4, 8, 512), F32),
            pltpu.VMEM((4, 8, 512), F32),
            pltpu.VMEM((2, 8, 128), F32),
            pltpu.VMEM((256, 512), BF),
            pltpu.VMEM((1, 512), F32),
            pltpu.SemaphoreType.DMA((2,)),
            pltpu.SemaphoreType.DMA((COPIES,)),
            pltpu.SemaphoreType.DMA((COPIES,)),
        ],
        compiler_params=pltpu.CompilerParams(
            collective_id=0, has_side_effects=True, vmem_limit_bytes=60 << 20
        ),
        name="pairs",
    )(factors.reshape(256, 512), occ_energy, vir_energy.reshape(1, 512))
    return energy, gamma.reshape(256, 1, 512)


def solution(mesh):
    return jax.shard_map(
        per_device,
        mesh=mesh,
        in_specs=(P("aux", "blk", None), P("blk"), P()),
        out_specs=(P("blk", None), P("aux", "blk", None)),
        check_vma=False,
    )
```

```python
import jax
import jax.numpy as jnp
from jax import lax
from jax.experimental import pallas as pl
from jax.experimental.pallas import tpu as pltpu
from jax.sharding import PartitionSpec as P

MESH = pl.DeviceIdType.MESH
BF = jnp.bfloat16
F32 = jnp.float32
NX = 4
NU = 64
HALF = NU // 2
COPIES = 144


def place(x, u, k):
    u = lax.rem(u, NU)
    return lax.rem(u, HALF) * 2 + k, lax.div(u, HALF) * NX + lax.rem(x, NX)


def nt(lhs, rhs):
    return lax.dot_general(lhs, rhs, (((1,), (1,)), ((), ())), preferred_element_type=F32)


def kernel(
    f_ref, occ_ref, vir_ref, gamma_ref, energy_ref,
    bo, bx, sf, sg, sv, rf, rg, t, a0, vv, acc, acc2, nacc, w, wt, tt,
    gown, goth, gf, out3, in3, eps, esum, en, f_own, vir, local, send, recv,
):
    b = lax.axis_index("blk")
    a = lax.axis_index("aux")
    k = lax.rem(b, 2)
    h = lax.div(a, NX)
    x = lax.rem(a, NX)
    u = HALF * h + lax.div(b, 2)
    y = lax.rem(u, 4)
    g = NX * h + x
    near = NX * h
    far = NX * (1 - h)
    gfar = far + x
    xs = [place(x + d, u, k) for d in (1, 2, 3)]
    partner = place(x, u + HALF, k)
    twin = place(x, u, 1 - k)
    down1, down2 = place(x, u + NU - 1, k), place(x, u + NU - 2, k)
    up1, up2 = place(x, u + 1, k), place(x, u + 2, k)
    h_down1 = lax.div(lax.rem(u + NU - 1, NU), HALF)
    h_down2 = lax.div(lax.rem(u + NU - 2, NU), HALF)
    h_up1, h_up2 = lax.div(lax.rem(u + 1, NU), HALF), lax.div(lax.rem(u + 2, NU), HALF)
    g_up1, g_up2 = NX * h_up1 + x, NX * h_up2 + x
    mine = pl.ds(pl.multiple_of(32 * x, 32), 32)

    barrier = pltpu.get_barrier_semaphore()
    down4, up4 = place(x, u + NU - 4, k), place(x, u + 4, k)
    others = xs + [partner, twin, down1, down2, up1, up2, down4, up4]
    for device in others:
        pl.semaphore_signal(barrier, inc=1, device_id=device, device_id_type=MESH)

    who = {
        "all": None,
        "even": k == 0,
        "skip": (k == 0) & (y > 0),
        "round": (k == 0) & (y == 0),
        "rounded": (k == 0) & (y == 2),
    }
    used, done = [], []

    def copy(src, dst, device, sender="all", lands_as=None):
        n = len(used)
        made = pltpu.make_async_remote_copy(
            src_ref=src, dst_ref=dst, send_sem=send.at[n],
            recv_sem=recv.at[n if lands_as is None else slot_of[id(lands_as)]],
            device_id=device, device_id_type=MESH,
        )
        slot_of[id(made)] = n
        used.append((made, sender))
        return made

    slot_of = {}

    def only(sender, body):
        pl.when(who[sender])(body)

    def sent(*copies):
        for c in copies:
            c.wait_send()
            done.append(c)

    def even(body):
        pl.when(k == 0)(body)

    def odd(body):
        pl.when(k == 1)(body)

    reads = [pltpu.make_async_copy(f_ref, f_own, local.at[0]), pltpu.make_async_copy(vir_ref, vir, local.at[1])]
    for c in reads:
        c.start()
    for c in reads:
        c.wait()

    bo[g] = f_own[...].T.reshape(4, 128, 256)
    eps[0] = jnp.full((8, 512), occ_ref[0], F32)
    row = jnp.broadcast_to(vir[...], (128, 512))
    for q in range(4):
        column = jnp.broadcast_to(row[:, 128 * q:128 * q + 128].T[:, 0:1], (128, 512))
        vv[q] = column + row
    esum[...] = jnp.zeros_like(esum)

    pl.semaphore_wait(barrier, len(others))

    def chunk(group, c):
        q, first, rows = ((0, 0, 128), (1, 0, 128), (2, 0, 128), (3, 0, 64), (3, 64, 64))[c]
        return bo.at[group, q, pl.ds(first, rows)]

    cz = [copy(chunk(g, c), chunk(g, c), partner) for c in range(5)]
    cx = [copy(bo.at[g], bo.at[g], xs[d]) for d in range(3)]
    ce = [copy(eps.at[0], eps.at[n], device) for n, device in ((1, twin), (2, down1), (3, down2))]
    cr_f = copy(bo.at[NX * h_down1 + x], rf, down1)
    cr_g = copy(bo.at[NX * h_down2 + x], rg, down2, "even")
    for c in cz[:2] + cx + ce:
        c.start()
    pl.when(y > 0)(cr_f.start)
    pl.when((y > 1) & (k == 0))(cr_g.start)
    near4, far4 = pl.ds(near, NX), pl.ds(far, NX)
    ct_near = copy(bo.at[near4], bx.at[near4], twin)

    def slices(groups, q):
        own = bo.at[groups, q, mine]
        there = sv.at[groups, q]
        f = copy(own, sf.at[groups, q], down1)
        g = copy(own, sg.at[groups, q], down2, "skip")
        g_out = copy(own, there, up2, "round")
        g_in = copy(there, sg.at[groups, q], down4, "rounded", g)

        def first():
            f.start()
            only("skip", g.start)
            only("round", g_out.start)

        def second():
            @pl.when(who["rounded"])
            def _():
                g_out.wait_recv()
                g_in.start()

        return first, second, f, g

    to_near = slices(near4, slice(None))
    sent(cz[0])
    cz[2].start()
    for c in cx:
        c.wait_recv()
    ct_near.start()
    to_near[0]()
    sent(cz[1])
    cz[3].start()
    cz[4].start()

    def gram(dst, lhs, rhs, base, init):
        @pl.loop(0, 2)
        def _(c):
            total = None
            for n in range(NX):
                part = nt(lhs[base + n].reshape(512, 256), rhs[base + n, pl.ds(2 * c, 2)].reshape(256, 256))
                total = part if total is None else total + part
            cols = pl.ds(pl.multiple_of(256 * c, 256), 256)
            dst[:, cols] = total if init else dst[:, cols] + total

    gram(acc, bo, bo, near, True)
    ct_near.wait_recv()
    odd(lambda: gram(acc2, bo, bx, near, True))

    def tile(piece, pq, whole, wq, base):
        total = None
        for n in range(NX):
            lhs, rhs = piece[base + n, pq], whole[base + n, wq]
            part = nt(lhs.reshape(-1, 256), rhs.reshape(-1, 256))
            total = part if total is None else total + part
        return total

    every = slice(0, 4)
    first_1, first_2 = NX * h_up1, NX * h_up2
    last_1, last_2 = NX - first_1, NX - first_2

    def half(p, piece, whole, base):
        nacc[p] = tile(piece, every, whole, every, base).reshape(4, 32, 512)

    def halves():
        half(0, sf, bo, first_1)
        half(1, sf, bx, first_1)

    def arrive(copies):
        for c in copies:
            c.wait_recv()

    cxf = [[copy(chunk(gfar, c), chunk(gfar, c), xs[d]) for d in range(3)] for c in range(5)]
    ct_far = [copy(bo.at[far4, q], bx.at[far4, q], twin) for q in range(4)]
    to_far = [slices(far4, q) for q in range(4)]
    for step in range(6):
        if step < 5:
            cz[step].wait_recv()
            for c in cxf[step]:
                c.start()
        if step == 3:
            to_near[1]()
        if step == 4:
            to_near[2].wait_recv()
            pl.when(h_up1 == h)(halves)
        if step > 0:
            arrive(cxf[step - 1])
        if step in (1, 2, 3, 5):
            q = min(step, 4) - 1
            to_far[q][0]()
            ct_far[q].start()
    for part in to_far[:3]:
        part[1]()
    pl.when(y == 0)(cr_f.start)
    pl.when((y < 2) & (k == 0))(cr_g.start)

    def amplitude(integral, first, second, q, rows, cols=slice(None)):
        gap = vv[q, rows, cols] - eps[first, 0:1, cols] - eps[second, 0:1, cols]
        return (-integral / gap).astype(BF)

    def parts(p, n):
        if n == 1:
            return [t.at[p, 0:2, mine, 0:256]]
        upto, new = slice(0, 128 * n + 128), slice(128 * n, 128 * n + 128)
        return [t.at[p, n, mine, upto], t.at[p, 0:n, mine, new]]

    gather = [
        [[copy(src, src, xs[d], "even" if p == 2 else "all") for d in range(3) for src in parts(p, n)] for n in (1, 2, 3)]
        for p in range(3)
    ]

    def batch(p, n, piece, whole, base, first, second):
        def block(rows, cols):
            total = tile(piece, slice(*rows), whole, slice(*cols), base)
            lanes = slice(128 * cols[0], 128 * cols[1])
            for q in range(*rows):
                start = 32 * (q - rows[0])
                whole_sum = nacc[p, q, :, lanes] + total[start:start + 32]
                t[p, q, mine, lanes] = amplitude(whole_sum, first, second, q, mine, lanes)

        if n == 1:
            block((0, 2), (0, 2))
        else:
            block((n, n + 1), (0, n + 1))
            block((0, n), (n, n + 1))
        for c in gather[p][n - 1]:
            c.start()

    def next_chip(n):
        batch(0, n, sf, bo, last_1, 0, 2)
        batch(1, n, sf, bx, last_1, 1, 2)

    def chip_after(n):
        batch(2, n, sg, bx, last_2, 1, 3)

    arrive(ce + [part[2] for part in to_far[:2]] + ct_far[:2])

    @pl.when(h_up1 != h)
    def _():
        arrive(ct_far[2:])
        halves()

    next_chip(1)
    pl.when(h_up1 == h)(lambda: arrive(ct_far[2:]))
    to_far[3][1]()

    @even
    def _():
        arrive([to_near[3]] + [part[3] for part in to_far[:2]])
        half(2, sg, bx, first_2)
        chip_after(1)

    to_far[2][2].wait_recv()
    next_chip(2)

    @even
    def _():
        to_far[2][3].wait_recv()
        chip_after(2)

    gram(acc, bo, bo, far, False)

    @pl.loop(0, 4)
    def _(q):
        rows = pl.ds(pl.multiple_of(128 * q, 128), 128)
        a0[q] = amplitude(acc[rows], 0, 0, q, slice(None))

    def weights(p, read, both):
        @pl.loop(0, 4)
        def _(q):
            rows = pl.ds(pl.multiple_of(128 * q, 128), 128)
            turned = jnp.concatenate([read(n, rows).T for n in range(4)], axis=1)
            tt[p, rows] = turned
            tq, turned = read(q, slice(None)).astype(F32), turned.astype(F32)
            if both:
                wt[rows] = (2.0 * tq - turned).astype(BF)
            w[p, rows] = (2.0 * turned - tq).astype(BF)

    def energy(p, read, first, second, slot):
        @pl.loop(0, 4)
        def _(q):
            rows = pl.ds(pl.multiple_of(128 * q, 128), 128)
            tq = read(q, slice(None)).astype(F32)
            gap = vv[q] - eps[first, 0:1, :] - eps[second, 0:1, :]
            wide = 2.0 * tq - tt[p, rows].astype(F32)
            esum[slot, 0:1] += jnp.sum(gap * tq * wide, axis=0, keepdims=True)

    def times(weight, factor):
        return jnp.dot(weight, factor.reshape(512, 256), preferred_element_type=F32)

    def amplitudes(p):
        return lambda q, cols: t[p, q, :, cols]

    def own_amplitudes(q, cols):
        return a0[q, :, cols]

    def own_pair():
        weights(3, own_amplitudes, False)
        gown[...] = times(w[3], bo[g])

    def chip_pair():
        gram(acc2, bo, bx, far, False)

        @pl.loop(0, 4)
        def _(q):
            rows = pl.ds(pl.multiple_of(128 * q, 128), 128)
            t[2, q] = amplitude(acc2[rows], 1, 0, q, slice(None))
        weights(2, amplitudes(2), True)
        gown[...] += times(wt[...], bx[g])
        goth[...] = times(w[2], bo[g])

    @odd
    def _():
        own_pair()
        chip_pair()

    to_far[3][2].wait_recv()
    next_chip(3)

    @even
    def _():
        to_far[3][3].wait_recv()
        chip_after(3)
        own_pair()

    c_f = copy(out3.at[0], in3.at[0], up1)
    c_g = copy(out3.at[1], in3.at[1], up2, "even")
    c_x = copy(out3.at[2], in3.at[2], twin)

    arrive(sum(gather[0], []))
    weights(0, amplitudes(0), True)
    gf[...] = times(wt[...], bo[g_up1])
    arrive(sum(gather[1], []))
    weights(1, amplitudes(1), True)
    out3[0] = (gf[...] + times(wt[...], bx[g_up1])).astype(BF)
    c_f.start()

    @even
    def _():
        arrive(sum(gather[2], []))
        weights(2, amplitudes(2), True)
        out3[1] = times(wt[...], bx[g_up2]).astype(BF)
        c_g.start()
        cr_g.wait_recv()
        goth[...] = times(w[2], rg[...])

    cr_f.wait_recv()
    out3[2] = (goth[...] + times(w[1], rf[...])).astype(BF)
    c_x.start()
    gown[...] += times(w[0], rf[...])
    energy(3, own_amplitudes, 0, 0, 0)
    energy(0, amplitudes(0), 0, 2, 2)
    energy(1, amplitudes(1), 1, 2, 1)
    energy(2, amplitudes(2), 1, 3 * (1 - k), 3)

    lane = lax.broadcasted_iota(jnp.int32, (8, 128), 1)
    total = [-jnp.sum(esum[n, 0:1], axis=1, keepdims=True) for n in range(4)]
    first_at = 1 + 2 * k
    en[0] = jnp.where(lane == first_at, total[1], jnp.where(lane == 4 - first_at, total[3], 0.0))
    c_e = copy(en.at[0], en.at[1], twin)
    c_e.start()
    kept = jnp.where(lane == 0, total[0], jnp.where(lane == 2, total[2], 0.0))
    c_e.wait_recv()
    energy_ref[...] = (kept + en[1])[0:1, 0:4]

    c_x.wait_recv()
    gown[...] += in3[2].astype(F32)
    c_f.wait_recv()
    gown[...] += in3[0].astype(F32)

    @even
    def _():
        c_g.wait_recv()
        gown[...] += in3[1].astype(F32)

    for n in range(4):
        gamma_ref[:, 128 * n:128 * n + 128] = gown[128 * n:128 * n + 128].T

    for name, sender in who.items():
        left = [c for c, n in used if n == name and all(c is not d for d in done)]

        def finish(left=left):
            for c in left:
                c.wait_send()
        finish() if sender is None else pl.when(sender)(finish)


def per_device(factors, occ_energy, vir_energy):
    vmem = pl.BlockSpec(memory_space=pltpu.VMEM)
    hbm = pl.BlockSpec(memory_space=pl.ANY)
    gamma, energy = pl.pallas_call(
        kernel,
        out_shape=(
            jax.ShapeDtypeStruct((256, 512), F32),
            jax.ShapeDtypeStruct((1, 4), F32),
        ),
        in_specs=[hbm, pl.BlockSpec(memory_space=pltpu.SMEM), hbm],
        out_specs=(vmem, vmem),
        scratch_shapes=[
            pltpu.VMEM((8, 4, 128, 256), BF),
            pltpu.VMEM((8, 4, 128, 256), BF),
            pltpu.VMEM((8, 4, 32, 256), BF),
            pltpu.VMEM((8, 4, 32, 256), BF),
            pltpu.VMEM((8, 4, 32, 256), BF),
            pltpu.VMEM((4, 128, 256), BF),
            pltpu.VMEM((4, 128, 256), BF),
            pltpu.VMEM((3, 4, 128, 512), BF),
            pltpu.VMEM((4, 128, 512), BF),
            pltpu.VMEM((4, 128, 512), F32),
            pltpu.VMEM((512, 512), F32),
            pltpu.VMEM((512, 512), F32),
            pltpu.VMEM((3, 4, 32, 512), F32),
            pltpu.VMEM((4, 512, 512), BF),
            pltpu.VMEM((512, 512), BF),
            pltpu.VMEM((4, 512, 512), BF),
            pltpu.VMEM((512, 256), F32),
            pltpu.VMEM((512, 256), F32),
            pltpu.VMEM((512, 256), F32),
            pltpu.VMEM((3, 512, 256), BF),
            pltpu.VMEM((3, 512, 256), BF),
            pltpu.VMEM((4, 8, 512), F32),
            pltpu.VMEM((4, 8, 512), F32),
            pltpu.VMEM((2, 8, 128), F32),
            pltpu.VMEM((256, 512), BF),
            pltpu.VMEM((1, 512), F32),
            pltpu.SemaphoreType.DMA((2,)),
            pltpu.SemaphoreType.DMA((COPIES,)),
            pltpu.SemaphoreType.DMA((COPIES,)),
        ],
        compiler_params=pltpu.CompilerParams(
            collective_id=0, has_side_effects=True, vmem_limit_bytes=60 << 20
        ),
        name="pairs",
    )(factors.reshape(256, 512), occ_energy, vir_energy.reshape(1, 512))
    return energy, gamma.reshape(256, 1, 512)


def solution(mesh):
    return jax.shard_map(
        per_device,
        mesh=mesh,
        in_specs=(P("aux", "blk", None), P("blk"), P()),
        out_specs=(P("blk", None), P("aux", "blk", None)),
        check_vma=False,
    )
```

```python
import jax
import jax.numpy as jnp
from jax import lax
from jax.experimental import pallas as pl
from jax.experimental.pallas import tpu as pltpu
from jax.sharding import PartitionSpec as P

MESH = pl.DeviceIdType.MESH
BF = jnp.bfloat16
F32 = jnp.float32
NX = 4
NU = 64
HALF = NU // 2
COPIES = 144


def place(x, u, k):
    u = lax.rem(u, NU)
    return lax.rem(u, HALF) * 2 + k, lax.div(u, HALF) * NX + lax.rem(x, NX)


def nt(lhs, rhs):
    return lax.dot_general(lhs, rhs, (((1,), (1,)), ((), ())), preferred_element_type=F32)


def kernel(
    f_ref, occ_ref, vir_ref, gamma_ref, energy_ref,
    bo, bx, sf, sg, sv, rf, rg, t, a0, vv, acc, acc2, nacc, w, wt, tt,
    gown, goth, gf, out3, in3, eps, esum, en, f_own, vir, local, send, recv,
):
    b = lax.axis_index("blk")
    a = lax.axis_index("aux")
    k = lax.rem(b, 2)
    h = lax.div(a, NX)
    x = lax.rem(a, NX)
    u = HALF * h + lax.div(b, 2)
    y = lax.rem(u, 4)
    g = NX * h + x
    near = NX * h
    far = NX * (1 - h)
    gfar = far + x
    xs = [place(x + d, u, k) for d in (1, 2, 3)]
    partner = place(x, u + HALF, k)
    twin = place(x, u, 1 - k)
    down1, down2 = place(x, u + NU - 1, k), place(x, u + NU - 2, k)
    up1, up2 = place(x, u + 1, k), place(x, u + 2, k)
    h_down1 = lax.div(lax.rem(u + NU - 1, NU), HALF)
    h_down2 = lax.div(lax.rem(u + NU - 2, NU), HALF)
    h_up1, h_up2 = lax.div(lax.rem(u + 1, NU), HALF), lax.div(lax.rem(u + 2, NU), HALF)
    g_up1, g_up2 = NX * h_up1 + x, NX * h_up2 + x
    mine = pl.ds(pl.multiple_of(32 * x, 32), 32)

    barrier = pltpu.get_barrier_semaphore()
    down4, up4 = place(x, u + NU - 4, k), place(x, u + 4, k)
    others = xs + [partner, twin, down1, down2, up1, up2, down4, up4]
    for device in others:
        pl.semaphore_signal(barrier, inc=1, device_id=device, device_id_type=MESH)

    who = {
        "all": None,
        "even": k == 0,
        "skip": (k == 0) & (y > 0),
        "round": (k == 0) & (y == 0),
        "rounded": (k == 0) & (y == 2),
    }
    used, done = [], []

    def copy(src, dst, device, sender="all", lands_as=None):
        n = len(used)
        made = pltpu.make_async_remote_copy(
            src_ref=src, dst_ref=dst, send_sem=send.at[n],
            recv_sem=recv.at[n if lands_as is None else slot_of[id(lands_as)]],
            device_id=device, device_id_type=MESH,
        )
        slot_of[id(made)] = n
        used.append((made, sender))
        return made

    slot_of = {}

    def only(sender, body):
        pl.when(who[sender])(body)

    def sent(*copies):
        for c in copies:
            c.wait_send()
            done.append(c)

    def even(body):
        pl.when(k == 0)(body)

    def odd(body):
        pl.when(k == 1)(body)

    reads = [pltpu.make_async_copy(f_ref, f_own, local.at[0]), pltpu.make_async_copy(vir_ref, vir, local.at[1])]
    for c in reads:
        c.start()
    for c in reads:
        c.wait()

    bo[g] = f_own[...].T.reshape(4, 128, 256)
    eps[0] = jnp.full((8, 512), occ_ref[0], F32)
    row = jnp.broadcast_to(vir[...], (128, 512))
    for q in range(4):
        column = jnp.broadcast_to(row[:, 128 * q:128 * q + 128].T[:, 0:1], (128, 512))
        vv[q] = column + row
    esum[...] = jnp.zeros_like(esum)

    pl.semaphore_wait(barrier, len(others))

    def chunk(group, c):
        q, first, rows = ((0, 0, 128), (1, 0, 128), (2, 0, 128), (3, 0, 64), (3, 64, 64))[c]
        return bo.at[group, q, pl.ds(first, rows)]

    cz = [copy(chunk(g, c), chunk(g, c), partner) for c in range(5)]
    cx = [copy(bo.at[g], bo.at[g], xs[d]) for d in range(3)]
    ce = [copy(eps.at[0], eps.at[n], device) for n, device in ((1, twin), (2, down1), (3, down2))]
    cr_f = copy(bo.at[NX * h_down1 + x], rf, down1)
    cr_g = copy(bo.at[NX * h_down2 + x], rg, down2, "even")
    for c in cz[:2] + cx + ce:
        c.start()
    pl.when(y > 0)(cr_f.start)
    pl.when((y > 1) & (k == 0))(cr_g.start)
    near4, far4 = pl.ds(near, NX), pl.ds(far, NX)
    ct_near = copy(bo.at[near4], bx.at[near4], twin)

    def slices(groups, q):
        own = bo.at[groups, q, mine]
        there = sv.at[groups, q]
        f = copy(own, sf.at[groups, q], down1)
        g = copy(own, sg.at[groups, q], down2, "skip")
        g_out = copy(own, there, up2, "round")
        g_in = copy(there, sg.at[groups, q], down4, "rounded", g)

        def first():
            f.start()
            only("skip", g.start)
            only("round", g_out.start)

        def second():
            @pl.when(who["rounded"])
            def _():
                g_out.wait_recv()
                g_in.start()

        return first, second, f, g

    to_near = slices(near4, slice(None))
    sent(cz[0])
    cz[2].start()
    for c in cx:
        c.wait_recv()
    ct_near.start()
    to_near[0]()
    sent(cz[1])
    cz[3].start()
    cz[4].start()

    def gram(dst, lhs, rhs, base, init):
        @pl.loop(0, 2)
        def _(c):
            total = None
            for n in range(NX):
                part = nt(lhs[base + n].reshape(512, 256), rhs[base + n, pl.ds(2 * c, 2)].reshape(256, 256))
                total = part if total is None else total + part
            cols = pl.ds(pl.multiple_of(256 * c, 256), 256)
            dst[:, cols] = total if init else dst[:, cols] + total

    gram(acc, bo, bo, near, True)
    ct_near.wait_recv()
    odd(lambda: gram(acc2, bo, bx, near, True))

    def tile(piece, pq, whole, wq, base):
        total = None
        for n in range(NX):
            lhs, rhs = piece[base + n, pq], whole[base + n, wq]
            part = nt(lhs.reshape(-1, 256), rhs.reshape(-1, 256))
            total = part if total is None else total + part
        return total

    every = slice(0, 4)
    first_1, first_2 = NX * h_up1, NX * h_up2
    last_1, last_2 = NX - first_1, NX - first_2

    def half(p, piece, whole, base):
        nacc[p] = tile(piece, every, whole, every, base).reshape(4, 32, 512)

    def halves():
        half(0, sf, bo, first_1)
        half(1, sf, bx, first_1)

    def arrive(copies):
        for c in copies:
            c.wait_recv()

    cxf = [[copy(chunk(gfar, c), chunk(gfar, c), xs[d]) for d in range(3)] for c in range(5)]
    ct_far = [copy(bo.at[far4, q], bx.at[far4, q], twin) for q in range(4)]
    to_far = [slices(far4, q) for q in range(4)]
    for step in range(6):
        if step < 5:
            cz[step].wait_recv()
            for c in cxf[step]:
                c.start()
        if step == 3:
            to_near[1]()
        if step == 4:
            to_near[2].wait_recv()
            pl.when(h_up1 == h)(halves)
        if step > 0:
            arrive(cxf[step - 1])
        if step in (1, 2, 3, 5):
            q = min(step, 4) - 1
            to_far[q][0]()
            ct_far[q].start()
    for part in to_far[:3]:
        part[1]()
    pl.when(y == 0)(cr_f.start)
    pl.when((y < 2) & (k == 0))(cr_g.start)

    def amplitude(integral, first, second, q, rows, cols=slice(None)):
        gap = vv[q, rows, cols] - eps[first, 0:1, cols] - eps[second, 0:1, cols]
        return (-integral / gap).astype(BF)

    def parts(p, n):
        if n == 1:
            return [t.at[p, 0:2, mine, 0:256]]
        upto, new = slice(0, 128 * n + 128), slice(128 * n, 128 * n + 128)
        return [t.at[p, n, mine, upto], t.at[p, 0:n, mine, new]]

    gather = [
        [[copy(src, src, xs[d], "even" if p == 2 else "all") for d in (1, 0, 2) for src in parts(p, n)] for n in (1, 2, 3)]
        for p in range(3)
    ]

    def batch(p, n, piece, whole, base, first, second):
        def block(rows, cols):
            total = tile(piece, slice(*rows), whole, slice(*cols), base)
            lanes = slice(128 * cols[0], 128 * cols[1])
            for q in range(*rows):
                start = 32 * (q - rows[0])
                whole_sum = nacc[p, q, :, lanes] + total[start:start + 32]
                t[p, q, mine, lanes] = amplitude(whole_sum, first, second, q, mine, lanes)

        if n == 1:
            block((0, 2), (0, 2))
        else:
            block((n, n + 1), (0, n + 1))
            block((0, n), (n, n + 1))
        for c in gather[p][n - 1]:
            c.start()

    def next_chip(n):
        batch(0, n, sf, bo, last_1, 0, 2)
        batch(1, n, sf, bx, last_1, 1, 2)

    def chip_after(n):
        batch(2, n, sg, bx, last_2, 1, 3)

    arrive(ce + [part[2] for part in to_far[:2]] + ct_far[:2])

    @pl.when(h_up1 != h)
    def _():
        arrive(ct_far[2:])
        halves()

    next_chip(1)
    pl.when(h_up1 == h)(lambda: arrive(ct_far[2:]))
    to_far[3][1]()

    @even
    def _():
        arrive([to_near[3]] + [part[3] for part in to_far[:2]])
        half(2, sg, bx, first_2)
        chip_after(1)

    @even
    def _():
        to_far[2][3].wait_recv()
        chip_after(2)

    to_far[2][2].wait_recv()
    next_chip(2)

    gram(acc, bo, bo, far, False)

    @pl.loop(0, 4)
    def _(q):
        rows = pl.ds(pl.multiple_of(128 * q, 128), 128)
        a0[q] = amplitude(acc[rows], 0, 0, q, slice(None))

    def weights(p, read, both):
        @pl.loop(0, 4)
        def _(q):
            rows = pl.ds(pl.multiple_of(128 * q, 128), 128)
            turned = jnp.concatenate([read(n, rows).T for n in range(4)], axis=1)
            tt[p, rows] = turned
            tq, turned = read(q, slice(None)).astype(F32), turned.astype(F32)
            if both:
                wt[rows] = (2.0 * tq - turned).astype(BF)
            w[p, rows] = (2.0 * turned - tq).astype(BF)

    def energy(p, read, first, second, slot):
        @pl.loop(0, 4)
        def _(q):
            rows = pl.ds(pl.multiple_of(128 * q, 128), 128)
            tq = read(q, slice(None)).astype(F32)
            gap = vv[q] - eps[first, 0:1, :] - eps[second, 0:1, :]
            wide = 2.0 * tq - tt[p, rows].astype(F32)
            esum[slot, 0:1] += jnp.sum(gap * tq * wide, axis=0, keepdims=True)

    def times(weight, factor):
        return jnp.dot(weight, factor.reshape(512, 256), preferred_element_type=F32)

    def amplitudes(p):
        return lambda q, cols: t[p, q, :, cols]

    def own_amplitudes(q, cols):
        return a0[q, :, cols]

    def own_pair():
        weights(3, own_amplitudes, False)
        gown[...] = times(w[3], bo[g])

    def chip_pair():
        gram(acc2, bo, bx, far, False)

        @pl.loop(0, 4)
        def _(q):
            rows = pl.ds(pl.multiple_of(128 * q, 128), 128)
            t[2, q] = amplitude(acc2[rows], 1, 0, q, slice(None))
        weights(2, amplitudes(2), True)
        gown[...] += times(wt[...], bx[g])
        goth[...] = times(w[2], bo[g])

    @odd
    def _():
        own_pair()
        chip_pair()

    @even
    def _():
        to_far[3][3].wait_recv()
        chip_after(3)

    to_far[3][2].wait_recv()
    next_chip(3)
    even(own_pair)

    c_f = copy(out3.at[0], in3.at[0], up1)
    c_g = copy(out3.at[1], in3.at[1], up2, "even")
    c_x = copy(out3.at[2], in3.at[2], twin)

    @even
    def _():
        arrive(sum(gather[2], []))
        weights(2, amplitudes(2), True)
        out3[1] = times(wt[...], bx[g_up2]).astype(BF)
        c_g.start()

    arrive(sum(gather[0], []))
    weights(0, amplitudes(0), True)
    gf[...] = times(wt[...], bo[g_up1])
    arrive(sum(gather[1], []))
    weights(1, amplitudes(1), True)
    out3[0] = (gf[...] + times(wt[...], bx[g_up1])).astype(BF)
    c_f.start()

    @even
    def _():
        cr_g.wait_recv()
        goth[...] = times(w[2], rg[...])

    cr_f.wait_recv()
    out3[2] = (goth[...] + times(w[1], rf[...])).astype(BF)
    c_x.start()
    gown[...] += times(w[0], rf[...])
    energy(3, own_amplitudes, 0, 0, 0)
    energy(0, amplitudes(0), 0, 2, 2)
    energy(1, amplitudes(1), 1, 2, 1)
    energy(2, amplitudes(2), 1, 3 * (1 - k), 3)

    lane = lax.broadcasted_iota(jnp.int32, (8, 128), 1)
    total = [-jnp.sum(esum[n, 0:1], axis=1, keepdims=True) for n in range(4)]
    first_at = 1 + 2 * k
    en[0] = jnp.where(lane == first_at, total[1], jnp.where(lane == 4 - first_at, total[3], 0.0))
    c_e = copy(en.at[0], en.at[1], twin)
    c_e.start()
    kept = jnp.where(lane == 0, total[0], jnp.where(lane == 2, total[2], 0.0))
    c_e.wait_recv()
    energy_ref[...] = (kept + en[1])[0:1, 0:4]

    c_x.wait_recv()
    gown[...] += in3[2].astype(F32)
    c_f.wait_recv()
    gown[...] += in3[0].astype(F32)

    @even
    def _():
        c_g.wait_recv()
        gown[...] += in3[1].astype(F32)

    for n in range(4):
        gamma_ref[:, 128 * n:128 * n + 128] = gown[128 * n:128 * n + 128].T

    for name, sender in who.items():
        left = [c for c, n in used if n == name and all(c is not d for d in done)]

        def finish(left=left):
            for c in left:
                c.wait_send()
        finish() if sender is None else pl.when(sender)(finish)


def per_device(factors, occ_energy, vir_energy):
    vmem = pl.BlockSpec(memory_space=pltpu.VMEM)
    hbm = pl.BlockSpec(memory_space=pl.ANY)
    gamma, energy = pl.pallas_call(
        kernel,
        out_shape=(
            jax.ShapeDtypeStruct((256, 512), F32),
            jax.ShapeDtypeStruct((1, 4), F32),
        ),
        in_specs=[hbm, pl.BlockSpec(memory_space=pltpu.SMEM), hbm],
        out_specs=(vmem, vmem),
        scratch_shapes=[
            pltpu.VMEM((8, 4, 128, 256), BF),
            pltpu.VMEM((8, 4, 128, 256), BF),
            pltpu.VMEM((8, 4, 32, 256), BF),
            pltpu.VMEM((8, 4, 32, 256), BF),
            pltpu.VMEM((8, 4, 32, 256), BF),
            pltpu.VMEM((4, 128, 256), BF),
            pltpu.VMEM((4, 128, 256), BF),
            pltpu.VMEM((3, 4, 128, 512), BF),
            pltpu.VMEM((4, 128, 512), BF),
            pltpu.VMEM((4, 128, 512), F32),
            pltpu.VMEM((512, 512), F32),
            pltpu.VMEM((512, 512), F32),
            pltpu.VMEM((3, 4, 32, 512), F32),
            pltpu.VMEM((4, 512, 512), BF),
            pltpu.VMEM((512, 512), BF),
            pltpu.VMEM((4, 512, 512), BF),
            pltpu.VMEM((512, 256), F32),
            pltpu.VMEM((512, 256), F32),
            pltpu.VMEM((512, 256), F32),
            pltpu.VMEM((3, 512, 256), BF),
            pltpu.VMEM((3, 512, 256), BF),
            pltpu.VMEM((4, 8, 512), F32),
            pltpu.VMEM((4, 8, 512), F32),
            pltpu.VMEM((2, 8, 128), F32),
            pltpu.VMEM((256, 512), BF),
            pltpu.VMEM((1, 512), F32),
            pltpu.SemaphoreType.DMA((2,)),
            pltpu.SemaphoreType.DMA((COPIES,)),
            pltpu.SemaphoreType.DMA((COPIES,)),
        ],
        compiler_params=pltpu.CompilerParams(
            collective_id=0, has_side_effects=True, vmem_limit_bytes=60 << 20
        ),
        name="pairs",
    )(factors.reshape(256, 512), occ_energy, vir_energy.reshape(1, 512))
    return energy, gamma.reshape(256, 1, 512)


def solution(mesh):
    return jax.shard_map(
        per_device,
        mesh=mesh,
        in_specs=(P("aux", "blk", None), P("blk"), P()),
        out_specs=(P("blk", None), P("aux", "blk", None)),
        check_vma=False,
    )
```

```python
import jax
import jax.numpy as jnp
from jax import lax
from jax.experimental import pallas as pl
from jax.experimental.pallas import tpu as pltpu
from jax.sharding import PartitionSpec as P

MESH = pl.DeviceIdType.MESH
BF = jnp.bfloat16
F32 = jnp.float32
NX = 4
NU = 64
HALF = NU // 2
COPIES = 128


def place(x, u, k):
    u = lax.rem(u, NU)
    return lax.rem(u, HALF) * 2 + k, lax.div(u, HALF) * NX + lax.rem(x, NX)


def nt(lhs, rhs):
    return lax.dot_general(lhs, rhs, (((1,), (1,)), ((), ())), preferred_element_type=F32)


def kernel(
    f_ref, occ_ref, vir_ref, gamma_ref, energy_ref,
    bo, bx, sf, sg, sv, rf, rg, t, a0, vv, acc, acc2, w, wt, tt,
    gown, goth, gf, out3, in3, eps, esum, en, f_own, vir, local, send, recv,
):
    b = lax.axis_index("blk")
    a = lax.axis_index("aux")
    k = lax.rem(b, 2)
    h = lax.div(a, NX)
    x = lax.rem(a, NX)
    u = HALF * h + lax.div(b, 2)
    y = lax.rem(u, 4)
    g = NX * h + x
    near = NX * h
    far = NX * (1 - h)
    gfar = far + x
    xs = [place(x + d, u, k) for d in (1, 2, 3)]
    partner = place(x, u + HALF, k)
    twin = place(x, u, 1 - k)
    down1, down2 = place(x, u + NU - 1, k), place(x, u + NU - 2, k)
    up1, up2 = place(x, u + 1, k), place(x, u + 2, k)
    h_down1 = lax.div(lax.rem(u + NU - 1, NU), HALF)
    h_down2 = lax.div(lax.rem(u + NU - 2, NU), HALF)
    g_up1 = NX * lax.div(lax.rem(u + 1, NU), HALF) + x
    g_up2 = NX * lax.div(lax.rem(u + 2, NU), HALF) + x
    mine = pl.ds(pl.multiple_of(32 * x, 32), 32)

    barrier = pltpu.get_barrier_semaphore()
    down4, up4 = place(x, u + NU - 4, k), place(x, u + 4, k)
    others = xs + [partner, twin, down1, down2, up1, up2, down4, up4]
    for device in others:
        pl.semaphore_signal(barrier, inc=1, device_id=device, device_id_type=MESH)

    who = {
        "all": None,
        "even": k == 0,
        "skip": (k == 0) & (y > 0),
        "round": (k == 0) & (y == 0),
        "rounded": (k == 0) & (y == 2),
    }
    used, done = [], []

    def copy(src, dst, device, sender="all", lands_as=None):
        n = len(used)
        made = pltpu.make_async_remote_copy(
            src_ref=src, dst_ref=dst, send_sem=send.at[n],
            recv_sem=recv.at[n if lands_as is None else slot_of[id(lands_as)]],
            device_id=device, device_id_type=MESH,
        )
        slot_of[id(made)] = n
        used.append((made, sender))
        return made

    slot_of = {}

    def only(sender, body):
        pl.when(who[sender])(body)

    def sent(*copies):
        for c in copies:
            c.wait_send()
            done.append(c)

    def even(body):
        pl.when(k == 0)(body)

    def odd(body):
        pl.when(k == 1)(body)

    reads = [pltpu.make_async_copy(f_ref, f_own, local.at[0]), pltpu.make_async_copy(vir_ref, vir, local.at[1])]
    for c in reads:
        c.start()
    for c in reads:
        c.wait()

    bo[g] = f_own[...].T.reshape(4, 128, 256)
    eps[0] = jnp.full((8, 512), occ_ref[0], F32)
    row = jnp.broadcast_to(vir[...], (128, 512))
    for q in range(4):
        column = jnp.broadcast_to(row[:, 128 * q:128 * q + 128].T[:, 0:1], (128, 512))
        vv[q] = column + row
    esum[...] = jnp.zeros_like(esum)

    pl.semaphore_wait(barrier, len(others))

    def chunk(group, c):
        q, first, rows = ((0, 0, 128), (1, 0, 128), (2, 0, 128), (3, 0, 64), (3, 64, 64))[c]
        return bo.at[group, q, pl.ds(first, rows)]

    cz = [copy(chunk(g, c), chunk(g, c), partner) for c in range(5)]
    cx = [copy(bo.at[g], bo.at[g], xs[d]) for d in range(3)]
    ce = [copy(eps.at[0], eps.at[n], device) for n, device in ((1, twin), (2, down1), (3, down2))]
    cr_f = copy(bo.at[NX * h_down1 + x], rf, down1)
    cr_g = copy(bo.at[NX * h_down2 + x], rg, down2, "even")
    for c in cz[:2] + cx + ce:
        c.start()
    pl.when(y > 0)(cr_f.start)
    pl.when((y > 1) & (k == 0))(cr_g.start)
    near4, far4 = pl.ds(near, NX), pl.ds(far, NX)
    ct_near = copy(bo.at[near4], bx.at[near4], twin)

    def slices(groups, q):
        own = bo.at[groups, q, mine]
        there = sv.at[groups, q]
        f = copy(own, sf.at[groups, q], down1)
        g = copy(own, sg.at[groups, q], down2, "skip")
        g_out = copy(own, there, up2, "round")
        g_in = copy(there, sg.at[groups, q], down4, "rounded", g)

        def first():
            f.start()
            only("skip", g.start)
            only("round", g_out.start)

        def second():
            @pl.when(who["rounded"])
            def _():
                g_out.wait_recv()
                g_in.start()

        return first, second, f, g

    to_near = slices(near4, slice(None))
    sent(cz[0])
    cz[2].start()
    for c in cx:
        c.wait_recv()
    ct_near.start()
    to_near[0]()
    sent(cz[1])
    cz[3].start()
    cz[4].start()

    def gram(dst, lhs, rhs, base, init):
        @pl.loop(0, 2)
        def _(c):
            total = None
            for n in range(NX):
                part = nt(lhs[base + n].reshape(512, 256), rhs[base + n, pl.ds(2 * c, 2)].reshape(256, 256))
                total = part if total is None else total + part
            cols = pl.ds(pl.multiple_of(256 * c, 256), 256)
            dst[:, cols] = total if init else dst[:, cols] + total

    gram(acc, bo, bo, near, True)
    to_near[1]()
    ct_near.wait_recv()
    odd(lambda: gram(acc2, bo, bx, near, True))

    cxf = [[copy(chunk(gfar, c), chunk(gfar, c), xs[d]) for d in range(3)] for c in range(5)]
    ct_far = [copy(bo.at[far4, q], bx.at[far4, q], twin) for q in range(4)]
    to_far = [slices(far4, q) for q in range(4)]
    for step in range(6):
        if step < 5:
            cz[step].wait_recv()
            for c in cxf[step]:
                c.start()
        if step in (2, 3, 4):
            to_far[step - 2][1]()
        if step > 0:
            for c in cxf[step - 1]:
                c.wait_recv()
        if step in (1, 2, 3, 5):
            q = min(step, 4) - 1
            to_far[q][0]()
            ct_far[q].start()
    to_far[3][1]()
    pl.when(y == 0)(cr_f.start)
    pl.when((y < 2) & (k == 0))(cr_g.start)

    def amplitude(integral, first, second, q, rows, cols=slice(None)):
        gap = vv[q, rows, cols] - eps[first, 0:1, cols] - eps[second, 0:1, cols]
        return (-integral / gap).astype(BF)

    def tile(piece, pq, whole, wq):
        halves = []
        for half in range(2):
            total = None
            for n in range(NX):
                lhs, rhs = piece[NX * half + n, pq], whole[NX * half + n, wq]
                part = nt(lhs.reshape(-1, 256), rhs.reshape(-1, 256))
                total = part if total is None else total + part
            halves.append(total)
        return halves[0] + halves[1]

    head, tail = slice(0, 384), slice(384, 512)
    early = [[copy(t.at[p, 0:3, mine, head], t.at[p, 0:3, mine, head], xs[d], "even" if p == 2 else "all")
              for d in range(3)] for p in range(3)]
    late = [[copy(src, src, xs[d], "even" if p == 2 else "all") for d in range(3)
             for src in (t.at[p, 3, mine], t.at[p, 0:3, mine, tail])] for p in range(3)]

    def begin(copies):
        for c in copies:
            c.start()

    def arrive(copies):
        for c in copies:
            c.wait_recv()

    def first_batch(p, piece, whole, first, second):
        total = tile(piece, slice(0, 3), whole, slice(0, 3))
        for q in range(3):
            t[p, q, mine, head] = amplitude(total[32 * q:32 * q + 32], first, second, q, mine, head)
        begin(early[p])

    def second_batch(p, piece, whole, first, second):
        t[p, 3, mine] = amplitude(tile(piece, slice(3, 4), whole, slice(0, 4)), first, second, 3, mine)
        total = tile(piece, slice(0, 3), whole, slice(3, 4))
        for q in range(3):
            t[p, q, mine, tail] = amplitude(total[32 * q:32 * q + 32], first, second, q, mine, tail)
        begin(late[p])

    arrive(ce + [to_near[2]] + [part[2] for part in to_far[:3]] + ct_far[:3])
    first_batch(0, sf, bo, 0, 2)
    first_batch(1, sf, bx, 1, 2)

    @even
    def _():
        arrive([to_near[3]] + [part[3] for part in to_far[:3]])
        first_batch(2, sg, bx, 1, 3)

    def weights(p, read, both):
        @pl.loop(0, 4)
        def _(q):
            rows = pl.ds(pl.multiple_of(128 * q, 128), 128)
            turned = jnp.concatenate([read(n, rows).T for n in range(4)], axis=1)
            tt[p, rows] = turned
            tq, turned = read(q, slice(None)).astype(F32), turned.astype(F32)
            if both:
                wt[rows] = (2.0 * tq - turned).astype(BF)
            w[p, rows] = (2.0 * turned - tq).astype(BF)

    def energy(p, read, first, second, slot):
        @pl.loop(0, 4)
        def _(q):
            rows = pl.ds(pl.multiple_of(128 * q, 128), 128)
            tq = read(q, slice(None)).astype(F32)
            gap = vv[q] - eps[first, 0:1, :] - eps[second, 0:1, :]
            wide = 2.0 * tq - tt[p, rows].astype(F32)
            esum[slot, 0:1] += jnp.sum(gap * tq * wide, axis=0, keepdims=True)

    def times(weight, factor):
        return jnp.dot(weight, factor.reshape(512, 256), preferred_element_type=F32)

    def amplitudes(p):
        return lambda q, cols: t[p, q, :, cols]

    def own_amplitudes(q, cols):
        return a0[q, :, cols]

    def own_pair():
        weights(3, own_amplitudes, False)
        gown[...] = times(w[3], bo[g])

    def chip_pair():
        gram(acc2, bo, bx, far, False)

        @pl.loop(0, 4)
        def _(q):
            rows = pl.ds(pl.multiple_of(128 * q, 128), 128)
            t[2, q] = amplitude(acc2[rows], 1, 0, q, slice(None))
        weights(2, amplitudes(2), True)
        gown[...] += times(wt[...], bx[g])
        goth[...] = times(w[2], bo[g])

    arrive([to_far[3][2], ct_far[3]])

    @even
    def _():
        to_far[3][3].wait_recv()
        second_batch(2, sg, bx, 1, 3)

    second_batch(0, sf, bo, 0, 2)
    second_batch(1, sf, bx, 1, 2)

    gram(acc, bo, bo, far, False)

    @pl.loop(0, 4)
    def _(q):
        rows = pl.ds(pl.multiple_of(128 * q, 128), 128)
        a0[q] = amplitude(acc[rows], 0, 0, q, slice(None))

    own_pair()
    odd(chip_pair)

    c_f = copy(out3.at[0], in3.at[0], up1)
    c_g = copy(out3.at[1], in3.at[1], up2, "even")
    c_x = copy(out3.at[2], in3.at[2], twin)

    @even
    def _():
        arrive(early[2] + late[2])
        weights(2, amplitudes(2), True)
        out3[1] = times(wt[...], bx[g_up2]).astype(BF)
        c_g.start()

    arrive(early[0] + late[0])
    weights(0, amplitudes(0), True)
    gf[...] = times(wt[...], bo[g_up1])
    arrive(early[1] + late[1])
    weights(1, amplitudes(1), True)
    out3[0] = (gf[...] + times(wt[...], bx[g_up1])).astype(BF)
    c_f.start()

    @even
    def _():
        cr_g.wait_recv()
        goth[...] = times(w[2], rg[...])

    cr_f.wait_recv()
    out3[2] = (goth[...] + times(w[1], rf[...])).astype(BF)
    c_x.start()
    gown[...] += times(w[0], rf[...])
    energy(3, own_amplitudes, 0, 0, 0)
    energy(0, amplitudes(0), 0, 2, 2)
    energy(1, amplitudes(1), 1, 2, 1)
    energy(2, amplitudes(2), 1, 3 * (1 - k), 3)

    lane = lax.broadcasted_iota(jnp.int32, (8, 128), 1)
    total = [-jnp.sum(esum[n, 0:1], axis=1, keepdims=True) for n in range(4)]
    first_at = 1 + 2 * k
    en[0] = jnp.where(lane == first_at, total[1], jnp.where(lane == 4 - first_at, total[3], 0.0))
    c_e = copy(en.at[0], en.at[1], twin)
    c_e.start()
    kept = jnp.where(lane == 0, total[0], jnp.where(lane == 2, total[2], 0.0))
    c_e.wait_recv()
    energy_ref[...] = (kept + en[1])[0:1, 0:4]

    c_x.wait_recv()
    gown[...] += in3[2].astype(F32)
    c_f.wait_recv()
    gown[...] += in3[0].astype(F32)

    @even
    def _():
        c_g.wait_recv()
        gown[...] += in3[1].astype(F32)

    for n in range(4):
        gamma_ref[:, 128 * n:128 * n + 128] = gown[128 * n:128 * n + 128].T

    for name, sender in who.items():
        left = [c for c, n in used if n == name and all(c is not d for d in done)]

        def finish(left=left):
            for c in left:
                c.wait_send()
        finish() if sender is None else pl.when(sender)(finish)


def per_device(factors, occ_energy, vir_energy):
    vmem = pl.BlockSpec(memory_space=pltpu.VMEM)
    hbm = pl.BlockSpec(memory_space=pl.ANY)
    gamma, energy = pl.pallas_call(
        kernel,
        out_shape=(
            jax.ShapeDtypeStruct((256, 512), F32),
            jax.ShapeDtypeStruct((1, 4), F32),
        ),
        in_specs=[hbm, pl.BlockSpec(memory_space=pltpu.SMEM), hbm],
        out_specs=(vmem, vmem),
        scratch_shapes=[
            pltpu.VMEM((8, 4, 128, 256), BF),
            pltpu.VMEM((8, 4, 128, 256), BF),
            pltpu.VMEM((8, 4, 32, 256), BF),
            pltpu.VMEM((8, 4, 32, 256), BF),
            pltpu.VMEM((8, 4, 32, 256), BF),
            pltpu.VMEM((4, 128, 256), BF),
            pltpu.VMEM((4, 128, 256), BF),
            pltpu.VMEM((3, 4, 128, 512), BF),
            pltpu.VMEM((4, 128, 512), BF),
            pltpu.VMEM((4, 128, 512), F32),
            pltpu.VMEM((512, 512), F32),
            pltpu.VMEM((512, 512), F32),
            pltpu.VMEM((4, 512, 512), BF),
            pltpu.VMEM((512, 512), BF),
            pltpu.VMEM((4, 512, 512), BF),
            pltpu.VMEM((512, 256), F32),
            pltpu.VMEM((512, 256), F32),
            pltpu.VMEM((512, 256), F32),
            pltpu.VMEM((3, 512, 256), BF),
            pltpu.VMEM((3, 512, 256), BF),
            pltpu.VMEM((4, 8, 512), F32),
            pltpu.VMEM((4, 8, 512), F32),
            pltpu.VMEM((2, 8, 128), F32),
            pltpu.VMEM((256, 512), BF),
            pltpu.VMEM((1, 512), F32),
            pltpu.SemaphoreType.DMA((2,)),
            pltpu.SemaphoreType.DMA((COPIES,)),
            pltpu.SemaphoreType.DMA((COPIES,)),
        ],
        compiler_params=pltpu.CompilerParams(
            collective_id=0, has_side_effects=True, vmem_limit_bytes=60 << 20
        ),
        name="pairs",
    )(factors.reshape(256, 512), occ_energy, vir_energy.reshape(1, 512))
    return energy, gamma.reshape(256, 1, 512)


def solution(mesh):
    return jax.shard_map(
        per_device,
        mesh=mesh,
        in_specs=(P("aux", "blk", None), P("blk"), P()),
        out_specs=(P("blk", None), P("aux", "blk", None)),
        check_vma=False,
    )
```
